32 devices in a mesh: expert: 8 (over y, x, core), hidden: 4 (over z).
Axes of the slice: x: 2, y: 2, z: 4, core: 2. Of those that a mesh axis runs over, the one named last changes fastest.
Arguments:
- tokens: bfloat16 [32, 196, 1024], P('expert'), may hold values from -32 to 32
- slot_keys: bfloat16 [1024, 16], replicated, may hold values from -1 to 1
- w_in: bfloat16 [16, 1024, 4096], P('expert', None, 'hidden'), may hold values from -0.1875 to 0.1875
- b_in: float32 [16, 4096], P('expert', 'hidden'), may hold values from -6 to 6
- w_out: bfloat16 [16, 4096, 1024], P('expert', 'hidden'), may hold values from -0.09375 to 0.09375
- b_out: float32 [16, 1024], replicated, may hold values from -6 to 6
- out_grad: bfloat16 [32, 196, 1024], P('expert'), may hold values from -6 to 6
Outputs:
- token_grad: bfloat16 [32, 196, 1024], P(('expert', 'hidden'))
The draws below stay inside these ranges and needn't reach their ends.
All inputs are finite; a program needn't handle non-finite values.
Results may differ from the reference program's by a relative error of at most 0.028.
Values may be sent and summed in bfloat16 or wider, within the bound.
No kernel may reach another device: no remote copies, remote signals or barrier semaphores. Data moves between devices by JAX's collectives and lax.ppermute only.
A program may use at most 64 MiB of HBM per device.

```python
import math
import jax
import jax.numpy as jnp
from jax import lax

D = 1024
FF = 4096
M = 196
EXPERTS = 16
IMAGES = 32
N_HIDDEN = 4


def make_keys(key):
    base = jax.random.normal(jax.random.fold_in(key, 11), (D, EXPERTS), jnp.float32) * (3.0 / math.sqrt(D))
    return jnp.clip(base, -1.0, 1.0)


def draw_slot_keys(key, part):
    return make_keys(key).astype(jnp.bfloat16)


def draw_tokens(key, part):
    base = jnp.clip(jax.random.normal(jax.random.fold_in(key, 21), (IMAGES, M, D), jnp.float32), -6.0, 6.0)
    return jnp.clip(base, -32.0, 32.0).astype(jnp.bfloat16)


def block_levels(own_key, dims, pieces, smallest, largest):
    def one(dim, parts):
        heights = jax.random.uniform(jax.random.fold_in(jax.random.fold_in(own_key, 6), dim), (parts,), jnp.float32, smallest / len(pieces), largest / len(pieces))
        return jnp.repeat(jnp.exp(heights), dims[dim] // parts).reshape((-1,) + (1,) * (len(dims) - dim - 1))

    gain = one(*pieces[0])
    for cut in pieces[1:]:
        gain = gain * one(*cut)
    return gain


def normal_values(rng, shape, scale, limit, shards=(), dtype=jnp.bfloat16):
    level = block_levels(rng, shape, shards, -0.22, 0.18) if shards else 1.0
    array = jax.random.normal(rng, shape, jnp.float32) * scale * level
    return jnp.minimum(jnp.maximum(array, -limit), limit).astype(dtype)


def setup_inputs(seed: int = 0) -> dict:
    seeds = jax.random.split(jax.random.key(seed), 8)
    tokens = draw_tokens(jax.random.fold_in(seeds[7], 71), 0)
    slot_keys = draw_slot_keys(jax.random.fold_in(seeds[7], 71), 0)
    w_in = normal_values(seeds[2], (EXPERTS, D, FF), D ** -0.5, 0.1875, ((0, 8), (2, 4)))
    b_in = normal_values(seeds[3], (EXPERTS, FF), 1.0, 6.0, ((0, 8), (1, 4)), jnp.float32)
    w_out = normal_values(seeds[4], (EXPERTS, FF, D), FF ** -0.5, 0.09375, ((0, 8), (1, 4)))
    b_out = normal_values(seeds[5], (EXPERTS, D), 1.0, 6.0, (), jnp.float32)
    out_grad = normal_values(seeds[6], (IMAGES, M, D), 1.0, 6.0, ((0, 8),))
    return dict(tokens=tokens, slot_keys=slot_keys, w_in=w_in, b_in=b_in, w_out=w_out, b_out=b_out, out_grad=out_grad)


def gelu_slope(pre_act):
    return 0.5 * (1.0 + lax.erf(pre_act * 0.7071067811865476)) + pre_act * jnp.exp(-0.5 * pre_act * pre_act) * 0.3989422804014327


def quarter_total(partials):
    rounded = partials.astype(jnp.bfloat16)
    rounded = lax.optimization_barrier(rounded)
    return jnp.sum(rounded.astype(jnp.float32), axis=0)


def expert_pass(operands):
    rows_in, rows_grad, weight_in, bias_in, weight_out, bias_out = operands
    batch = rows_in.shape[0]
    width = rows_in.shape[1]
    quarter_units = weight_in.shape[1] // N_HIDDEN
    pre_act = jnp.dot(rows_in, weight_in, preferred_element_type=jnp.float32) + bias_in
    hidden_act = jax.nn.gelu(pre_act, approximate=False).astype(jnp.bfloat16)
    out_parts = jnp.einsum("bqf,qfd->qbd", hidden_act.reshape(batch, N_HIDDEN, quarter_units).astype(jnp.float32), weight_out.reshape(N_HIDDEN, quarter_units, width).astype(jnp.float32))
    slot_out = (quarter_total(out_parts) + bias_out).astype(jnp.bfloat16)
    act_grad = jnp.dot(rows_grad, weight_out.T, preferred_element_type=jnp.float32)
    pre_grad = (act_grad * gelu_slope(pre_act)).astype(jnp.bfloat16)
    in_parts = jnp.einsum("bqf,dqf->qbd", pre_grad.reshape(batch, N_HIDDEN, quarter_units).astype(jnp.float32), weight_in.reshape(width, N_HIDDEN, quarter_units).astype(jnp.float32))
    slot_in_grad = quarter_total(in_parts).astype(jnp.bfloat16)
    return slot_out, slot_in_grad


def reference(tokens, slot_keys, w_in, b_in, w_out, b_out, out_grad):
    tokens_wide = tokens.astype(jnp.float32)
    keys_wide = slot_keys.astype(jnp.float32)
    grad_wide = out_grad.astype(jnp.float32)
    logits = jnp.einsum("btd,ds->bts", tokens_wide, keys_wide)
    dispatch = jax.nn.softmax(logits, axis=1).astype(jnp.bfloat16)
    combine = jax.nn.softmax(logits, axis=2).astype(jnp.bfloat16)
    disp_wide = dispatch.astype(jnp.float32)
    comb_wide = combine.astype(jnp.float32)
    slot_in = jnp.einsum("bts,btd->bsd", disp_wide, tokens_wide).astype(jnp.bfloat16)
    slot_grad = jnp.einsum("bts,btd->bsd", comb_wide, grad_wide).astype(jnp.bfloat16)
    per_expert = (jnp.swapaxes(slot_in, 0, 1), jnp.swapaxes(slot_grad, 0, 1), w_in, b_in, w_out, b_out)
    slot_out, slot_in_grad = lax.map(expert_pass, per_expert)
    slot_out = jnp.swapaxes(slot_out, 0, 1).astype(jnp.float32)
    slot_in_grad = jnp.swapaxes(slot_in_grad, 0, 1).astype(jnp.float32)
    comb_grad = jnp.einsum("btd,bsd->bts", grad_wide, slot_out)
    disp_grad = jnp.einsum("btd,bsd->bts", tokens_wide, slot_in_grad)
    logit_grad = comb_wide * (comb_grad - jnp.sum(comb_wide * comb_grad, axis=2, keepdims=True))
    logit_grad = logit_grad + disp_wide * (disp_grad - jnp.sum(disp_wide * disp_grad, axis=1, keepdims=True))
    logit_grad = logit_grad.astype(jnp.bfloat16).astype(jnp.float32)
    token_grad = jnp.einsum("bts,bsd->btd", disp_wide, slot_in_grad) + jnp.einsum("bts,ds->btd", logit_grad, keys_wide)
    return token_grad.astype(jnp.bfloat16)
```

```python
import jax
import jax.numpy as jnp
from jax import lax
from jax.sharding import PartitionSpec as P


def gelu_slope(pre_act):
    return (
        0.5 * (1.0 + lax.erf(pre_act * 0.7071067811865476))
        + pre_act * jnp.exp(-0.5 * pre_act * pre_act) * 0.3989422804014327
    )


def local(tokens, slot_keys, w_in, b_in, w_out, b_out, out_grad):
    n_expert = lax.axis_size("expert")
    n_hidden = lax.axis_size("hidden")
    n_all = n_expert * n_hidden
    images, positions, width = tokens.shape
    quarter = images // n_hidden
    slots = slot_keys.shape[1]
    k = w_in.shape[0]
    logits = jnp.einsum("btd,ds->bts", tokens, slot_keys, preferred_element_type=jnp.float32)
    dispatch = jax.nn.softmax(logits, axis=1).astype(jnp.bfloat16)
    combine = jax.nn.softmax(logits, axis=2).astype(jnp.bfloat16)
    slot_in = jnp.einsum(
        "bts,btd->sbd", dispatch, tokens, preferred_element_type=jnp.float32
    ).astype(jnp.bfloat16)
    slot_grad = jnp.einsum(
        "bts,btd->sbd", combine, out_grad, preferred_element_type=jnp.float32
    ).astype(jnp.bfloat16)
    sent = jnp.concatenate(
        [
            slot_in.reshape(n_expert, k * images, width),
            slot_grad.reshape(n_expert, k * images, width),
        ],
        axis=1,
    )
    got = lax.all_to_all(sent, "expert", split_axis=0, concat_axis=0, tiled=True)
    got = got.reshape(n_expert, 2, k, images, width)
    rows_in = got[:, 0].swapaxes(0, 1).reshape(k, n_expert * images, width)
    rows_grad = got[:, 1].swapaxes(0, 1).reshape(k, n_expert * images, width)
    pre_act = (
        jnp.einsum("krd,kdf->krf", rows_in, w_in, preferred_element_type=jnp.float32)
        + b_in[:, None]
    )
    hidden_act = jax.nn.gelu(pre_act, approximate=False).astype(jnp.bfloat16)
    out_part = jnp.einsum("krf,kfd->krd", hidden_act, w_out, preferred_element_type=jnp.float32)
    act_grad = jnp.einsum("krd,kfd->krf", rows_grad, w_out, preferred_element_type=jnp.float32)
    pre_grad = (act_grad * gelu_slope(pre_act)).astype(jnp.bfloat16)
    in_part = jnp.einsum("krf,kdf->krd", pre_grad, w_in, preferred_element_type=jnp.float32)

    def home(part):
        part = part.astype(jnp.bfloat16).reshape(k, n_all, quarter, width)
        part = part.swapaxes(0, 1).reshape(n_all, k * quarter, width)
        return part

    back = jnp.concatenate([home(out_part), home(in_part)], axis=1)
    back = lax.all_to_all(back, ("expert", "hidden"), split_axis=0, concat_axis=0, tiled=True)
    back = back.reshape(n_expert, n_hidden, 2, k, quarter, width).astype(jnp.float32)
    back = jnp.sum(back, axis=1)
    back = back.transpose(1, 3, 0, 2, 4).reshape(2, quarter, slots, width)
    slot_out = (back[0] + b_out[None]).astype(jnp.bfloat16)
    slot_in_grad = back[1].astype(jnp.bfloat16)
    offset = lax.axis_index("hidden") * quarter
    mine_tokens = lax.dynamic_slice_in_dim(tokens, offset, quarter, 0)
    mine_grad = lax.dynamic_slice_in_dim(out_grad, offset, quarter, 0)
    mine_dispatch = lax.dynamic_slice_in_dim(dispatch, offset, quarter, 0)
    mine_combine = lax.dynamic_slice_in_dim(combine, offset, quarter, 0)
    comb_grad = jnp.einsum("btd,bsd->bts", mine_grad, slot_out, preferred_element_type=jnp.float32)
    disp_grad = jnp.einsum(
        "btd,bsd->bts", mine_tokens, slot_in_grad, preferred_element_type=jnp.float32
    )
    comb_wide = mine_combine.astype(jnp.float32)
    disp_wide = mine_dispatch.astype(jnp.float32)
    logit_grad = comb_wide * (comb_grad - jnp.sum(comb_wide * comb_grad, axis=2, keepdims=True))
    logit_grad = logit_grad + disp_wide * (
        disp_grad - jnp.sum(disp_wide * disp_grad, axis=1, keepdims=True)
    )
    logit_grad = logit_grad.astype(jnp.bfloat16)
    token_grad = jnp.einsum(
        "bts,bsd->btd", mine_dispatch, slot_in_grad, preferred_element_type=jnp.float32
    )
    token_grad = token_grad + jnp.einsum(
        "bts,ds->btd", logit_grad, slot_keys, preferred_element_type=jnp.float32
    )
    return token_grad.astype(jnp.bfloat16)


def solution(mesh):
    return jax.shard_map(
        local,
        mesh=mesh,
        in_specs=(
            P("expert", None, None),
            P(),
            P("expert", None, "hidden"),
            P("expert", "hidden"),
            P("expert", "hidden", None),
            P(),
            P("expert", None, None),
        ),
        out_specs=P(("expert", "hidden"), None, None),
        check_vma=False,
    )
```

```python
import jax
import jax.numpy as jnp
from jax import lax
from jax.sharding import PartitionSpec as P


def gelu_slope(pre_act):
    return (
        0.5 * (1.0 + lax.erf(pre_act * 0.7071067811865476))
        + pre_act * jnp.exp(-0.5 * pre_act * pre_act) * 0.3989422804014327
    )


def exchange(blocks, axis, sign):
    n = lax.axis_size(axis)
    got = [blocks[0]]
    for j in range(1, n):
        got.append(lax.ppermute(blocks[j], axis, [(i, (i + sign * j) % n) for i in range(n)]))
    return got


def local(tokens, slot_keys, w_in, b_in, w_out, b_out, out_grad):
    n_expert = lax.axis_size("expert")
    n_hidden = lax.axis_size("hidden")
    n_all = n_expert * n_hidden
    images, positions, width = tokens.shape
    quarter = images // n_hidden
    slots = slot_keys.shape[1]
    k = w_in.shape[0]
    logits = jnp.einsum("btd,ds->bts", tokens, slot_keys, preferred_element_type=jnp.float32)
    dispatch = jax.nn.softmax(logits, axis=1).astype(jnp.bfloat16)
    combine = jax.nn.softmax(logits, axis=2).astype(jnp.bfloat16)
    slot_in = jnp.einsum(
        "bts,btd->sbd", dispatch, tokens, preferred_element_type=jnp.float32
    ).astype(jnp.bfloat16)
    slot_grad = jnp.einsum(
        "bts,btd->sbd", combine, out_grad, preferred_element_type=jnp.float32
    ).astype(jnp.bfloat16)
    sent = jnp.concatenate(
        [
            slot_in.reshape(n_expert, k * images, width),
            slot_grad.reshape(n_expert, k * images, width),
        ],
        axis=1,
    )
    sent = jnp.roll(sent, -lax.axis_index("expert"), 0)
    got = exchange([sent[j] for j in range(n_expert)], "expert", 1)
    rows_in = jnp.concatenate([g[: k * images].reshape(k, images, width) for g in got], axis=1)
    rows_grad = jnp.concatenate([g[k * images :].reshape(k, images, width) for g in got], axis=1)
    pre_act = (
        jnp.einsum("krd,kdf->krf", rows_in, w_in, preferred_element_type=jnp.float32)
        + b_in[:, None]
    )
    hidden_act = jax.nn.gelu(pre_act, approximate=False).astype(jnp.bfloat16)
    out_part = jnp.einsum("krf,kfd->krd", hidden_act, w_out, preferred_element_type=jnp.float32)
    act_grad = jnp.einsum("krd,kfd->krf", rows_grad, w_out, preferred_element_type=jnp.float32)
    pre_grad = (act_grad * gelu_slope(pre_act)).astype(jnp.bfloat16)
    in_part = jnp.einsum("krf,kdf->krd", pre_grad, w_in, preferred_element_type=jnp.float32)

    def gather_quarters(part):
        part = part.astype(jnp.bfloat16).reshape(k, n_expert, n_hidden, quarter, width)
        part = part.transpose(2, 1, 0, 3, 4).reshape(n_hidden, n_expert * k * quarter, width)
        return jnp.roll(part, -lax.axis_index("hidden"), 0)

    parts = jnp.concatenate([gather_quarters(out_part), gather_quarters(in_part)], axis=1)
    parts = exchange([parts[j] for j in range(n_hidden)], "hidden", 1)
    total = sum(p.astype(jnp.float32) for p in parts)
    total = total.reshape(2, n_expert, k, quarter, width)
    bias = lax.dynamic_slice_in_dim(b_out, lax.axis_index("expert") * k, k, 0)
    both = jnp.stack([total[0] + bias[None, :, None], total[1]], axis=1).astype(jnp.bfloat16)
    both = both.reshape(n_expert, 2 * k * quarter, width)
    back = exchange([both[j] for j in range(n_expert)], "expert", -1)
    back = jnp.stack(back)
    back = back.reshape(n_expert, 2, k, quarter, width)
    back = jnp.roll(back, lax.axis_index("expert"), 0)
    back = back.transpose(1, 3, 0, 2, 4).reshape(2, quarter, slots, width)
    slot_out, slot_in_grad = back[0], back[1]
    offset = lax.axis_index("hidden") * quarter
    mine_tokens = lax.dynamic_slice_in_dim(tokens, offset, quarter, 0)
    mine_grad = lax.dynamic_slice_in_dim(out_grad, offset, quarter, 0)
    mine_dispatch = lax.dynamic_slice_in_dim(dispatch, offset, quarter, 0)
    mine_combine = lax.dynamic_slice_in_dim(combine, offset, quarter, 0)
    comb_grad = jnp.einsum("btd,bsd->bts", mine_grad, slot_out, preferred_element_type=jnp.float32)
    disp_grad = jnp.einsum(
        "btd,bsd->bts", mine_tokens, slot_in_grad, preferred_element_type=jnp.float32
    )
    comb_wide = mine_combine.astype(jnp.float32)
    disp_wide = mine_dispatch.astype(jnp.float32)
    logit_grad = comb_wide * (comb_grad - jnp.sum(comb_wide * comb_grad, axis=2, keepdims=True))
    logit_grad = logit_grad + disp_wide * (
        disp_grad - jnp.sum(disp_wide * disp_grad, axis=1, keepdims=True)
    )
    logit_grad = logit_grad.astype(jnp.bfloat16)
    token_grad = jnp.einsum(
        "bts,bsd->btd", mine_dispatch, slot_in_grad, preferred_element_type=jnp.float32
    )
    token_grad = token_grad + jnp.einsum(
        "bts,ds->btd", logit_grad, slot_keys, preferred_element_type=jnp.float32
    )
    return token_grad.astype(jnp.bfloat16)


def solution(mesh):
    return jax.shard_map(
        local,
        mesh=mesh,
        in_specs=(
            P("expert", None, None),
            P(),
            P("expert", None, "hidden"),
            P("expert", "hidden"),
            P("expert", "hidden", None),
            P(),
            P("expert", None, None),
        ),
        out_specs=P(("expert", "hidden"), None, None),
        check_vma=False,
    )
```

```python
import functools

import jax
import jax.numpy as jnp
import numpy as np
from jax import lax
from jax.experimental import pallas as pl
from jax.experimental.pallas import tpu as pltpu
from jax.sharding import PartitionSpec as P

BF = jnp.bfloat16
F32 = jnp.float32
NN = (((1,), (0,)), ((), ()))
NT = (((1,), (1,)), ((), ()))


def mm(a, b, dims=NN):
    return lax.dot_general(a, b, dims, preferred_element_type=F32)


def block_of(n_expert):
    return 8 if n_expert % 8 == 0 else n_expert


def one_hot_rows(source, count):
    return np.asarray(np.asarray(source).reshape(-1)[:, None] == np.arange(count)[None], BF)


def dispatch_kernel(images, k, gb, tok_ref, grad_ref, keys_ref, perm_ref, send_ref, disp_ref, comb_ref):
    slots = keys_ref.shape[0]
    keys = keys_ref[...]
    slot_rows = [[], []]
    for b in range(images):
        tok = tok_ref[b]
        logits = mm(keys, tok, NT)
        e = jnp.exp(logits - jnp.max(logits, axis=1, keepdims=True))
        disp = (e / jnp.sum(e, axis=1, keepdims=True)).astype(BF)
        e = jnp.exp(logits - jnp.max(logits, axis=0, keepdims=True))
        comb = (e / jnp.sum(e, axis=0, keepdims=True)).astype(BF)
        disp_ref[b] = disp
        comb_ref[b] = comb
        slot_rows[0].append(mm(disp, tok).astype(BF))
        slot_rows[1].append(mm(comb, grad_ref[b]).astype(BF))
    perm = perm_ref[...]
    step = gb * k
    rows = perm.shape[0]
    for i in range(slots // step):
        block = jnp.concatenate(
            [r[i * step : (i + 1) * step] for kind in slot_rows for r in kind], axis=0
        )
        send_ref[i * rows : (i + 1) * rows] = mm(perm, block).astype(BF)


def expert_kernel(
    images, n_expert, k, gb, got_ref, win_hbm, bin_ref, wout_hbm, q_ref, t_ref, back_ref,
    win, wout, sems,
):
    copies = []
    for e in range(k):
        pair = []
        for i, (src, dst) in enumerate(((win_hbm, win), (wout_hbm, wout))):
            copy = pltpu.make_async_copy(src.at[e], dst.at[e], sems.at[e, i])
            copy.start()
            pair.append(copy)
        copies.append(pair)
    rows = gb * images
    q = q_ref[...]
    per_block = q.shape[0]
    blocks = n_expert // gb
    sorted_rows = [
        mm(q, got_ref[i * per_block : (i + 1) * per_block]).astype(BF) for i in range(blocks)
    ]

    def pick(kind, e):
        start = (kind * k + e) * rows
        return jnp.concatenate([s[start : start + rows] for s in sorted_rows], axis=0)

    width = got_ref.shape[1]
    half = width // 2
    results = [[None] * k, [None] * k]
    for e in range(k):
        copies[e][0].wait()
        pre = mm(pick(0, e), win[e]) + bin_ref[e : e + 1]
        cdf = 0.5 * (1.0 + lax.erf(pre * 0.7071067811865476))
        hidden = (pre * cdf).astype(BF)
        slope = cdf + pre * jnp.exp(-0.5 * pre * pre) * 0.3989422804014327
        copies[e][1].wait()
        act_grad = mm(pick(1, e), wout[e], NT)
        results[0][e] = mm(hidden, wout[e]).astype(BF)
        pre_grad = (act_grad * slope).astype(BF)
        results[1][e] = mm(pre_grad, win[e], NT).astype(BF)
    t = t_ref[...]
    out_rows = t.shape[0]
    for i in range(blocks):
        stack = jnp.concatenate(
            [
                r[i * rows : (i + 1) * rows, h * half : (h + 1) * half]
                for kind in results
                for r in kind
                for h in range(2)
            ],
            axis=0,
        )
        back_ref[i * out_rows : (i + 1) * out_rows] = mm(t, stack).astype(BF)


def final_kernel(
    quarter, k, gb, home_ref, bias_ref, tok_ref, grad_ref, disp_ref, comb_ref, keys_ref, sel_ref, out_ref,
):
    slots = keys_ref.shape[0]
    step = gb * k
    blocks = slots // step
    per_block = home_ref.shape[0] // blocks
    sel = sel_ref[...]
    sums = [mm(sel, home_ref[i * per_block : (i + 1) * per_block]) for i in range(blocks)]

    def assemble(kind, m):
        halves = []
        for h in range(2):
            start = ((m * 2 + kind) * 2 + h) * step
            halves.append(jnp.concatenate([s[start : start + step] for s in sums], axis=0))
        return jnp.concatenate(halves, axis=1)

    keys = keys_ref[...]
    for m in range(quarter):
        slot_out = (assemble(0, m) + bias_ref[...]).astype(BF)
        slot_in_grad = assemble(1, m).astype(BF)
        comb_grad = mm(slot_out, grad_ref[m], NT)
        disp_grad = mm(slot_in_grad, tok_ref[m], NT)
        disp = disp_ref[m]
        comb = comb_ref[m].astype(F32)
        wide = disp.astype(F32)
        logit_grad = comb * (comb_grad - jnp.sum(comb * comb_grad, axis=0, keepdims=True))
        logit_grad = logit_grad + wide * (
            disp_grad - jnp.sum(wide * disp_grad, axis=1, keepdims=True)
        )
        logit_grad = logit_grad.astype(BF).astype(F32)
        left = jnp.concatenate([wide, logit_grad], axis=0).T.astype(BF)
        right = jnp.concatenate([slot_in_grad, keys], axis=0)
        out_ref[m] = mm(left, right).astype(BF)


def local(n_expert, n_hidden, tokens, slot_keys, w_in, b_in, w_out, b_out, out_grad):
    n_all = n_expert * n_hidden
    images, positions, width = tokens.shape
    quarter = images // n_hidden
    slots = slot_keys.shape[1]
    k, _, units = w_in.shape
    gb = block_of(n_expert)
    half = width // 2
    vmem = pl.BlockSpec(memory_space=pltpu.VMEM)
    anywhere = pl.BlockSpec(memory_space=pl.ANY)
    keys = slot_keys.T

    order = np.arange(2 * images * gb * k).reshape(2, images, gb, k).transpose(2, 0, 3, 1)
    perm = one_hot_rows(order, order.size)
    send_rows = 2 * k * images
    send, disp, comb = pl.pallas_call(
        functools.partial(dispatch_kernel, images, k, gb),
        out_shape=(
            jax.ShapeDtypeStruct((n_expert * send_rows, width), BF),
            jax.ShapeDtypeStruct((images, slots, positions), BF),
            jax.ShapeDtypeStruct((images, slots, positions), BF),
        ),
        in_specs=[vmem] * 4,
        out_specs=(vmem,) * 3,
        compiler_params=pltpu.CompilerParams(vmem_limit_bytes=24 << 20),
        name="dispatch",
    )(tokens, out_grad, keys, perm)

    got = lax.all_to_all(
        send.reshape(n_expert, send_rows, width), "expert", split_axis=0, concat_axis=0, tiled=True
    )

    order = np.arange(gb * send_rows).reshape(gb, 2, k, images).transpose(1, 2, 0, 3)
    sort = one_hot_rows(order, order.size)
    order = np.arange(2 * k * 2 * gb * images).reshape(2, k, 2, gb, n_hidden, quarter)
    order = order.transpose(3, 4, 0, 1, 5, 2)
    spread = one_hot_rows(order, order.size)
    back_rows = 2 * k * quarter * 2
    back = pl.pallas_call(
        functools.partial(expert_kernel, images, n_expert, k, gb),
        out_shape=jax.ShapeDtypeStruct((n_all * back_rows, half), BF),
        in_specs=[vmem, anywhere, vmem, anywhere, vmem, vmem],
        out_specs=vmem,
        scratch_shapes=[
            pltpu.VMEM(w_in.shape, BF),
            pltpu.VMEM(w_out.shape, BF),
            pltpu.SemaphoreType.DMA((k, 2)),
        ],
        compiler_params=pltpu.CompilerParams(vmem_limit_bytes=40 << 20),
        name="experts",
    )(got.reshape(n_expert * send_rows, width), w_in, b_in, w_out, sort, spread)

    home = lax.all_to_all(
        back.reshape(n_all, back_rows, half),
        ("expert", "hidden"),
        split_axis=0,
        concat_axis=0,
        tiled=True,
    )

    offset = lax.axis_index("hidden") * quarter
    mine = functools.partial(lax.dynamic_slice_in_dim, start_index=offset, slice_size=quarter, axis=0)
    label = np.arange(quarter * 2 * 2 * gb * k).reshape(quarter, 2, 2, gb, k).transpose(3, 1, 4, 0, 2)
    label = np.broadcast_to(label[:, None], (gb, n_hidden) + label.shape[1:])
    select = np.ascontiguousarray(one_hot_rows(label, quarter * 4 * gb * k).T)
    return pl.pallas_call(
        functools.partial(final_kernel, quarter, k, gb),
        out_shape=jax.ShapeDtypeStruct((quarter, positions, width), BF),
        in_specs=[vmem] * 8,
        out_specs=vmem,
        compiler_params=pltpu.CompilerParams(vmem_limit_bytes=24 << 20),
        name="tokens_back",
    )(home.reshape(n_all * back_rows, half), b_out, mine(tokens), mine(out_grad), mine(disp), mine(comb), keys, select)


def solution(mesh):
    return jax.shard_map(
        functools.partial(local, mesh.shape["expert"], mesh.shape["hidden"]),
        mesh=mesh,
        in_specs=(
            P("expert", None, None),
            P(),
            P("expert", None, "hidden"),
            P("expert", "hidden"),
            P("expert", "hidden", None),
            P(),
            P("expert", None, None),
        ),
        out_specs=P(("expert", "hidden"), None, None),
        check_vma=False,
    )
```

```python
import functools

import jax
import jax.numpy as jnp
import numpy as np
from jax import lax
from jax.experimental import pallas as pl
from jax.experimental.pallas import tpu as pltpu
from jax.sharding import PartitionSpec as P

BF = jnp.bfloat16
F32 = jnp.float32
NN = (((1,), (0,)), ((), ()))
NT = (((1,), (1,)), ((), ()))


def mm(a, b, dims=NN):
    return lax.dot_general(a, b, dims, preferred_element_type=F32)


def block_of(n_expert):
    return 8 if n_expert % 8 == 0 else n_expert


def one_hot_rows(source, count):
    return np.asarray(np.asarray(source).reshape(-1)[:, None] == np.arange(count)[None], BF)


def dispatch_kernel(
    images, quarter, k, gb, tok_ref, grad_ref, keys_ref, perm_ref,
    send_ref, disp_ref, comb_ref, my_tok_ref, my_grad_ref, disp_all, comb_all,
):
    slots = keys_ref.shape[0]
    keys = keys_ref[...]
    slot_rows = [[], []]
    for b in range(images):
        tok = tok_ref[b]
        logits = mm(keys, tok, NT)
        e = jnp.exp(logits - jnp.max(logits, axis=1, keepdims=True))
        disp = (e / jnp.sum(e, axis=1, keepdims=True)).astype(BF)
        e = jnp.exp(logits - jnp.max(logits, axis=0, keepdims=True))
        comb = (e / jnp.sum(e, axis=0, keepdims=True)).astype(BF)
        disp_all[b] = disp
        comb_all[b] = comb
        slot_rows[0].append(mm(disp, tok).astype(BF))
        slot_rows[1].append(mm(comb, grad_ref[b]).astype(BF))
    perm = perm_ref[...]
    step = gb * k
    rows = perm.shape[0]
    for i in range(slots // step):
        block = jnp.concatenate(
            [r[i * step : (i + 1) * step] for kind in slot_rows for r in kind], axis=0
        )
        send_ref[i * rows : (i + 1) * rows] = mm(perm, block).astype(BF)
    first = lax.axis_index("hidden") * quarter
    for m in range(quarter):
        disp_ref[m] = disp_all[first + m]
        comb_ref[m] = comb_all[first + m]
        my_tok_ref[m] = tok_ref[first + m]
        my_grad_ref[m] = grad_ref[first + m]


def expert_kernel(
    images, n_expert, k, gb, got_ref, win_ref, bin_ref, wout_ref, q_ref, t_ref, back_ref
):
    rows = gb * images
    q = q_ref[...]
    per_block = q.shape[0]
    blocks = n_expert // gb
    sorted_rows = [
        mm(q, got_ref[i * per_block : (i + 1) * per_block]).astype(BF) for i in range(blocks)
    ]

    def pick(kind, e):
        start = (kind * k + e) * rows
        return jnp.concatenate([s[start : start + rows] for s in sorted_rows], axis=0)

    width = got_ref.shape[1]
    half = width // 2
    results = [[None] * k, [None] * k]
    for e in range(k):
        pre = mm(pick(0, e), win_ref[e]) + bin_ref[e : e + 1]
        cdf = 0.5 * (1.0 + lax.erf(pre * 0.7071067811865476))
        hidden = (pre * cdf).astype(BF)
        slope = cdf + pre * jnp.exp(-0.5 * pre * pre) * 0.3989422804014327
        act_grad = mm(pick(1, e), wout_ref[e], NT)
        results[0][e] = mm(hidden, wout_ref[e]).astype(BF)
        pre_grad = (act_grad * slope).astype(BF)
        results[1][e] = mm(pre_grad, win_ref[e], NT).astype(BF)
    t = t_ref[...]
    out_rows = t.shape[0]
    for i in range(blocks):
        stack = jnp.concatenate(
            [
                r[i * rows : (i + 1) * rows, h * half : (h + 1) * half]
                for kind in results
                for r in kind
                for h in range(2)
            ],
            axis=0,
        )
        back_ref[i * out_rows : (i + 1) * out_rows] = mm(t, stack).astype(BF)


def final_kernel(
    quarter, k, gb, home_ref, bias_ref, tok_ref, grad_ref, disp_ref, comb_ref, keys_ref, sel_ref, out_ref,
):
    slots = keys_ref.shape[0]
    step = gb * k
    blocks = slots // step
    per_block = home_ref.shape[0] // blocks
    sel = sel_ref[...]
    sums = [mm(sel, home_ref[i * per_block : (i + 1) * per_block]) for i in range(blocks)]

    def assemble(kind, m):
        halves = []
        for h in range(2):
            start = ((m * 2 + kind) * 2 + h) * step
            halves.append(jnp.concatenate([s[start : start + step] for s in sums], axis=0))
        return jnp.concatenate(halves, axis=1)

    keys = keys_ref[...]
    for m in range(quarter):
        slot_out = (assemble(0, m) + bias_ref[...]).astype(BF)
        slot_in_grad = assemble(1, m).astype(BF)
        comb_grad = mm(slot_out, grad_ref[m], NT)
        disp_grad = mm(slot_in_grad, tok_ref[m], NT)
        disp = disp_ref[m]
        comb = comb_ref[m].astype(F32)
        wide = disp.astype(F32)
        logit_grad = comb * (comb_grad - jnp.sum(comb * comb_grad, axis=0, keepdims=True))
        logit_grad = logit_grad + wide * (
            disp_grad - jnp.sum(wide * disp_grad, axis=1, keepdims=True)
        )
        logit_grad = logit_grad.astype(BF).astype(F32)
        left = jnp.concatenate([wide, logit_grad], axis=0).T.astype(BF)
        right = jnp.concatenate([slot_in_grad, keys], axis=0)
        out_ref[m] = mm(left, right).astype(BF)


def local(n_expert, n_hidden, tokens, slot_keys, w_in, b_in, w_out, b_out, out_grad):
    n_all = n_expert * n_hidden
    images, positions, width = tokens.shape
    quarter = images // n_hidden
    slots = slot_keys.shape[1]
    k, _, units = w_in.shape
    gb = block_of(n_expert)
    half = width // 2
    vmem = pl.BlockSpec(memory_space=pltpu.VMEM)
    keys = slot_keys.T

    order = np.arange(2 * images * gb * k).reshape(2, images, gb, k).transpose(2, 0, 3, 1)
    perm = one_hot_rows(order, order.size)
    send_rows = 2 * k * images
    send, disp, comb, my_tok, my_grad = pl.pallas_call(
        functools.partial(dispatch_kernel, images, quarter, k, gb),
        out_shape=(
            jax.ShapeDtypeStruct((n_expert * send_rows, width), BF),
            jax.ShapeDtypeStruct((quarter, slots, positions), BF),
            jax.ShapeDtypeStruct((quarter, slots, positions), BF),
            jax.ShapeDtypeStruct((quarter, positions, width), BF),
            jax.ShapeDtypeStruct((quarter, positions, width), BF),
        ),
        in_specs=[vmem] * 4,
        out_specs=(vmem,) * 5,
        scratch_shapes=[pltpu.VMEM((images, slots, positions), BF)] * 2,
        compiler_params=pltpu.CompilerParams(vmem_limit_bytes=12 << 20),
        name="dispatch",
    )(tokens, out_grad, keys, perm)

    got = lax.all_to_all(
        send.reshape(n_expert, send_rows, width), "expert", split_axis=0, concat_axis=0, tiled=True
    )

    order = np.arange(gb * send_rows).reshape(gb, 2, k, images).transpose(1, 2, 0, 3)
    sort = one_hot_rows(order, order.size)
    order = np.arange(2 * k * 2 * gb * images).reshape(2, k, 2, gb, n_hidden, quarter)
    order = order.transpose(3, 4, 0, 1, 5, 2)
    spread = one_hot_rows(order, order.size)
    back_rows = 2 * k * quarter * 2
    back = pl.pallas_call(
        functools.partial(expert_kernel, images, n_expert, k, gb),
        out_shape=jax.ShapeDtypeStruct((n_all * back_rows, half), BF),
        in_specs=[vmem] * 6,
        out_specs=vmem,
        compiler_params=pltpu.CompilerParams(vmem_limit_bytes=20 << 20),
        name="experts",
    )(got.reshape(n_expert * send_rows, width), w_in, b_in, w_out, sort, spread)

    home = lax.all_to_all(
        back.reshape(n_all, back_rows, half),
        ("expert", "hidden"),
        split_axis=0,
        concat_axis=0,
        tiled=True,
    )

    label = np.arange(quarter * 2 * 2 * gb * k).reshape(quarter, 2, 2, gb, k).transpose(3, 1, 4, 0, 2)
    label = np.broadcast_to(label[:, None], (gb, n_hidden) + label.shape[1:])
    select = np.ascontiguousarray(one_hot_rows(label, quarter * 4 * gb * k).T)
    return pl.pallas_call(
        functools.partial(final_kernel, quarter, k, gb),
        out_shape=jax.ShapeDtypeStruct((quarter, positions, width), BF),
        in_specs=[vmem] * 8,
        out_specs=vmem,
        compiler_params=pltpu.CompilerParams(vmem_limit_bytes=8 << 20),
        name="tokens_back",
    )(home.reshape(n_all * back_rows, half), b_out, my_tok, my_grad, disp, comb, keys, select)


def solution(mesh):
    return jax.shard_map(
        functools.partial(local, mesh.shape["expert"], mesh.shape["hidden"]),
        mesh=mesh,
        in_specs=(
            P("expert", None, None),
            P(),
            P("expert", None, "hidden"),
            P("expert", "hidden"),
            P("expert", "hidden", None),
            P(),
            P("expert", None, None),
        ),
        out_specs=P(("expert", "hidden"), None, None),
        check_vma=False,
    )
```

```python
import functools

import jax
import jax.numpy as jnp
import numpy as np
from jax import lax
from jax.experimental import pallas as pl
from jax.experimental.pallas import tpu as pltpu
from jax.sharding import PartitionSpec as P

BF = jnp.bfloat16
F32 = jnp.float32
NN = (((1,), (0,)), ((), ()))
NT = (((1,), (1,)), ((), ()))


def mm(a, b, dims=NN):
    return lax.dot_general(a, b, dims, preferred_element_type=F32)


def block_of(n_expert):
    return 8 if n_expert % 8 == 0 else n_expert


def one_hot_rows(source, count):
    return np.asarray(np.asarray(source).reshape(-1)[:, None] == np.arange(count)[None], BF)


def levels(n_expert):
    inner = 2 if n_expert % 2 == 0 else 1
    return n_expert // inner, inner


def partner(c, j, outer, back=False):
    if outer & (outer - 1) == 0:
        return c ^ j
    return lax.rem(c + (outer - j if back else j), outer) if not isinstance(c, int) else (
        (c + (outer - j if back else j)) % outer
    )


def position(inner):
    me = lax.axis_index("expert")
    return lax.div(me, inner), lax.rem(me, inner)


def dispatch_kernel(
    images, quarter, k, gb, n_expert, tok_ref, grad_ref, keys_ref, perm_ref,
    disp_ref, comb_ref, my_tok_ref, my_grad_ref, *rest,
):
    outer, inner = levels(n_expert)
    leave_refs = rest[:outer]
    send_ref, disp_all, comb_all = rest[outer:]
    slots = keys_ref.shape[0]
    keys = keys_ref[...]
    slot_rows = [[], []]
    for b in range(images):
        tok = tok_ref[b]
        logits = mm(keys, tok, NT)
        e = jnp.exp(logits - jnp.max(logits, axis=1, keepdims=True))
        disp = (e / jnp.sum(e, axis=1, keepdims=True)).astype(BF)
        e = jnp.exp(logits - jnp.max(logits, axis=0, keepdims=True))
        comb = (e / jnp.sum(e, axis=0, keepdims=True)).astype(BF)
        disp_all[b] = disp
        comb_all[b] = comb
        slot_rows[0].append(mm(disp, tok).astype(BF))
        slot_rows[1].append(mm(comb, grad_ref[b]).astype(BF))
    perm = perm_ref[...]
    step = gb * k
    rows = perm.shape[0]
    for i in range(slots // step):
        block = jnp.concatenate(
            [r[i * step : (i + 1) * step] for kind in slot_rows for r in kind], axis=0
        )
        send_ref[i * rows : (i + 1) * rows] = mm(perm, block).astype(BF)
    block = send_ref.shape[0] // n_expert
    c, l = position(inner)
    for j in range(outer):
        to = partner(c, j, outer)
        for i in range(inner):
            start = pl.multiple_of((to * inner + lax.rem(l + i, inner)) * block, block)
            leave_refs[j][i * block : (i + 1) * block] = send_ref[pl.ds(start, block)]
    first = lax.axis_index("hidden") * quarter
    for m in range(quarter):
        disp_ref[m] = disp_all[first + m]
        comb_ref[m] = comb_all[first + m]
        my_tok_ref[m] = tok_ref[first + m]
        my_grad_ref[m] = grad_ref[first + m]


def expert_kernel(
    images, n_expert, k, gb, win_ref, bin_ref, wout_ref, q_ref, t_ref, *rest
):
    outer, inner = levels(n_expert)
    come_refs = rest[:outer]
    swap_refs = rest[outer:-2]
    back_ref, got_ref = rest[-2:]
    block = got_ref.shape[0] // n_expert
    c, l = position(inner)
    for j in range(outer):
        source = partner(c, j, outer, True)
        for i in range(inner):
            start = pl.multiple_of((source * inner + lax.rem(l + i, inner)) * block, block)
            if i == 0:
                got_ref[pl.ds(start, block)] = come_refs[j][:block]
            else:
                got_ref[pl.ds(start, block)] = swap_refs[0][j * block : (j + 1) * block]
    rows = gb * images
    q = q_ref[...]
    per_block = q.shape[0]
    blocks = n_expert // gb
    sorted_rows = [
        mm(q, got_ref[i * per_block : (i + 1) * per_block]).astype(BF) for i in range(blocks)
    ]

    def pick(kind, e):
        start = (kind * k + e) * rows
        return jnp.concatenate([s[start : start + rows] for s in sorted_rows], axis=0)

    width = got_ref.shape[1]
    half = width // 2
    results = [[None] * k, [None] * k]
    for e in range(k):
        pre = mm(pick(0, e), win_ref[e]) + bin_ref[e : e + 1]
        cdf = 0.5 * (1.0 + lax.erf(pre * 0.7071067811865476))
        hidden = (pre * cdf).astype(BF)
        slope = cdf + pre * jnp.exp(-0.5 * pre * pre) * 0.3989422804014327
        act_grad = mm(pick(1, e), wout_ref[e], NT)
        results[0][e] = mm(hidden, wout_ref[e]).astype(BF)
        pre_grad = (act_grad * slope).astype(BF)
        results[1][e] = mm(pre_grad, win_ref[e], NT).astype(BF)
    t = t_ref[...]
    out_rows = t.shape[0]
    for i in range(blocks):
        stack = jnp.concatenate(
            [
                r[i * rows : (i + 1) * rows, h * half : (h + 1) * half]
                for kind in results
                for r in kind
                for h in range(2)
            ],
            axis=0,
        )
        back_ref[i * out_rows : (i + 1) * out_rows] = mm(t, stack).astype(BF)


def final_kernel(
    quarter, k, gb, home_ref, bias_ref, tok_ref, grad_ref, disp_ref, comb_ref, keys_ref, sel_ref, out_ref,
):
    slots = keys_ref.shape[0]
    step = gb * k
    blocks = slots // step
    per_block = home_ref.shape[0] // blocks
    sel = sel_ref[...]
    sums = [mm(sel, home_ref[i * per_block : (i + 1) * per_block]) for i in range(blocks)]

    def assemble(kind, m):
        halves = []
        for h in range(2):
            start = ((m * 2 + kind) * 2 + h) * step
            halves.append(jnp.concatenate([s[start : start + step] for s in sums], axis=0))
        return jnp.concatenate(halves, axis=1)

    keys = keys_ref[...]
    for m in range(quarter):
        slot_out = (assemble(0, m) + bias_ref[...]).astype(BF)
        slot_in_grad = assemble(1, m).astype(BF)
        comb_grad = mm(slot_out, grad_ref[m], NT)
        disp_grad = mm(slot_in_grad, tok_ref[m], NT)
        disp = disp_ref[m]
        comb = comb_ref[m].astype(F32)
        wide = disp.astype(F32)
        logit_grad = comb * (comb_grad - jnp.sum(comb * comb_grad, axis=0, keepdims=True))
        logit_grad = logit_grad + wide * (
            disp_grad - jnp.sum(wide * disp_grad, axis=1, keepdims=True)
        )
        logit_grad = logit_grad.astype(BF).astype(F32)
        left = jnp.concatenate([wide, logit_grad], axis=0).T.astype(BF)
        right = jnp.concatenate([slot_in_grad, keys], axis=0)
        out_ref[m] = mm(left, right).astype(BF)


def local(n_expert, n_hidden, tokens, slot_keys, w_in, b_in, w_out, b_out, out_grad):
    n_all = n_expert * n_hidden
    images, positions, width = tokens.shape
    quarter = images // n_hidden
    slots = slot_keys.shape[1]
    k, _, units = w_in.shape
    gb = block_of(n_expert)
    half = width // 2
    vmem = pl.BlockSpec(memory_space=pltpu.VMEM)
    keys = slot_keys.T

    order = np.arange(2 * images * gb * k).reshape(2, images, gb, k).transpose(2, 0, 3, 1)
    perm = one_hot_rows(order, order.size)
    send_rows = 2 * k * images
    outer, inner = levels(n_expert)
    disp, comb, my_tok, my_grad, *leave = pl.pallas_call(
        functools.partial(dispatch_kernel, images, quarter, k, gb, n_expert),
        out_shape=(
            jax.ShapeDtypeStruct((quarter, slots, positions), BF),
            jax.ShapeDtypeStruct((quarter, slots, positions), BF),
            jax.ShapeDtypeStruct((quarter, positions, width), BF),
            jax.ShapeDtypeStruct((quarter, positions, width), BF),
        )
        + (jax.ShapeDtypeStruct((inner * send_rows, width), BF),) * outer,
        in_specs=[vmem] * 4,
        out_specs=(vmem,) * (4 + outer),
        scratch_shapes=[pltpu.VMEM((n_expert * send_rows, width), BF)]
        + [pltpu.VMEM((images, slots, positions), BF)] * 2,
        compiler_params=pltpu.CompilerParams(vmem_limit_bytes=12 << 20),
        name="dispatch",
    )(tokens, out_grad, keys, perm)

    everyone = [(c, l) for c in range(outer) for l in range(inner)]
    come = leave[:1] + [None] * (outer - 1)
    for j in range(outer - 1, 0, -1):
        pairs = [(c * inner + l, partner(c, j, outer) * inner + l) for c, l in everyone]
        come[j] = lax.ppermute(leave[j], "expert", pairs)
    swapped = []
    if inner == 2:
        pairs = [(c * inner + l, c * inner + 1 - l) for c, l in everyone]
        swapped = [lax.ppermute(jnp.concatenate([r[send_rows:] for r in come]), "expert", pairs)]

    order = np.arange(gb * send_rows).reshape(gb, 2, k, images).transpose(1, 2, 0, 3)
    sort = one_hot_rows(order, order.size)
    order = np.arange(2 * k * 2 * gb * images).reshape(2, k, 2, gb, n_hidden, quarter)
    order = order.transpose(3, 4, 0, 1, 5, 2)
    spread = one_hot_rows(order, order.size)
    back_rows = 2 * k * quarter * 2
    back = pl.pallas_call(
        functools.partial(expert_kernel, images, n_expert, k, gb),
        out_shape=jax.ShapeDtypeStruct((n_all * back_rows, half), BF),
        in_specs=[vmem] * (5 + outer + len(swapped)),
        out_specs=vmem,
        scratch_shapes=[pltpu.VMEM((n_expert * send_rows, width), BF)],
        compiler_params=pltpu.CompilerParams(vmem_limit_bytes=20 << 20),
        name="experts",
    )(w_in, b_in, w_out, sort, spread, *come, *swapped)

    home = lax.all_to_all(
        back.reshape(n_all, back_rows, half),
        ("expert", "hidden"),
        split_axis=0,
        concat_axis=0,
        tiled=True,
    )

    label = np.arange(quarter * 2 * 2 * gb * k).reshape(quarter, 2, 2, gb, k).transpose(3, 1, 4, 0, 2)
    label = np.broadcast_to(label[:, None], (gb, n_hidden) + label.shape[1:])
    select = np.ascontiguousarray(one_hot_rows(label, quarter * 4 * gb * k).T)
    return pl.pallas_call(
        functools.partial(final_kernel, quarter, k, gb),
        out_shape=jax.ShapeDtypeStruct((quarter, positions, width), BF),
        in_specs=[vmem] * 8,
        out_specs=vmem,
        compiler_params=pltpu.CompilerParams(vmem_limit_bytes=8 << 20),
        name="tokens_back",
    )(home.reshape(n_all * back_rows, half), b_out, my_tok, my_grad, disp, comb, keys, select)


def solution(mesh):
    return jax.shard_map(
        functools.partial(local, mesh.shape["expert"], mesh.shape["hidden"]),
        mesh=mesh,
        in_specs=(
            P("expert", None, None),
            P(),
            P("expert", None, "hidden"),
            P("expert", "hidden"),
            P("expert", "hidden", None),
            P(),
            P("expert", None, None),
        ),
        out_specs=P(("expert", "hidden"), None, None),
        check_vma=False,
    )
```

```python
import functools

import jax
import jax.numpy as jnp
import numpy as np
from jax import lax
from jax.experimental import pallas as pl
from jax.experimental.pallas import tpu as pltpu
from jax.sharding import PartitionSpec as P

BF = jnp.bfloat16
F32 = jnp.float32
NN = (((1,), (0,)), ((), ()))
NT = (((1,), (1,)), ((), ()))


def mm(a, b, dims=NN):
    return lax.dot_general(a, b, dims, preferred_element_type=F32)


def block_of(n_expert):
    return 8 if n_expert % 8 == 0 else n_expert


def one_hot_rows(source, count):
    return np.asarray(np.asarray(source).reshape(-1)[:, None] == np.arange(count)[None], BF)


def partner(me, j, n, back=False):
    if n & (n - 1) == 0:
        return me ^ j
    shifted = me + (n - j if back else j)
    return shifted % n if isinstance(me, int) else lax.rem(shifted, n)


def dispatch_kernel(
    images, quarter, k, gb, n_expert, tok_ref, grad_ref, keys_ref, perm_ref,
    disp_ref, comb_ref, my_tok_ref, my_grad_ref, *rest,
):
    leave_refs = rest[:n_expert]
    send_ref, disp_all, comb_all = rest[n_expert:]
    slots = keys_ref.shape[0]
    keys = keys_ref[...]
    slot_rows = [[], []]
    for b in range(images):
        tok = tok_ref[b]
        logits = mm(keys, tok, NT)
        e = jnp.exp(logits - jnp.max(logits, axis=1, keepdims=True))
        disp = (e / jnp.sum(e, axis=1, keepdims=True)).astype(BF)
        e = jnp.exp(logits - jnp.max(logits, axis=0, keepdims=True))
        comb = (e / jnp.sum(e, axis=0, keepdims=True)).astype(BF)
        disp_all[b] = disp
        comb_all[b] = comb
        slot_rows[0].append(mm(disp, tok).astype(BF))
        slot_rows[1].append(mm(comb, grad_ref[b]).astype(BF))
    perm = perm_ref[...]
    step = gb * k
    rows = perm.shape[0]
    for i in range(slots // step):
        block = jnp.concatenate(
            [r[i * step : (i + 1) * step] for kind in slot_rows for r in kind], axis=0
        )
        send_ref[i * rows : (i + 1) * rows] = mm(perm, block).astype(BF)
    block = send_ref.shape[0] // n_expert
    me = lax.axis_index("expert")
    for j in range(n_expert):
        start = pl.multiple_of(partner(me, j, n_expert) * block, block)
        leave_refs[j][...] = send_ref[pl.ds(start, block)]
    first = lax.axis_index("hidden") * quarter
    for m in range(quarter):
        disp_ref[m] = disp_all[first + m]
        comb_ref[m] = comb_all[first + m]
        my_tok_ref[m] = tok_ref[first + m]
        my_grad_ref[m] = grad_ref[first + m]


def expert_kernel(images, n_expert, k, gb, win_ref, bin_ref, wout_ref, t_ref, *rest):
    come_refs = rest[:n_expert]
    back_ref, got_ref = rest[n_expert:]
    rows = k * images
    me = lax.axis_index("expert")
    for j in range(n_expert):
        got_ref[partner(me, j, n_expert, True)] = come_refs[j][...]
    width = got_ref.shape[2]
    total = n_expert * rows
    got = got_ref[...]
    rows_in = got[:, :rows].reshape(total, width)
    rows_grad = got[:, rows:].reshape(total, width)
    half = width // 2
    expert = lax.rem(lax.div(lax.broadcasted_iota(jnp.int32, (total, 1), 0), images), k)

    def own(parts):
        out = parts[0]
        for e in range(1, k):
            out = jnp.where(expert == e, parts[e], out)
        return out

    pre = own([mm(rows_in, win_ref[e]) + bin_ref[e : e + 1] for e in range(k)])
    cdf = 0.5 * (1.0 + lax.erf(pre * 0.7071067811865476))
    hidden = (pre * cdf).astype(BF)
    slope = cdf + pre * jnp.exp(-0.5 * pre * pre) * 0.3989422804014327
    out_part = own([mm(hidden, wout_ref[e]) for e in range(k)]).astype(BF)
    act_grad = own([mm(rows_grad, wout_ref[e], NT) for e in range(k)])
    pre_grad = (act_grad * slope).astype(BF)
    in_part = own([mm(pre_grad, win_ref[e], NT) for e in range(k)]).astype(BF)
    rows = gb * k * images
    t = t_ref[...]
    out_rows = t.shape[0]
    for i in range(n_expert // gb):
        stack = jnp.concatenate(
            [
                part[i * rows : (i + 1) * rows, h * half : (h + 1) * half]
                for part in (out_part, in_part)
                for h in range(2)
            ],
            axis=0,
        )
        back_ref[i * out_rows : (i + 1) * out_rows] = mm(t, stack).astype(BF)


def final_kernel(
    quarter, k, gb, home_ref, bias_ref, tok_ref, grad_ref, disp_ref, comb_ref, keys_ref, sel_ref, out_ref,
):
    slots = keys_ref.shape[0]
    step = gb * k
    blocks = slots // step
    per_block = home_ref.shape[0] // blocks
    sel = sel_ref[...]
    sums = [mm(sel, home_ref[i * per_block : (i + 1) * per_block]) for i in range(blocks)]

    def assemble(kind, m):
        halves = []
        for h in range(2):
            start = ((m * 2 + kind) * 2 + h) * step
            halves.append(jnp.concatenate([s[start : start + step] for s in sums], axis=0))
        return jnp.concatenate(halves, axis=1)

    keys = keys_ref[...]
    for m in range(quarter):
        slot_out = (assemble(0, m) + bias_ref[...]).astype(BF)
        slot_in_grad = assemble(1, m).astype(BF)
        comb_grad = mm(slot_out, grad_ref[m], NT)
        disp_grad = mm(slot_in_grad, tok_ref[m], NT)
        disp = disp_ref[m]
        comb = comb_ref[m].astype(F32)
        wide = disp.astype(F32)
        logit_grad = comb * (comb_grad - jnp.sum(comb * comb_grad, axis=0, keepdims=True))
        logit_grad = logit_grad + wide * (
            disp_grad - jnp.sum(wide * disp_grad, axis=1, keepdims=True)
        )
        logit_grad = logit_grad.astype(BF).astype(F32)
        left = jnp.concatenate([wide, logit_grad], axis=0).T.astype(BF)
        right = jnp.concatenate([slot_in_grad, keys], axis=0)
        out_ref[m] = mm(left, right).astype(BF)


def local(n_expert, n_hidden, tokens, slot_keys, w_in, b_in, w_out, b_out, out_grad):
    n_all = n_expert * n_hidden
    images, positions, width = tokens.shape
    quarter = images // n_hidden
    slots = slot_keys.shape[1]
    k, _, units = w_in.shape
    gb = block_of(n_expert)
    half = width // 2
    vmem = pl.BlockSpec(memory_space=pltpu.VMEM)
    keys = slot_keys.T

    order = np.arange(2 * images * gb * k).reshape(2, images, gb, k).transpose(2, 0, 3, 1)
    perm = one_hot_rows(order, order.size)
    send_rows = 2 * k * images
    disp, comb, my_tok, my_grad, *leave = pl.pallas_call(
        functools.partial(dispatch_kernel, images, quarter, k, gb, n_expert),
        out_shape=(
            jax.ShapeDtypeStruct((quarter, slots, positions), BF),
            jax.ShapeDtypeStruct((quarter, slots, positions), BF),
            jax.ShapeDtypeStruct((quarter, positions, width), BF),
            jax.ShapeDtypeStruct((quarter, positions, width), BF),
        )
        + (jax.ShapeDtypeStruct((send_rows, width), BF),) * n_expert,
        in_specs=[vmem] * 4,
        out_specs=(vmem,) * (4 + n_expert),
        scratch_shapes=[pltpu.VMEM((n_expert * send_rows, width), BF)]
        + [pltpu.VMEM((images, slots, positions), BF)] * 2,
        compiler_params=pltpu.CompilerParams(vmem_limit_bytes=12 << 20),
        name="dispatch",
    )(tokens, out_grad, keys, perm)

    come = leave[:1] + [None] * (n_expert - 1)
    for j in range(n_expert - 1, 0, -1):
        pairs = [(i, partner(i, j, n_expert)) for i in range(n_expert)]
        come[j] = lax.ppermute(leave[j], "expert", pairs)

    order = np.arange(2 * k * 2 * gb * images).reshape(2, 2, gb, k, n_hidden, quarter)
    order = order.transpose(2, 4, 0, 3, 5, 1)
    spread = one_hot_rows(order, order.size)
    back_rows = 2 * k * quarter * 2
    back = pl.pallas_call(
        functools.partial(expert_kernel, images, n_expert, k, gb),
        out_shape=jax.ShapeDtypeStruct((n_all * back_rows, half), BF),
        in_specs=[vmem] * (4 + n_expert),
        out_specs=vmem,
        scratch_shapes=[pltpu.VMEM((n_expert, send_rows, width), BF)],
        compiler_params=pltpu.CompilerParams(vmem_limit_bytes=20 << 20),
        name="experts",
    )(w_in, b_in, w_out, spread, *come)

    home = lax.all_to_all(
        back.reshape(n_all, back_rows, half),
        ("expert", "hidden"),
        split_axis=0,
        concat_axis=0,
        tiled=True,
    )

    label = np.arange(quarter * 2 * 2 * gb * k).reshape(quarter, 2, 2, gb, k).transpose(3, 1, 4, 0, 2)
    label = np.broadcast_to(label[:, None], (gb, n_hidden) + label.shape[1:])
    select = np.ascontiguousarray(one_hot_rows(label, quarter * 4 * gb * k).T)
    return pl.pallas_call(
        functools.partial(final_kernel, quarter, k, gb),
        out_shape=jax.ShapeDtypeStruct((quarter, positions, width), BF),
        in_specs=[vmem] * 8,
        out_specs=vmem,
        compiler_params=pltpu.CompilerParams(vmem_limit_bytes=8 << 20),
        name="tokens_back",
    )(home.reshape(n_all * back_rows, half), b_out, my_tok, my_grad, disp, comb, keys, select)


def solution(mesh):
    return jax.shard_map(
        functools.partial(local, mesh.shape["expert"], mesh.shape["hidden"]),
        mesh=mesh,
        in_specs=(
            P("expert", None, None),
            P(),
            P("expert", None, "hidden"),
            P("expert", "hidden"),
            P("expert", "hidden", None),
            P(),
            P("expert", None, None),
        ),
        out_specs=P(("expert", "hidden"), None, None),
        check_vma=False,
    )
```

```python
import functools

import jax
import jax.numpy as jnp
import numpy as np
from jax import lax
from jax.experimental import pallas as pl
from jax.experimental.pallas import tpu as pltpu
from jax.sharding import PartitionSpec as P

BF = jnp.bfloat16
F32 = jnp.float32
NN = (((1,), (0,)), ((), ()))
NT = (((1,), (1,)), ((), ()))


def mm(a, b, dims=NN):
    return lax.dot_general(a, b, dims, preferred_element_type=F32)


def block_of(n_expert):
    return 8 if n_expert % 8 == 0 else n_expert


def one_hot_rows(source, count):
    return np.asarray(np.asarray(source).reshape(-1)[:, None] == np.arange(count)[None], BF)


def partner(me, j, n, back=False):
    if n & (n - 1) == 0:
        return me ^ j
    shifted = me + (n - j if back else j)
    return shifted % n if isinstance(me, int) else lax.rem(shifted, n)


def levels(n_expert):
    inner = 2 if n_expert % 2 == 0 else 1
    return n_expert // inner, inner


def position(inner):
    me = lax.axis_index("expert")
    return lax.div(me, inner), lax.rem(me, inner)


def dispatch_kernel(
    images, quarter, k, gb, n_expert, tok_ref, grad_ref, keys_ref, perm_ref,
    disp_ref, comb_ref, my_tok_ref, my_grad_ref, *rest,
):
    outer, inner = levels(n_expert)
    leave_refs = rest[:inner]
    send_ref, disp_all, comb_all = rest[inner:]
    slots = keys_ref.shape[0]
    keys = keys_ref[...]
    slot_rows = [[], []]
    for b in range(images):
        tok = tok_ref[b]
        logits = mm(keys, tok, NT)
        e = jnp.exp(logits - jnp.max(logits, axis=1, keepdims=True))
        disp = (e / jnp.sum(e, axis=1, keepdims=True)).astype(BF)
        e = jnp.exp(logits - jnp.max(logits, axis=0, keepdims=True))
        comb = (e / jnp.sum(e, axis=0, keepdims=True)).astype(BF)
        disp_all[b] = disp
        comb_all[b] = comb
        slot_rows[0].append(mm(disp, tok).astype(BF))
        slot_rows[1].append(mm(comb, grad_ref[b]).astype(BF))
    perm = perm_ref[...]
    step = gb * k
    rows = perm.shape[0]
    for i in range(slots // step):
        block = jnp.concatenate(
            [r[i * step : (i + 1) * step] for kind in slot_rows for r in kind], axis=0
        )
        send_ref[i * rows : (i + 1) * rows] = mm(perm, block).astype(BF)
    block = send_ref.shape[0] // n_expert
    c, l = position(inner)
    for i in range(inner):
        for j in range(outer):
            to = partner(c, j, outer) * inner + lax.rem(l + i, inner)
            leave_refs[i][j * block : (j + 1) * block] = send_ref[
                pl.ds(pl.multiple_of(to * block, block), block)
            ]
    first = lax.axis_index("hidden") * quarter
    for m in range(quarter):
        disp_ref[m] = disp_all[first + m]
        comb_ref[m] = comb_all[first + m]
        my_tok_ref[m] = tok_ref[first + m]
        my_grad_ref[m] = grad_ref[first + m]


def expert_kernel(images, n_expert, k, gb, win_ref, bin_ref, wout_ref, t_ref, *rest):
    outer, inner = levels(n_expert)
    come_refs = rest[:outer]
    back_ref, got_ref = rest[outer:]
    rows = k * images
    c, l = position(inner)
    block = got_ref.shape[1]
    for j in range(outer):
        source = partner(c, j, outer, True) * inner
        for i in range(inner):
            got_ref[source + lax.rem(l + i, inner)] = come_refs[j][i * block : (i + 1) * block]
    width = got_ref.shape[2]
    total = n_expert * rows
    got = got_ref[...]
    rows_in = got[:, :rows].reshape(total, width)
    rows_grad = got[:, rows:].reshape(total, width)
    half = width // 2
    expert = lax.rem(lax.div(lax.broadcasted_iota(jnp.int32, (total, 1), 0), images), k)

    def own(parts):
        out = parts[0]
        for e in range(1, k):
            out = jnp.where(expert == e, parts[e], out)
        return out

    pre = own([mm(rows_in, win_ref[e]) + bin_ref[e : e + 1] for e in range(k)])
    cdf = 0.5 * (1.0 + lax.erf(pre * 0.7071067811865476))
    hidden = (pre * cdf).astype(BF)
    slope = cdf + pre * jnp.exp(-0.5 * pre * pre) * 0.3989422804014327
    out_part = own([mm(hidden, wout_ref[e]) for e in range(k)]).astype(BF)
    act_grad = own([mm(rows_grad, wout_ref[e], NT) for e in range(k)])
    pre_grad = (act_grad * slope).astype(BF)
    in_part = own([mm(pre_grad, win_ref[e], NT) for e in range(k)]).astype(BF)
    rows = gb * k * images
    t = t_ref[...]
    out_rows = t.shape[0]
    for i in range(n_expert // gb):
        stack = jnp.concatenate(
            [
                part[i * rows : (i + 1) * rows, h * half : (h + 1) * half]
                for part in (out_part, in_part)
                for h in range(2)
            ],
            axis=0,
        )
        back_ref[i * out_rows : (i + 1) * out_rows] = mm(t, stack).astype(BF)


def final_kernel(
    quarter, k, gb, home_ref, bias_ref, tok_ref, grad_ref, disp_ref, comb_ref, keys_ref, sel_ref, out_ref,
):
    slots = keys_ref.shape[0]
    step = gb * k
    blocks = slots // step
    per_block = home_ref.shape[0] // blocks
    sel = sel_ref[...]
    sums = [mm(sel, home_ref[i * per_block : (i + 1) * per_block]) for i in range(blocks)]

    def assemble(kind, m):
        halves = []
        for h in range(2):
            start = ((m * 2 + kind) * 2 + h) * step
            halves.append(jnp.concatenate([s[start : start + step] for s in sums], axis=0))
        return jnp.concatenate(halves, axis=1)

    keys = keys_ref[...]
    for m in range(quarter):
        slot_out = (assemble(0, m) + bias_ref[...]).astype(BF)
        slot_in_grad = assemble(1, m).astype(BF)
        comb_grad = mm(slot_out, grad_ref[m], NT)
        disp_grad = mm(slot_in_grad, tok_ref[m], NT)
        disp = disp_ref[m]
        comb = comb_ref[m].astype(F32)
        wide = disp.astype(F32)
        logit_grad = comb * (comb_grad - jnp.sum(comb * comb_grad, axis=0, keepdims=True))
        logit_grad = logit_grad + wide * (
            disp_grad - jnp.sum(wide * disp_grad, axis=1, keepdims=True)
        )
        logit_grad = logit_grad.astype(BF).astype(F32)
        left = jnp.concatenate([wide, logit_grad], axis=0).T.astype(BF)
        right = jnp.concatenate([slot_in_grad, keys], axis=0)
        out_ref[m] = mm(left, right).astype(BF)


def local(n_expert, n_hidden, tokens, slot_keys, w_in, b_in, w_out, b_out, out_grad):
    n_all = n_expert * n_hidden
    images, positions, width = tokens.shape
    quarter = images // n_hidden
    slots = slot_keys.shape[1]
    k, _, units = w_in.shape
    gb = block_of(n_expert)
    half = width // 2
    vmem = pl.BlockSpec(memory_space=pltpu.VMEM)
    keys = slot_keys.T

    order = np.arange(2 * images * gb * k).reshape(2, images, gb, k).transpose(2, 0, 3, 1)
    perm = one_hot_rows(order, order.size)
    send_rows = 2 * k * images
    outer, inner = levels(n_expert)
    disp, comb, my_tok, my_grad, *leave = pl.pallas_call(
        functools.partial(dispatch_kernel, images, quarter, k, gb, n_expert),
        out_shape=(
            jax.ShapeDtypeStruct((quarter, slots, positions), BF),
            jax.ShapeDtypeStruct((quarter, slots, positions), BF),
            jax.ShapeDtypeStruct((quarter, positions, width), BF),
            jax.ShapeDtypeStruct((quarter, positions, width), BF),
        )
        + (jax.ShapeDtypeStruct((outer * send_rows, width), BF),) * inner,
        in_specs=[vmem] * 4,
        out_specs=(vmem,) * (4 + inner),
        scratch_shapes=[pltpu.VMEM((n_expert * send_rows, width), BF)]
        + [pltpu.VMEM((images, slots, positions), BF)] * 2,
        compiler_params=pltpu.CompilerParams(vmem_limit_bytes=12 << 20),
        name="dispatch",
    )(tokens, out_grad, keys, perm)

    everyone = [(c, l) for c in range(outer) for l in range(inner)]
    held = leave[:1]
    if inner == 2:
        pairs = [(c * inner + l, c * inner + 1 - l) for c, l in everyone]
        held.append(lax.ppermute(leave[1], "expert", pairs))
    come = []
    for j in range(outer):
        both = jnp.concatenate([r[j * send_rows : (j + 1) * send_rows] for r in held])
        pairs = [(c * inner + l, partner(c, j, outer) * inner + l) for c, l in everyone]
        come.append(lax.ppermute(both, "expert", pairs) if j else both)

    order = np.arange(2 * k * 2 * gb * images).reshape(2, 2, gb, k, n_hidden, quarter)
    order = order.transpose(2, 4, 0, 3, 5, 1)
    spread = one_hot_rows(order, order.size)
    back_rows = 2 * k * quarter * 2
    back = pl.pallas_call(
        functools.partial(expert_kernel, images, n_expert, k, gb),
        out_shape=jax.ShapeDtypeStruct((n_all * back_rows, half), BF),
        in_specs=[vmem] * (4 + outer),
        out_specs=vmem,
        scratch_shapes=[pltpu.VMEM((n_expert, send_rows, width), BF)],
        compiler_params=pltpu.CompilerParams(vmem_limit_bytes=20 << 20),
        name="experts",
    )(w_in, b_in, w_out, spread, *come)

    home = lax.all_to_all(
        back.reshape(n_all, back_rows, half),
        ("expert", "hidden"),
        split_axis=0,
        concat_axis=0,
        tiled=True,
    )

    label = np.arange(quarter * 2 * 2 * gb * k).reshape(quarter, 2, 2, gb, k).transpose(3, 1, 4, 0, 2)
    label = np.broadcast_to(label[:, None], (gb, n_hidden) + label.shape[1:])
    select = np.ascontiguousarray(one_hot_rows(label, quarter * 4 * gb * k).T)
    return pl.pallas_call(
        functools.partial(final_kernel, quarter, k, gb),
        out_shape=jax.ShapeDtypeStruct((quarter, positions, width), BF),
        in_specs=[vmem] * 8,
        out_specs=vmem,
        compiler_params=pltpu.CompilerParams(vmem_limit_bytes=8 << 20),
        name="tokens_back",
    )(home.reshape(n_all * back_rows, half), b_out, my_tok, my_grad, disp, comb, keys, select)


def solution(mesh):
    return jax.shard_map(
        functools.partial(local, mesh.shape["expert"], mesh.shape["hidden"]),
        mesh=mesh,
        in_specs=(
            P("expert", None, None),
            P(),
            P("expert", None, "hidden"),
            P("expert", "hidden"),
            P("expert", "hidden", None),
            P(),
            P("expert", None, None),
        ),
        out_specs=P(("expert", "hidden"), None, None),
        check_vma=False,
    )
```

```python
import functools

import jax
import jax.numpy as jnp
import numpy as np
from jax import lax
from jax.experimental import pallas as pl
from jax.experimental.pallas import tpu as pltpu
from jax.sharding import PartitionSpec as P

BF = jnp.bfloat16
F32 = jnp.float32
NN = (((1,), (0,)), ((), ()))
NT = (((1,), (1,)), ((), ()))
DISPATCH_VMEM = 16


def mm(a, b, dims=NN):
    return lax.dot_general(a, b, dims, preferred_element_type=F32)


def block_of(n_expert):
    return 8 if n_expert % 8 == 0 else n_expert


def one_hot_rows(source, count):
    return np.asarray(np.asarray(source).reshape(-1)[:, None] == np.arange(count)[None], BF)


def partner(me, j, n, back=False):
    if n & (n - 1) == 0:
        return me ^ j
    shifted = me + (n - j if back else j)
    return shifted % n if isinstance(me, int) else lax.rem(shifted, n)


def levels(n_expert):
    inner = 2 if n_expert % 2 == 0 else 1
    return n_expert // inner, inner


def position(inner):
    me = lax.axis_index("expert")
    return lax.div(me, inner), lax.rem(me, inner)


def softmax_rows(logits):
    e = jnp.exp(logits - jnp.max(logits, axis=0, keepdims=True))
    return e / jnp.sum(e, axis=0, keepdims=True)


def across_class(x, combine, group):
    shift = group
    while shift < 128:
        x = combine(x, pltpu.roll(x, shift, 1))
        shift *= 2
    return x


def dispatch_kernel(
    images, quarter, k, gb, n_expert, tok_hbm, grad_hbm, keys_hbm, perm_hbm, first_ref, *rest
):
    outer, inner = levels(n_expert)
    leave_refs = rest[:inner]
    tok_ref, grad_ref, keys_ref, perm_ref, send_ref, sems = rest[inner:]
    positions, _, lanes = tok_hbm.shape
    padded, group, part = tok_ref.shape
    first_ref[0] = lax.axis_index("hidden") * quarter
    if padded > positions:
        for ref in (tok_ref, grad_ref):
            ref[positions:] = jnp.zeros((padded - positions, group, part), BF)
    copies = [pltpu.make_async_copy(keys_hbm, keys_ref, sems.at[0])]
    for i, (hbm, ref) in enumerate(((tok_hbm, tok_ref), (grad_hbm, grad_ref))):
        for j in range(part // lanes):
            copies.append(
                pltpu.make_async_copy(
                    hbm.at[:, j * group : (j + 1) * group],
                    ref.at[:positions, :, j * lanes : (j + 1) * lanes],
                    sems.at[1 + i],
                )
            )
    copies.append(pltpu.make_async_copy(perm_hbm, perm_ref, sems.at[3]))
    for copy in copies:
        copy.start()
    blocks = part // lanes
    rows = padded * group
    slots = keys_ref.shape[0]
    halves = group // images
    lane = lax.broadcasted_iota(jnp.int32, (1, rows), 1)
    which = lax.rem(lane, group)
    for copy in copies[: 1 + blocks]:
        copy.wait()
    keys = keys_ref[...]
    tok = tok_ref[...].reshape(rows, part)
    split = jnp.concatenate(
        [
            jnp.concatenate(
                [
                    keys[:, (j * halves + h) * lanes : (j * halves + h + 1) * lanes]
                    for j in range(blocks)
                ],
                axis=1,
            )
            for h in range(halves)
        ],
        axis=0,
    )
    each = mm(split, tok, NT)
    partial = each[:slots]
    for h in range(1, halves):
        partial = jnp.where(which < h * images, partial, each[h * slots : (h + 1) * slots])
    logits = partial
    for h in range(1, halves):
        ahead = pltpu.roll(partial, rows - h * images, 1)
        behind = pltpu.roll(partial, group - h * images, 1)
        logits = logits + jnp.where(which < (halves - h) * images, ahead, behind)
    tiles = rows // 128
    valid = lane < positions * group
    top = jnp.where(valid, logits, -jnp.inf)
    best = functools.reduce(jnp.maximum, [top[:, i * 128 : (i + 1) * 128] for i in range(tiles)])
    best = across_class(best, jnp.maximum, group)
    e = jnp.exp(top - jnp.concatenate([best] * tiles, axis=1))
    total = functools.reduce(jnp.add, [e[:, i * 128 : (i + 1) * 128] for i in range(tiles)])
    total = across_class(total, jnp.add, group)
    disp = e / jnp.concatenate([total] * tiles, axis=1)
    comb = jnp.where(valid, softmax_rows(logits), 0.0)

    def slot_sums(weights, x):
        wide = jnp.concatenate(
            [jnp.where(which == i, weights, 0.0) for i in range(group)], axis=0
        ).astype(BF)
        out = mm(wide, x).astype(BF)
        per = images * slots
        return jnp.concatenate(
            [
                out[h * per : (h + 1) * per, j * lanes : (j + 1) * lanes]
                for j in range(blocks)
                for h in range(halves)
            ],
            axis=1,
        )

    sums = [slot_sums(disp, tok)]
    for copy in copies[1 + blocks : 1 + 2 * blocks]:
        copy.wait()
    sums.append(slot_sums(comb, grad_ref[...].reshape(rows, part)))
    copies[-1].wait()
    perm = perm_ref[...]
    step = gb * k
    count = perm.shape[0]
    for i in range(slots // step):
        block = jnp.concatenate(
            [
                r[b * slots + i * step : b * slots + (i + 1) * step]
                for r in sums
                for b in range(images)
            ],
            axis=0,
        )
        send_ref[i * count : (i + 1) * count] = mm(perm, block).astype(BF)
    block = send_ref.shape[0] // n_expert
    c, l = position(inner)
    for i in range(inner):
        for j in range(outer):
            to = partner(c, j, outer) * inner + lax.rem(l + i, inner)
            leave_refs[i][j * block : (j + 1) * block] = send_ref[
                pl.ds(pl.multiple_of(to * block, block), block)
            ]


def own_kernel(tok_ref, keys_ref, disp_ref, comb_ref):
    keys = keys_ref[...]
    for m in range(tok_ref.shape[0]):
        logits = mm(keys, tok_ref[m], NT)
        e = jnp.exp(logits - jnp.max(logits, axis=1, keepdims=True))
        disp_ref[m] = (e / jnp.sum(e, axis=1, keepdims=True)).astype(BF)
        comb_ref[m] = softmax_rows(logits).astype(BF)


def expert_kernel(images, n_expert, k, gb, win_ref, bin_ref, wout_ref, t_ref, *rest):
    outer, inner = levels(n_expert)
    come_refs = rest[:outer]
    back_ref, got_ref = rest[outer:]
    rows = k * images
    c, l = position(inner)
    block = got_ref.shape[1]
    for j in range(outer):
        source = partner(c, j, outer, True) * inner
        for i in range(inner):
            got_ref[source + lax.rem(l + i, inner)] = come_refs[j][i * block : (i + 1) * block]
    width = got_ref.shape[2]
    total = n_expert * rows
    got = got_ref[...]
    rows_in = got[:, :rows].reshape(total, width)
    rows_grad = got[:, rows:].reshape(total, width)
    half = width // 2
    expert = lax.rem(lax.div(lax.broadcasted_iota(jnp.int32, (total, 1), 0), images), k)

    def own(parts):
        out = parts[0]
        for e in range(1, k):
            out = jnp.where(expert == e, parts[e], out)
        return out

    pre = own([mm(rows_in, win_ref[e]) + bin_ref[e : e + 1] for e in range(k)])
    cdf = 0.5 * (1.0 + lax.erf(pre * 0.7071067811865476))
    hidden = (pre * cdf).astype(BF)
    slope = cdf + pre * jnp.exp(-0.5 * pre * pre) * 0.3989422804014327
    out_part = own([mm(hidden, wout_ref[e]) for e in range(k)]).astype(BF)
    act_grad = own([mm(rows_grad, wout_ref[e], NT) for e in range(k)])
    pre_grad = (act_grad * slope).astype(BF)
    in_part = own([mm(pre_grad, win_ref[e], NT) for e in range(k)]).astype(BF)
    rows = gb * k * images
    t = t_ref[...]
    out_rows = t.shape[0]
    for i in range(n_expert // gb):
        stack = jnp.concatenate(
            [
                part[i * rows : (i + 1) * rows, h * half : (h + 1) * half]
                for part in (out_part, in_part)
                for h in range(2)
            ],
            axis=0,
        )
        back_ref[i * out_rows : (i + 1) * out_rows] = mm(t, stack).astype(BF)


def final_kernel(
    quarter, k, gb, home_ref, bias_ref, tok_ref, grad_ref, disp_ref, comb_ref, keys_ref, sel_ref, out_ref,
):
    slots = keys_ref.shape[0]
    step = gb * k
    blocks = slots // step
    per_block = home_ref.shape[0] // blocks
    sel = sel_ref[...]
    sums = [mm(sel, home_ref[i * per_block : (i + 1) * per_block]) for i in range(blocks)]

    def assemble(kind, m):
        halves = []
        for h in range(2):
            start = ((m * 2 + kind) * 2 + h) * step
            halves.append(jnp.concatenate([s[start : start + step] for s in sums], axis=0))
        return jnp.concatenate(halves, axis=1)

    keys = keys_ref[...]
    for m in range(quarter):
        slot_out = (assemble(0, m) + bias_ref[...]).astype(BF)
        slot_in_grad = assemble(1, m).astype(BF)
        comb_grad = mm(slot_out, grad_ref[m], NT)
        disp_grad = mm(slot_in_grad, tok_ref[m], NT)
        disp = disp_ref[m]
        comb = comb_ref[m].astype(F32)
        wide = disp.astype(F32)
        logit_grad = comb * (comb_grad - jnp.sum(comb * comb_grad, axis=0, keepdims=True))
        logit_grad = logit_grad + wide * (
            disp_grad - jnp.sum(wide * disp_grad, axis=1, keepdims=True)
        )
        logit_grad = logit_grad.astype(BF).astype(F32)
        left = jnp.concatenate([wide, logit_grad], axis=0).T.astype(BF)
        right = jnp.concatenate([slot_in_grad, keys], axis=0)
        out_ref[m] = mm(left, right).astype(BF)


def local(n_expert, n_hidden, tokens, slot_keys, w_in, b_in, w_out, b_out, out_grad):
    n_all = n_expert * n_hidden
    images, positions, width = tokens.shape
    quarter = images // n_hidden
    slots = slot_keys.shape[1]
    k, _, units = w_in.shape
    gb = block_of(n_expert)
    half = width // 2
    vmem = pl.BlockSpec(memory_space=pltpu.VMEM)
    keys = slot_keys.T

    order = np.arange(2 * images * gb * k).reshape(2, images, gb, k).transpose(2, 0, 3, 1)
    perm = one_hot_rows(order, order.size)
    send_rows = 2 * k * images
    outer, inner = levels(n_expert)
    hbm = pl.BlockSpec(memory_space=pltpu.HBM)
    smem = pl.BlockSpec(memory_space=pltpu.SMEM)
    group = 8
    lanes = 128
    part = width * images // group
    padded = -(-positions * group // 128) * 128 // group

    def in_hbm(x):
        return pltpu.with_memory_space_constraint(x, pltpu.HBM)

    def as_it_lies(x):
        x = x.transpose(1, 0, 2).reshape(positions, images, width // lanes, lanes)
        x = x.transpose(0, 2, 1, 3).reshape(positions, width // lanes * images, lanes)
        return in_hbm(x)

    first, *leave = pl.pallas_call(
        functools.partial(dispatch_kernel, images, quarter, k, gb, n_expert),
        out_shape=(jax.ShapeDtypeStruct((1,), jnp.int32),)
        + (jax.ShapeDtypeStruct((outer * send_rows, width), BF),) * inner,
        in_specs=[hbm] * 4,
        out_specs=(smem,) + (vmem,) * inner,
        scratch_shapes=[pltpu.VMEM((padded, group, part), BF)] * 2
        + [
            pltpu.VMEM(keys.shape, BF),
            pltpu.VMEM(perm.shape, BF),
            pltpu.VMEM((n_expert * send_rows, width), BF),
            pltpu.SemaphoreType.DMA((4,)),
        ],
        compiler_params=pltpu.CompilerParams(vmem_limit_bytes=DISPATCH_VMEM << 20),
        name="dispatch",
    )(as_it_lies(tokens), as_it_lies(out_grad), in_hbm(keys), in_hbm(jnp.asarray(perm)))

    everyone = [(c, l) for c in range(outer) for l in range(inner)]
    held = leave[:1]
    if inner == 2:
        pairs = [(c * inner + l, c * inner + 1 - l) for c, l in everyone]
        held.append(lax.ppermute(leave[1], "expert", pairs))
    both = [
        jnp.concatenate([r[j * send_rows : (j + 1) * send_rows] for r in held])
        for j in range(outer)
    ]
    *both, first = lax.optimization_barrier((*both, first))
    come = both[:1]
    for j in range(1, outer):
        pairs = [(c * inner + l, partner(c, j, outer) * inner + l) for c, l in everyone]
        come.append(lax.ppermute(both[j], "expert", pairs))

    mine = functools.partial(
        lax.dynamic_slice_in_dim, start_index=first[0], slice_size=quarter, axis=0
    )
    my_tok, my_grad = mine(tokens), mine(out_grad)
    disp, comb = pl.pallas_call(
        own_kernel,
        out_shape=(jax.ShapeDtypeStruct((quarter, slots, positions), BF),) * 2,
        in_specs=[vmem] * 2,
        out_specs=(vmem,) * 2,
        compiler_params=pltpu.CompilerParams(vmem_limit_bytes=8 << 20),
        name="own_softmax",
    )(my_tok, keys)

    order = np.arange(2 * k * 2 * gb * images).reshape(2, 2, gb, k, n_hidden, quarter)
    order = order.transpose(2, 4, 0, 3, 5, 1)
    spread = one_hot_rows(order, order.size)
    back_rows = 2 * k * quarter * 2
    back = pl.pallas_call(
        functools.partial(expert_kernel, images, n_expert, k, gb),
        out_shape=jax.ShapeDtypeStruct((n_all * back_rows, half), BF),
        in_specs=[vmem] * (4 + outer),
        out_specs=vmem,
        scratch_shapes=[pltpu.VMEM((n_expert, send_rows, width), BF)],
        compiler_params=pltpu.CompilerParams(vmem_limit_bytes=20 << 20),
        name="experts",
    )(w_in, b_in, w_out, spread, *come)

    home = lax.all_to_all(
        back.reshape(n_all, back_rows, half),
        ("expert", "hidden"),
        split_axis=0,
        concat_axis=0,
        tiled=True,
    )

    label = np.arange(quarter * 2 * 2 * gb * k).reshape(quarter, 2, 2, gb, k).transpose(3, 1, 4, 0, 2)
    label = np.broadcast_to(label[:, None], (gb, n_hidden) + label.shape[1:])
    select = np.ascontiguousarray(one_hot_rows(label, quarter * 4 * gb * k).T)
    return pl.pallas_call(
        functools.partial(final_kernel, quarter, k, gb),
        out_shape=jax.ShapeDtypeStruct((quarter, positions, width), BF),
        in_specs=[vmem] * 8,
        out_specs=vmem,
        compiler_params=pltpu.CompilerParams(vmem_limit_bytes=8 << 20),
        name="tokens_back",
    )(home.reshape(n_all * back_rows, half), b_out, my_tok, my_grad, disp, comb, keys, select)


def solution(mesh):
    return jax.shard_map(
        functools.partial(local, mesh.shape["expert"], mesh.shape["hidden"]),
        mesh=mesh,
        in_specs=(
            P("expert", None, None),
            P(),
            P("expert", None, "hidden"),
            P("expert", "hidden"),
            P("expert", "hidden", None),
            P(),
            P("expert", None, None),
        ),
        out_specs=P(("expert", "hidden"), None, None),
        check_vma=False,
    )
```

```python
import functools

import jax
import jax.numpy as jnp
import numpy as np
from jax import lax
from jax.experimental import pallas as pl
from jax.experimental.pallas import tpu as pltpu
from jax.sharding import PartitionSpec as P

BF = jnp.bfloat16
F32 = jnp.float32
NN = (((1,), (0,)), ((), ()))
NT = (((1,), (1,)), ((), ()))


def mm(a, b, dims=NN):
    return lax.dot_general(a, b, dims, preferred_element_type=F32)


def block_of(n_expert):
    return 8 if n_expert % 8 == 0 else n_expert


def one_hot_rows(source, count):
    return np.asarray(np.asarray(source).reshape(-1)[:, None] == np.arange(count)[None], BF)


def partner(me, j, n, back=False):
    if n & (n - 1) == 0:
        return me ^ j
    shifted = me + (n - j if back else j)
    return shifted % n if isinstance(me, int) else lax.rem(shifted, n)


def levels(n_expert):
    inner = 2 if n_expert % 2 == 0 else 1
    return n_expert // inner, inner


def position(inner):
    me = lax.axis_index("expert")
    return lax.div(me, inner), lax.rem(me, inner)


def dispatch_kernel(
    images, quarter, k, gb, n_expert, tok_ref, grad_ref, keys_ref, perm_ref,
    disp_ref, comb_ref, my_tok_ref, my_grad_ref, *rest,
):
    outer, inner = levels(n_expert)
    leave_refs = rest[:inner]
    send_ref, disp_all, comb_all = rest[inner:]
    slots = keys_ref.shape[0]
    keys = keys_ref[...]
    slot_rows = [[], []]
    for b in range(images):
        tok = tok_ref[b]
        logits = mm(keys, tok, NT)
        e = jnp.exp(logits - jnp.max(logits, axis=1, keepdims=True))
        disp = (e / jnp.sum(e, axis=1, keepdims=True)).astype(BF)
        e = jnp.exp(logits - jnp.max(logits, axis=0, keepdims=True))
        comb = (e / jnp.sum(e, axis=0, keepdims=True)).astype(BF)
        disp_all[b] = disp
        comb_all[b] = comb
        slot_rows[0].append(mm(disp, tok).astype(BF))
        slot_rows[1].append(mm(comb, grad_ref[b]).astype(BF))
    perm = perm_ref[...]
    step = gb * k
    rows = perm.shape[0]
    for i in range(slots // step):
        block = jnp.concatenate(
            [r[i * step : (i + 1) * step] for kind in slot_rows for r in kind], axis=0
        )
        send_ref[i * rows : (i + 1) * rows] = mm(perm, block).astype(BF)
    block = send_ref.shape[0] // n_expert
    c, l = position(inner)
    for i in range(inner):
        for j in range(outer):
            to = partner(c, j, outer) * inner + lax.rem(l + i, inner)
            leave_refs[i][j * block : (j + 1) * block] = send_ref[
                pl.ds(pl.multiple_of(to * block, block), block)
            ]
    first = lax.axis_index("hidden") * quarter
    for m in range(quarter):
        disp_ref[m] = disp_all[first + m]
        comb_ref[m] = comb_all[first + m]
        my_tok_ref[m] = tok_ref[first + m]
        my_grad_ref[m] = grad_ref[first + m]


def expert_kernel(images, n_expert, n_hidden, k, gb, win_ref, bin_ref, wout_ref, t_ref, *rest):
    outer, inner = levels(n_expert)
    come_refs = rest[:outer]
    back_ref, got_ref = rest[outer:]
    rows = k * images
    c, l = position(inner)
    block = got_ref.shape[1]
    for j in range(outer):
        source = partner(c, j, outer, True) * inner
        for i in range(inner):
            got_ref[source + lax.rem(l + i, inner)] = come_refs[j][i * block : (i + 1) * block]
    width = got_ref.shape[2]
    total = n_expert * rows
    got = got_ref[...]
    rows_in = got[:, :rows].reshape(total, width)
    rows_grad = got[:, rows:].reshape(total, width)
    half = width // 2
    expert = lax.rem(lax.div(lax.broadcasted_iota(jnp.int32, (total, 1), 0), images), k)

    def own(parts):
        out = parts[0]
        for e in range(1, k):
            out = jnp.where(expert == e, parts[e], out)
        return out

    pre = own([mm(rows_in, win_ref[e]) + bin_ref[e : e + 1] for e in range(k)])
    act_grad = own([mm(rows_grad, wout_ref[e], NT) for e in range(k)])
    cdf = 0.5 * (1.0 + lax.erf(pre * 0.7071067811865476))
    hidden = (pre * cdf).astype(BF)
    slope = cdf + pre * jnp.exp(-0.5 * pre * pre) * 0.3989422804014327
    out_part = own([mm(hidden, wout_ref[e]) for e in range(k)]).astype(BF)
    pre_grad = (act_grad * slope).astype(BF)
    in_part = own([mm(pre_grad, win_ref[e], NT) for e in range(k)]).astype(BF)
    rows = gb * k * images
    t = t_ref[...]
    out_rows = t.shape[0]
    for i in range(n_expert // gb):
        stack = jnp.concatenate(
            [
                part[i * rows : (i + 1) * rows, h * half : (h + 1) * half]
                for part in (out_part, in_part)
                for h in range(2)
            ],
            axis=0,
        )
        spread = mm(t, stack).astype(BF)
        per = out_rows // n_hidden
        for h in range(n_hidden):
            start = (h * n_expert // gb + i) * per
            back_ref[start : start + per] = spread[h * per : (h + 1) * per]


def final_kernel(
    quarter, n_hidden, k, gb, home_ref, bias_ref, tok_ref, grad_ref, disp_ref, comb_ref, keys_ref, sel_ref, out_hbm,
    out_ref, sems,
):
    slots = keys_ref.shape[0]
    step = gb * k
    blocks = slots // step
    per = home_ref.shape[0] // (blocks * n_hidden)
    sel = sel_ref[...]
    sums = []
    for i in range(blocks):
        starts = [(q * blocks + i) * per for q in range(n_hidden)]
        sums.append(mm(sel, jnp.concatenate([home_ref[a : a + per] for a in starts], axis=0)))

    def assemble(kind, m):
        halves = []
        for h in range(2):
            start = ((m * 2 + kind) * 2 + h) * step
            halves.append(jnp.concatenate([s[start : start + step] for s in sums], axis=0))
        return jnp.concatenate(halves, axis=1)

    keys = keys_ref[...]
    copies = []
    for m in range(quarter):
        slot_out = (assemble(0, m) + bias_ref[...]).astype(BF)
        slot_in_grad = assemble(1, m).astype(BF)
        comb_grad = mm(slot_out, grad_ref[m], NT)
        disp_grad = mm(slot_in_grad, tok_ref[m], NT)
        disp = disp_ref[m]
        comb = comb_ref[m].astype(F32)
        wide = disp.astype(F32)
        logit_grad = comb * (comb_grad - jnp.sum(comb * comb_grad, axis=0, keepdims=True))
        logit_grad = logit_grad + wide * (
            disp_grad - jnp.sum(wide * disp_grad, axis=1, keepdims=True)
        )
        logit_grad = logit_grad.astype(BF).astype(F32)
        left = jnp.concatenate([wide, logit_grad], axis=0).T.astype(BF)
        right = jnp.concatenate([slot_in_grad, keys], axis=0)
        chunk = right.shape[1] // sems.shape[1]
        for i in range(sems.shape[1]):
            columns = slice(i * chunk, (i + 1) * chunk)
            out_ref[m, :, columns] = mm(left, right[:, columns]).astype(BF)
            copies.append(
                pltpu.make_async_copy(
                    out_ref.at[m, :, columns], out_hbm.at[m, :, columns], sems.at[m, i]
                )
            )
            copies[-1].start()
    for copy in copies:
        copy.wait()


def local(n_expert, n_hidden, tokens, slot_keys, w_in, b_in, w_out, b_out, out_grad):
    n_all = n_expert * n_hidden
    images, positions, width = tokens.shape
    quarter = images // n_hidden
    slots = slot_keys.shape[1]
    k, _, units = w_in.shape
    gb = block_of(n_expert)
    half = width // 2
    vmem = pl.BlockSpec(memory_space=pltpu.VMEM)
    keys = slot_keys.T

    order = np.arange(2 * images * gb * k).reshape(2, images, gb, k).transpose(2, 0, 3, 1)
    perm = one_hot_rows(order, order.size)
    send_rows = 2 * k * images
    outer, inner = levels(n_expert)
    disp, comb, my_tok, my_grad, *leave = pl.pallas_call(
        functools.partial(dispatch_kernel, images, quarter, k, gb, n_expert),
        out_shape=(
            jax.ShapeDtypeStruct((quarter, slots, positions), BF),
            jax.ShapeDtypeStruct((quarter, slots, positions), BF),
            jax.ShapeDtypeStruct((quarter, positions, width), BF),
            jax.ShapeDtypeStruct((quarter, positions, width), BF),
        )
        + (jax.ShapeDtypeStruct((outer * send_rows, width), BF),) * inner,
        in_specs=[vmem] * 4,
        out_specs=(vmem,) * (4 + inner),
        scratch_shapes=[pltpu.VMEM((n_expert * send_rows, width), BF)]
        + [pltpu.VMEM((images, slots, positions), BF)] * 2,
        compiler_params=pltpu.CompilerParams(vmem_limit_bytes=12 << 20),
        name="dispatch",
    )(tokens, out_grad, keys, perm)

    everyone = [(c, l) for c in range(outer) for l in range(inner)]
    held = leave[:1]
    if inner == 2:
        pairs = [(c * inner + l, c * inner + 1 - l) for c, l in everyone]
        held.append(lax.ppermute(leave[1], "expert", pairs))
    come = []
    for j in range(outer):
        both = jnp.concatenate([r[j * send_rows : (j + 1) * send_rows] for r in held])
        pairs = [(c * inner + l, partner(c, j, outer) * inner + l) for c, l in everyone]
        come.append(lax.ppermute(both, "expert", pairs) if j else both)

    order = np.arange(2 * k * 2 * gb * images).reshape(2, 2, gb, k, n_hidden, quarter)
    order = order.transpose(4, 2, 0, 3, 5, 1)
    spread = one_hot_rows(order, order.size)
    back_rows = 2 * k * quarter * 2
    back = pl.pallas_call(
        functools.partial(expert_kernel, images, n_expert, n_hidden, k, gb),
        out_shape=jax.ShapeDtypeStruct((n_all * back_rows, half), BF),
        in_specs=[vmem] * (4 + outer),
        out_specs=vmem,
        scratch_shapes=[pltpu.VMEM((n_expert, send_rows, width), BF)],
        compiler_params=pltpu.CompilerParams(vmem_limit_bytes=20 << 20),
        name="experts",
    )(w_in, b_in, w_out, spread, *come)

    home = lax.all_to_all(
        back.reshape(n_all, back_rows, half),
        ("hidden", "expert"),
        split_axis=0,
        concat_axis=0,
        tiled=True,
    )

    label = np.arange(quarter * 2 * 2 * gb * k).reshape(quarter, 2, 2, gb, k).transpose(3, 1, 4, 0, 2)
    label = np.broadcast_to(label[None], (n_hidden,) + label.shape)
    select = np.ascontiguousarray(one_hot_rows(label, quarter * 4 * gb * k).T)
    return pl.pallas_call(
        functools.partial(final_kernel, quarter, n_hidden, k, gb),
        out_shape=jax.ShapeDtypeStruct((quarter, positions, width), BF),
        in_specs=[vmem] * 8,
        out_specs=pl.BlockSpec(memory_space=pltpu.HBM),
        scratch_shapes=[
            pltpu.VMEM((quarter, positions, width), BF),
            pltpu.SemaphoreType.DMA((quarter, 4)),
        ],
        compiler_params=pltpu.CompilerParams(vmem_limit_bytes=8 << 20),
        name="tokens_back",
    )(home.reshape(n_all * back_rows, half), b_out, my_tok, my_grad, disp, comb, keys, select)


def solution(mesh):
    return jax.shard_map(
        functools.partial(local, mesh.shape["expert"], mesh.shape["hidden"]),
        mesh=mesh,
        in_specs=(
            P("expert", None, None),
            P(),
            P("expert", None, "hidden"),
            P("expert", "hidden"),
            P("expert", "hidden", None),
            P(),
            P("expert", None, None),
        ),
        out_specs=P(("expert", "hidden"), None, None),
        check_vma=False,
    )
```

```python
import functools

import jax
import jax.numpy as jnp
import numpy as np
from jax import lax
from jax.experimental import pallas as pl
from jax.experimental.pallas import tpu as pltpu
from jax.sharding import PartitionSpec as P

BF = jnp.bfloat16
F32 = jnp.float32
NN = (((1,), (0,)), ((), ()))
NT = (((1,), (1,)), ((), ()))


def mm(a, b, dims=NN):
    return lax.dot_general(a, b, dims, preferred_element_type=F32)


def block_of(n_expert):
    return 8 if n_expert % 8 == 0 else n_expert


def one_hot_rows(source, count):
    return np.asarray(np.asarray(source).reshape(-1)[:, None] == np.arange(count)[None], BF)


def partner(me, j, n, back=False):
    if n & (n - 1) == 0:
        return me ^ j
    shifted = me + (n - j if back else j)
    return shifted % n if isinstance(me, int) else lax.rem(shifted, n)


def levels(n_expert):
    inner = 2 if n_expert % 2 == 0 else 1
    return n_expert // inner, inner


def position(inner):
    me = lax.axis_index("expert")
    return lax.div(me, inner), lax.rem(me, inner)


def dispatch_kernel(
    images, quarter, k, gb, n_expert, tok_ref, grad_ref, keys_ref, perm_ref,
    disp_ref, comb_ref, my_tok_ref, my_grad_ref, *rest,
):
    outer, inner = levels(n_expert)
    leave_refs = rest[:inner]
    send_ref, disp_all, comb_all = rest[inner:]
    slots = keys_ref.shape[0]
    keys = keys_ref[...]
    slot_rows = [[], []]
    for b in range(images):
        tok = tok_ref[b]
        logits = mm(keys, tok, NT)
        e = jnp.exp(logits - jnp.max(logits, axis=1, keepdims=True))
        disp = (e / jnp.sum(e, axis=1, keepdims=True)).astype(BF)
        e = jnp.exp(logits - jnp.max(logits, axis=0, keepdims=True))
        comb = (e / jnp.sum(e, axis=0, keepdims=True)).astype(BF)
        disp_all[b] = disp
        comb_all[b] = comb
        slot_rows[0].append(mm(disp, tok).astype(BF))
        slot_rows[1].append(mm(comb, grad_ref[b]).astype(BF))
    perm = perm_ref[...]
    step = gb * k
    rows = perm.shape[0]
    for i in range(slots // step):
        block = jnp.concatenate(
            [r[i * step : (i + 1) * step] for kind in slot_rows for r in kind], axis=0
        )
        send_ref[i * rows : (i + 1) * rows] = mm(perm, block).astype(BF)
    block = send_ref.shape[0] // n_expert
    c, l = position(inner)
    for i in range(inner):
        for j in range(outer):
            to = partner(c, j, outer) * inner + lax.rem(l + i, inner)
            leave_refs[i][j * block : (j + 1) * block] = send_ref[
                pl.ds(pl.multiple_of(to * block, block), block)
            ]
    first = lax.axis_index("hidden") * quarter
    for m in range(quarter):
        disp_ref[m] = disp_all[first + m]
        comb_ref[m] = comb_all[first + m]
        my_tok_ref[m] = tok_ref[first + m]
        my_grad_ref[m] = grad_ref[first + m]


def expert_kernel(images, n_expert, k, gb, win_ref, bin_ref, wout_ref, t_ref, *rest):
    outer, inner = levels(n_expert)
    come_refs = rest[:outer]
    back_ref, got_ref = rest[outer:]
    rows = k * images
    c, l = position(inner)
    block = got_ref.shape[1]
    for j in range(outer):
        source = partner(c, j, outer, True) * inner
        for i in range(inner):
            got_ref[source + lax.rem(l + i, inner)] = come_refs[j][i * block : (i + 1) * block]
    width = got_ref.shape[2]
    total = n_expert * rows
    got = got_ref[...]
    rows_in = got[:, :rows].reshape(total, width)
    rows_grad = got[:, rows:].reshape(total, width)
    half = width // 2
    expert = lax.rem(lax.div(lax.broadcasted_iota(jnp.int32, (total, 1), 0), images), k)

    def own(parts):
        out = parts[0]
        for e in range(1, k):
            out = jnp.where(expert == e, parts[e], out)
        return out

    pre = own([mm(rows_in, win_ref[e]) + bin_ref[e : e + 1] for e in range(k)])
    cdf = 0.5 * (1.0 + lax.erf(pre * 0.7071067811865476))
    hidden = (pre * cdf).astype(BF)
    slope = cdf + pre * jnp.exp(-0.5 * pre * pre) * 0.3989422804014327
    out_part = own([mm(hidden, wout_ref[e]) for e in range(k)]).astype(BF)
    act_grad = own([mm(rows_grad, wout_ref[e], NT) for e in range(k)])
    pre_grad = (act_grad * slope).astype(BF)
    in_part = own([mm(pre_grad, win_ref[e], NT) for e in range(k)]).astype(BF)
    rows = gb * k * images
    t = t_ref[...]
    out_rows = t.shape[0]
    for i in range(n_expert // gb):
        stack = jnp.concatenate(
            [
                part[i * rows : (i + 1) * rows, h * half : (h + 1) * half]
                for part in (out_part, in_part)
                for h in range(2)
            ],
            axis=0,
        )
        back_ref[i * out_rows : (i + 1) * out_rows] = mm(t, stack).astype(BF)


def final_kernel(
    quarter, k, gb, home_ref, bias_ref, tok_ref, grad_ref, disp_ref, comb_ref, keys_ref, sel_ref, out_ref,
):
    slots = keys_ref.shape[0]
    step = gb * k
    blocks = slots // step
    per_block = home_ref.shape[0] // blocks
    sel = sel_ref[...]
    sums = [mm(sel, home_ref[i * per_block : (i + 1) * per_block]) for i in range(blocks)]

    def assemble(kind, m):
        halves = []
        for h in range(2):
            start = ((m * 2 + kind) * 2 + h) * step
            halves.append(jnp.concatenate([s[start : start + step] for s in sums], axis=0))
        return jnp.concatenate(halves, axis=1)

    keys = keys_ref[...]
    for m in range(quarter):
        slot_out = (assemble(0, m) + bias_ref[...]).astype(BF)
        slot_in_grad = assemble(1, m).astype(BF)
        comb_grad = mm(slot_out, grad_ref[m], NT)
        disp_grad = mm(slot_in_grad, tok_ref[m], NT)
        disp = disp_ref[m]
        comb = comb_ref[m].astype(F32)
        wide = disp.astype(F32)
        logit_grad = comb * (comb_grad - jnp.sum(comb * comb_grad, axis=0, keepdims=True))
        logit_grad = logit_grad + wide * (
            disp_grad - jnp.sum(wide * disp_grad, axis=1, keepdims=True)
        )
        logit_grad = logit_grad.astype(BF).astype(F32)
        left = jnp.concatenate([wide, logit_grad], axis=0).T.astype(BF)
        right = jnp.concatenate([slot_in_grad, keys], axis=0)
        out_ref[m] = mm(left, right).astype(BF)


def local(n_expert, n_hidden, tokens, slot_keys, w_in, b_in, w_out, b_out, out_grad):
    n_all = n_expert * n_hidden
    images, positions, width = tokens.shape
    quarter = images // n_hidden
    slots = slot_keys.shape[1]
    k, _, units = w_in.shape
    gb = block_of(n_expert)
    half = width // 2
    vmem = pl.BlockSpec(memory_space=pltpu.VMEM)
    keys = slot_keys.T

    order = np.arange(2 * images * gb * k).reshape(2, images, gb, k).transpose(2, 0, 3, 1)
    perm = one_hot_rows(order, order.size)
    send_rows = 2 * k * images
    outer, inner = levels(n_expert)
    disp, comb, my_tok, my_grad, *leave = pl.pallas_call(
        functools.partial(dispatch_kernel, images, quarter, k, gb, n_expert),
        out_shape=(
            jax.ShapeDtypeStruct((quarter, slots, positions), BF),
            jax.ShapeDtypeStruct((quarter, slots, positions), BF),
            jax.ShapeDtypeStruct((quarter, positions, width), BF),
            jax.ShapeDtypeStruct((quarter, positions, width), BF),
        )
        + (jax.ShapeDtypeStruct((outer * send_rows, width), BF),) * inner,
        in_specs=[vmem] * 4,
        out_specs=(vmem,) * (4 + inner),
        scratch_shapes=[pltpu.VMEM((n_expert * send_rows, width), BF)]
        + [pltpu.VMEM((images, slots, positions), BF)] * 2,
        compiler_params=pltpu.CompilerParams(vmem_limit_bytes=12 << 20),
        cost_estimate=pl.CostEstimate(flops=8000000000, bytes_accessed=0, transcendentals=0),
        name="dispatch",
    )(tokens, out_grad, keys, perm)

    everyone = [(c, l) for c in range(outer) for l in range(inner)]
    held = leave[:1]
    if inner == 2:
        pairs = [(c * inner + l, c * inner + 1 - l) for c, l in everyone]
        held.append(lax.ppermute(leave[1], "expert", pairs))
    come = []
    for j in range(outer):
        both = jnp.concatenate([r[j * send_rows : (j + 1) * send_rows] for r in held])
        pairs = [(c * inner + l, partner(c, j, outer) * inner + l) for c, l in everyone]
        come.append(lax.ppermute(both, "expert", pairs) if j else both)

    order = np.arange(2 * k * 2 * gb * images).reshape(2, 2, gb, k, n_hidden, quarter)
    order = order.transpose(2, 4, 0, 3, 5, 1)
    spread = one_hot_rows(order, order.size)
    back_rows = 2 * k * quarter * 2
    back = pl.pallas_call(
        functools.partial(expert_kernel, images, n_expert, k, gb),
        out_shape=jax.ShapeDtypeStruct((n_all * back_rows, half), BF),
        in_specs=[vmem] * (4 + outer),
        out_specs=vmem,
        scratch_shapes=[pltpu.VMEM((n_expert, send_rows, width), BF)],
        compiler_params=pltpu.CompilerParams(vmem_limit_bytes=20 << 20),
        name="experts",
    )(w_in, b_in, w_out, spread, *come)

    home = lax.all_to_all(
        back.reshape(n_all, back_rows, half),
        ("expert", "hidden"),
        split_axis=0,
        concat_axis=0,
        tiled=True,
    )

    label = np.arange(quarter * 2 * 2 * gb * k).reshape(quarter, 2, 2, gb, k).transpose(3, 1, 4, 0, 2)
    label = np.broadcast_to(label[:, None], (gb, n_hidden) + label.shape[1:])
    select = np.ascontiguousarray(one_hot_rows(label, quarter * 4 * gb * k).T)
    return pl.pallas_call(
        functools.partial(final_kernel, quarter, k, gb),
        out_shape=jax.ShapeDtypeStruct((quarter, positions, width), BF),
        in_specs=[vmem] * 8,
        out_specs=vmem,
        compiler_params=pltpu.CompilerParams(vmem_limit_bytes=8 << 20),
        name="tokens_back",
    )(home.reshape(n_all * back_rows, half), b_out, my_tok, my_grad, disp, comb, keys, select)


def solution(mesh):
    return jax.shard_map(
        functools.partial(local, mesh.shape["expert"], mesh.shape["hidden"]),
        mesh=mesh,
        in_specs=(
            P("expert", None, None),
            P(),
            P("expert", None, "hidden"),
            P("expert", "hidden"),
            P("expert", "hidden", None),
            P(),
            P("expert", None, None),
        ),
        out_specs=P(("expert", "hidden"), None, None),
        check_vma=False,
    )
```

```python
import functools

import jax
import jax.numpy as jnp
import numpy as np
from jax import lax
from jax.experimental import pallas as pl
from jax.experimental.pallas import tpu as pltpu
from jax.sharding import PartitionSpec as P

BF = jnp.bfloat16
F32 = jnp.float32
NN = (((1,), (0,)), ((), ()))
NT = (((1,), (1,)), ((), ()))
DISPATCH_VMEM = 16


def mm(a, b, dims=NN):
    return lax.dot_general(a, b, dims, preferred_element_type=F32)


def block_of(n_expert):
    return 8 if n_expert % 8 == 0 else n_expert


def one_hot_rows(source, count):
    return np.asarray(np.asarray(source).reshape(-1)[:, None] == np.arange(count)[None], BF)


def partner(me, j, n, back=False):
    if n & (n - 1) == 0:
        return me ^ j
    shifted = me + (n - j if back else j)
    return shifted % n if isinstance(me, int) else lax.rem(shifted, n)


def levels(n_expert):
    inner = 2 if n_expert % 2 == 0 else 1
    return n_expert // inner, inner


def position(inner):
    me = lax.axis_index("expert")
    return lax.div(me, inner), lax.rem(me, inner)


def softmax_rows(logits):
    e = jnp.exp(logits - jnp.max(logits, axis=0, keepdims=True))
    return e / jnp.sum(e, axis=0, keepdims=True)


def across_class(x, combine, group):
    shift = group
    while shift < 128:
        x = combine(x, pltpu.roll(x, shift, 1))
        shift *= 2
    return x


def dispatch_kernel(
    images, quarter, k, gb, n_expert, tok_hbm, grad_hbm, keys_hbm, perm_hbm, first_ref, *rest
):
    outer, inner = levels(n_expert)
    leave_refs = rest[:inner]
    tok_ref, grad_ref, keys_ref, perm_ref, send_ref, sems = rest[inner:]
    positions, _, lanes = tok_hbm.shape
    padded, group, part = tok_ref.shape
    first_ref[0] = lax.axis_index("hidden") * quarter
    if padded > positions:
        for ref in (tok_ref, grad_ref):
            ref[positions:] = jnp.zeros((padded - positions, group, part), BF)
    copies = [pltpu.make_async_copy(keys_hbm, keys_ref, sems.at[0])]
    for i, (hbm, ref) in enumerate(((tok_hbm, tok_ref), (grad_hbm, grad_ref))):
        for j in range(part // lanes):
            copies.append(
                pltpu.make_async_copy(
                    hbm.at[:, j * group : (j + 1) * group],
                    ref.at[:positions, :, j * lanes : (j + 1) * lanes],
                    sems.at[1 + i],
                )
            )
    copies.append(pltpu.make_async_copy(perm_hbm, perm_ref, sems.at[3]))
    for copy in copies:
        copy.start()
    blocks = part // lanes
    rows = padded * group
    slots = keys_ref.shape[0]
    halves = group // images
    lane = lax.broadcasted_iota(jnp.int32, (1, rows), 1)
    which = lax.rem(lane, group)
    for copy in copies[: 1 + blocks]:
        copy.wait()
    keys = keys_ref[...]
    tok = tok_ref[...].reshape(rows, part)
    split = jnp.concatenate(
        [
            jnp.concatenate(
                [
                    keys[:, (j * halves + h) * lanes : (j * halves + h + 1) * lanes]
                    for j in range(blocks)
                ],
                axis=1,
            )
            for h in range(halves)
        ],
        axis=0,
    )
    each = mm(split, tok, NT)
    partial = each[:slots]
    for h in range(1, halves):
        partial = jnp.where(which < h * images, partial, each[h * slots : (h + 1) * slots])
    logits = partial
    for h in range(1, halves):
        ahead = pltpu.roll(partial, rows - h * images, 1)
        behind = pltpu.roll(partial, group - h * images, 1)
        logits = logits + jnp.where(which < (halves - h) * images, ahead, behind)
    tiles = rows // 128
    valid = lane < positions * group
    top = jnp.where(valid, logits, -jnp.inf)
    best = functools.reduce(jnp.maximum, [top[:, i * 128 : (i + 1) * 128] for i in range(tiles)])
    best = across_class(best, jnp.maximum, group)
    e = jnp.exp(top - jnp.concatenate([best] * tiles, axis=1))
    total = functools.reduce(jnp.add, [e[:, i * 128 : (i + 1) * 128] for i in range(tiles)])
    total = across_class(total, jnp.add, group)
    disp = e / jnp.concatenate([total] * tiles, axis=1)
    comb = jnp.where(valid, softmax_rows(logits), 0.0)

    def slot_sums(weights, x):
        wide = jnp.concatenate(
            [jnp.where(which == i, weights, 0.0) for i in range(group)], axis=0
        ).astype(BF)
        out = mm(wide, x).astype(BF)
        per = images * slots
        return jnp.concatenate(
            [
                out[h * per : (h + 1) * per, j * lanes : (j + 1) * lanes]
                for j in range(blocks)
                for h in range(halves)
            ],
            axis=1,
        )

    sums = [slot_sums(disp, tok)]
    for copy in copies[1 + blocks : 1 + 2 * blocks]:
        copy.wait()
    sums.append(slot_sums(comb, grad_ref[...].reshape(rows, part)))
    copies[-1].wait()
    perm = perm_ref[...]
    step = gb * k
    count = perm.shape[0]
    for i in range(slots // step):
        block = jnp.concatenate(
            [
                r[b * slots + i * step : b * slots + (i + 1) * step]
                for r in sums
                for b in range(images)
            ],
            axis=0,
        )
        send_ref[i * count : (i + 1) * count] = mm(perm, block).astype(BF)
    block = send_ref.shape[0] // n_expert
    c, l = position(inner)
    for i in range(inner):
        for j in range(outer):
            to = partner(c, j, outer) * inner + lax.rem(l + i, inner)
            leave_refs[i][j * block : (j + 1) * block] = send_ref[
                pl.ds(pl.multiple_of(to * block, block), block)
            ]


def own_kernel(tok_ref, keys_ref, disp_ref, comb_ref):
    keys = keys_ref[...]
    for m in range(tok_ref.shape[0]):
        logits = mm(keys, tok_ref[m], NT)
        e = jnp.exp(logits - jnp.max(logits, axis=1, keepdims=True))
        disp_ref[m] = (e / jnp.sum(e, axis=1, keepdims=True)).astype(BF)
        comb_ref[m] = softmax_rows(logits).astype(BF)


def expert_kernel(
    images, n_expert, k, gb, ahead, win_ref, bin_ref, wout_ref, t_ref, *rest
):
    rest = rest[ahead:]
    outer, inner = levels(n_expert)
    come_refs = rest[:outer]
    back_ref, got_ref = rest[outer:]
    rows = k * images
    c, l = position(inner)
    block = got_ref.shape[1]
    for j in range(outer):
        source = partner(c, j, outer, True) * inner
        for i in range(inner):
            got_ref[source + lax.rem(l + i, inner)] = come_refs[j][i * block : (i + 1) * block]
    width = got_ref.shape[2]
    total = n_expert * rows
    got = got_ref[...]
    rows_in = got[:, :rows].reshape(total, width)
    rows_grad = got[:, rows:].reshape(total, width)
    half = width // 2
    expert = lax.rem(lax.div(lax.broadcasted_iota(jnp.int32, (total, 1), 0), images), k)

    def own(parts):
        out = parts[0]
        for e in range(1, k):
            out = jnp.where(expert == e, parts[e], out)
        return out

    pre = own([mm(rows_in, win_ref[e]) + bin_ref[e : e + 1] for e in range(k)])
    cdf = 0.5 * (1.0 + lax.erf(pre * 0.7071067811865476))
    hidden = (pre * cdf).astype(BF)
    slope = cdf + pre * jnp.exp(-0.5 * pre * pre) * 0.3989422804014327
    out_part = own([mm(hidden, wout_ref[e]) for e in range(k)]).astype(BF)
    act_grad = own([mm(rows_grad, wout_ref[e], NT) for e in range(k)])
    pre_grad = (act_grad * slope).astype(BF)
    in_part = own([mm(pre_grad, win_ref[e], NT) for e in range(k)]).astype(BF)
    rows = gb * k * images
    t = t_ref[...]
    out_rows = t.shape[0]
    for i in range(n_expert // gb):
        stack = jnp.concatenate(
            [
                part[i * rows : (i + 1) * rows, h * half : (h + 1) * half]
                for part in (out_part, in_part)
                for h in range(2)
            ],
            axis=0,
        )
        back_ref[i * out_rows : (i + 1) * out_rows] = mm(t, stack).astype(BF)


def final_kernel(
    quarter, k, gb, home_ref, bias_ref, tok_ref, grad_ref, disp_ref, comb_ref, keys_ref, sel_ref, out_ref,
):
    slots = keys_ref.shape[0]
    step = gb * k
    blocks = slots // step
    per_block = home_ref.shape[0] // blocks
    sel = sel_ref[...]
    sums = [mm(sel, home_ref[i * per_block : (i + 1) * per_block]) for i in range(blocks)]

    def assemble(kind, m):
        halves = []
        for h in range(2):
            start = ((m * 2 + kind) * 2 + h) * step
            halves.append(jnp.concatenate([s[start : start + step] for s in sums], axis=0))
        return jnp.concatenate(halves, axis=1)

    keys = keys_ref[...]
    for m in range(quarter):
        slot_out = (assemble(0, m) + bias_ref[...]).astype(BF)
        slot_in_grad = assemble(1, m).astype(BF)
        comb_grad = mm(slot_out, grad_ref[m], NT)
        disp_grad = mm(slot_in_grad, tok_ref[m], NT)
        disp = disp_ref[m]
        comb = comb_ref[m].astype(F32)
        wide = disp.astype(F32)
        logit_grad = comb * (comb_grad - jnp.sum(comb * comb_grad, axis=0, keepdims=True))
        logit_grad = logit_grad + wide * (
            disp_grad - jnp.sum(wide * disp_grad, axis=1, keepdims=True)
        )
        logit_grad = logit_grad.astype(BF).astype(F32)
        left = jnp.concatenate([wide, logit_grad], axis=0).T.astype(BF)
        right = jnp.concatenate([slot_in_grad, keys], axis=0)
        out_ref[m] = mm(left, right).astype(BF)


def local(n_expert, n_hidden, tokens, slot_keys, w_in, b_in, w_out, b_out, out_grad):
    n_all = n_expert * n_hidden
    images, positions, width = tokens.shape
    quarter = images // n_hidden
    slots = slot_keys.shape[1]
    k, _, units = w_in.shape
    gb = block_of(n_expert)
    half = width // 2
    vmem = pl.BlockSpec(memory_space=pltpu.VMEM)
    keys = slot_keys.T

    order = np.arange(2 * images * gb * k).reshape(2, images, gb, k).transpose(2, 0, 3, 1)
    perm = one_hot_rows(order, order.size)
    send_rows = 2 * k * images
    outer, inner = levels(n_expert)
    hbm = pl.BlockSpec(memory_space=pltpu.HBM)
    smem = pl.BlockSpec(memory_space=pltpu.SMEM)
    group = 8
    lanes = 128
    part = width * images // group
    padded = -(-positions * group // 128) * 128 // group

    def in_hbm(x):
        return pltpu.with_memory_space_constraint(x, pltpu.HBM)

    def as_it_lies(x):
        x = x.transpose(1, 0, 2).reshape(positions, images, width // lanes, lanes)
        x = x.transpose(0, 2, 1, 3).reshape(positions, width // lanes * images, lanes)
        return in_hbm(x)

    first, *leave = pl.pallas_call(
        functools.partial(dispatch_kernel, images, quarter, k, gb, n_expert),
        out_shape=(jax.ShapeDtypeStruct((1,), jnp.int32),)
        + (jax.ShapeDtypeStruct((outer * send_rows, width), BF),) * inner,
        in_specs=[hbm] * 4,
        out_specs=(smem,) + (vmem,) * inner,
        scratch_shapes=[pltpu.VMEM((padded, group, part), BF)] * 2
        + [
            pltpu.VMEM(keys.shape, BF),
            pltpu.VMEM(perm.shape, BF),
            pltpu.VMEM((n_expert * send_rows, width), BF),
            pltpu.SemaphoreType.DMA((4,)),
        ],
        compiler_params=pltpu.CompilerParams(vmem_limit_bytes=DISPATCH_VMEM << 20),
        name="dispatch",
    )(as_it_lies(tokens), as_it_lies(out_grad), in_hbm(keys), in_hbm(jnp.asarray(perm)))

    everyone = [(c, l) for c in range(outer) for l in range(inner)]
    held = leave[:1]
    if inner == 2:
        pairs = [(c * inner + l, c * inner + 1 - l) for c, l in everyone]
        held.append(lax.ppermute(leave[1], "expert", pairs))
    both = [
        jnp.concatenate([r[j * send_rows : (j + 1) * send_rows] for r in held])
        for j in range(outer)
    ]
    *both, first = lax.optimization_barrier((*both, first))
    come = both[:1]
    for j in range(1, outer):
        pairs = [(c * inner + l, partner(c, j, outer) * inner + l) for c, l in everyone]
        come.append(lax.ppermute(both[j], "expert", pairs))

    mine = functools.partial(
        lax.dynamic_slice_in_dim, start_index=first[0], slice_size=quarter, axis=0
    )
    my_tok, my_grad = mine(tokens), mine(out_grad)
    disp, comb = pl.pallas_call(
        own_kernel,
        out_shape=(jax.ShapeDtypeStruct((quarter, slots, positions), BF),) * 2,
        in_specs=[vmem] * 2,
        out_specs=(vmem,) * 2,
        compiler_params=pltpu.CompilerParams(vmem_limit_bytes=8 << 20),
        cost_estimate=pl.CostEstimate(flops=1000000000, bytes_accessed=0, transcendentals=0),
        name="own_softmax",
    )(my_tok, keys)

    order = np.arange(2 * k * 2 * gb * images).reshape(2, 2, gb, k, n_hidden, quarter)
    order = order.transpose(2, 4, 0, 3, 5, 1)
    spread = one_hot_rows(order, order.size)
    back_rows = 2 * k * quarter * 2
    ahead = (my_tok, my_grad, disp, comb)
    back = pl.pallas_call(
        functools.partial(expert_kernel, images, n_expert, k, gb, len(ahead)),
        out_shape=jax.ShapeDtypeStruct((n_all * back_rows, half), BF),
        in_specs=[vmem] * 4 + [pl.BlockSpec(memory_space=pl.ANY)] * len(ahead) + [vmem] * outer,
        out_specs=vmem,
        scratch_shapes=[pltpu.VMEM((n_expert, send_rows, width), BF)],
        compiler_params=pltpu.CompilerParams(vmem_limit_bytes=20 << 20),
        name="experts",
    )(w_in, b_in, w_out, spread, *ahead, *come)

    home = lax.all_to_all(
        back.reshape(n_all, back_rows, half),
        ("expert", "hidden"),
        split_axis=0,
        concat_axis=0,
        tiled=True,
    )

    label = np.arange(quarter * 2 * 2 * gb * k).reshape(quarter, 2, 2, gb, k).transpose(3, 1, 4, 0, 2)
    label = np.broadcast_to(label[:, None], (gb, n_hidden) + label.shape[1:])
    select = np.ascontiguousarray(one_hot_rows(label, quarter * 4 * gb * k).T)
    return pl.pallas_call(
        functools.partial(final_kernel, quarter, k, gb),
        out_shape=jax.ShapeDtypeStruct((quarter, positions, width), BF),
        in_specs=[vmem] * 8,
        out_specs=vmem,
        compiler_params=pltpu.CompilerParams(vmem_limit_bytes=8 << 20),
        name="tokens_back",
    )(home.reshape(n_all * back_rows, half), b_out, my_tok, my_grad, disp, comb, keys, select)


def solution(mesh):
    return jax.shard_map(
        functools.partial(local, mesh.shape["expert"], mesh.shape["hidden"]),
        mesh=mesh,
        in_specs=(
            P("expert", None, None),
            P(),
            P("expert", None, "hidden"),
            P("expert", "hidden"),
            P("expert", "hidden", None),
            P(),
            P("expert", None, None),
        ),
        out_specs=P(("expert", "hidden"), None, None),
        check_vma=False,
    )
```

```python
import functools

import jax
import jax.numpy as jnp
import numpy as np
from jax import lax
from jax.experimental import pallas as pl
from jax.experimental.pallas import tpu as pltpu
from jax.sharding import PartitionSpec as P

BF = jnp.bfloat16
F32 = jnp.float32
NN = (((1,), (0,)), ((), ()))
NT = (((1,), (1,)), ((), ()))


def mm(a, b, dims=NN):
    return lax.dot_general(a, b, dims, preferred_element_type=F32)


def block_of(n_expert):
    return 8 if n_expert % 8 == 0 else n_expert


def one_hot_rows(source, count):
    return np.asarray(np.asarray(source).reshape(-1)[:, None] == np.arange(count)[None], BF)


def partner(me, j, n, back=False):
    if n & (n - 1) == 0:
        return me ^ j
    shifted = me + (n - j if back else j)
    return shifted % n if isinstance(me, int) else lax.rem(shifted, n)


def levels(n_expert):
    inner = 2 if n_expert % 2 == 0 else 1
    return n_expert // inner, inner


def position(inner):
    me = lax.axis_index("expert")
    return lax.div(me, inner), lax.rem(me, inner)


def load_kernel(count, *refs):
    sources, targets, sems = refs[:count], refs[count:-1], refs[-1]
    copies = [
        pltpu.make_async_copy(source, target, sems.at[i])
        for i, (source, target) in enumerate(zip(sources, targets))
    ]
    for copy in copies:
        copy.start()
    for copy in copies:
        copy.wait()


def load(*arrays):
    hbm = pl.BlockSpec(memory_space=pltpu.HBM)
    return pl.pallas_call(
        functools.partial(load_kernel, len(arrays)),
        out_shape=[jax.ShapeDtypeStruct(x.shape, x.dtype) for x in arrays],
        in_specs=[hbm] * len(arrays),
        out_specs=[pl.BlockSpec(memory_space=pltpu.VMEM)] * len(arrays),
        scratch_shapes=[pltpu.SemaphoreType.DMA((len(arrays),))],
        compiler_params=pltpu.CompilerParams(vmem_limit_bytes=8 << 20),
        cost_estimate=pl.CostEstimate(
            flops=0, bytes_accessed=4 * sum(x.size for x in arrays), transcendentals=0
        ),
        name="load",
    )(*(pltpu.with_memory_space_constraint(x, pltpu.HBM) for x in arrays))


def dispatch_kernel(
    images, quarter, k, gb, n_expert, tok_ref, grad_ref, keys_ref, perm_ref,
    disp_ref, comb_ref, my_tok_ref, my_grad_ref, *rest,
):
    outer, inner = levels(n_expert)
    leave_refs = rest[:inner]
    send_ref, disp_all, comb_all = rest[inner:]
    slots = keys_ref.shape[0]
    keys = keys_ref[...]
    slot_rows = [[], []]
    for b in range(images):
        tok = tok_ref[b]
        logits = mm(keys, tok, NT)
        e = jnp.exp(logits - jnp.max(logits, axis=1, keepdims=True))
        disp = (e / jnp.sum(e, axis=1, keepdims=True)).astype(BF)
        e = jnp.exp(logits - jnp.max(logits, axis=0, keepdims=True))
        comb = (e / jnp.sum(e, axis=0, keepdims=True)).astype(BF)
        disp_all[b] = disp
        comb_all[b] = comb
        slot_rows[0].append(mm(disp, tok).astype(BF))
        slot_rows[1].append(mm(comb, grad_ref[b]).astype(BF))
    perm = perm_ref[...]
    step = gb * k
    rows = perm.shape[0]
    for i in range(slots // step):
        block = jnp.concatenate(
            [r[i * step : (i + 1) * step] for kind in slot_rows for r in kind], axis=0
        )
        send_ref[i * rows : (i + 1) * rows] = mm(perm, block).astype(BF)
    block = send_ref.shape[0] // n_expert
    c, l = position(inner)
    for i in range(inner):
        for j in range(outer):
            to = partner(c, j, outer) * inner + lax.rem(l + i, inner)
            leave_refs[i][j * block : (j + 1) * block] = send_ref[
                pl.ds(pl.multiple_of(to * block, block), block)
            ]
    first = lax.axis_index("hidden") * quarter
    for m in range(quarter):
        disp_ref[m] = disp_all[first + m]
        comb_ref[m] = comb_all[first + m]
        my_tok_ref[m] = tok_ref[first + m]
        my_grad_ref[m] = grad_ref[first + m]


def expert_kernel(images, n_expert, k, gb, win_ref, bin_ref, wout_ref, t_ref, *rest):
    outer, inner = levels(n_expert)
    come_refs = rest[:outer]
    back_ref, got_ref = rest[outer:]
    rows = k * images
    c, l = position(inner)
    block = got_ref.shape[1]
    for j in range(outer):
        source = partner(c, j, outer, True) * inner
        for i in range(inner):
            got_ref[source + lax.rem(l + i, inner)] = come_refs[j][i * block : (i + 1) * block]
    width = got_ref.shape[2]
    total = n_expert * rows
    got = got_ref[...]
    rows_in = got[:, :rows].reshape(total, width)
    rows_grad = got[:, rows:].reshape(total, width)
    half = width // 2
    expert = lax.rem(lax.div(lax.broadcasted_iota(jnp.int32, (total, 1), 0), images), k)

    def own(parts):
        out = parts[0]
        for e in range(1, k):
            out = jnp.where(expert == e, parts[e], out)
        return out

    pre = own([mm(rows_in, win_ref[e]) + bin_ref[e : e + 1] for e in range(k)])
    cdf = 0.5 * (1.0 + lax.erf(pre * 0.7071067811865476))
    hidden = (pre * cdf).astype(BF)
    slope = cdf + pre * jnp.exp(-0.5 * pre * pre) * 0.3989422804014327
    out_part = own([mm(hidden, wout_ref[e]) for e in range(k)]).astype(BF)
    act_grad = own([mm(rows_grad, wout_ref[e], NT) for e in range(k)])
    pre_grad = (act_grad * slope).astype(BF)
    in_part = own([mm(pre_grad, win_ref[e], NT) for e in range(k)]).astype(BF)
    rows = gb * k * images
    t = t_ref[...]
    out_rows = t.shape[0]
    for i in range(n_expert // gb):
        stack = jnp.concatenate(
            [
                part[i * rows : (i + 1) * rows, h * half : (h + 1) * half]
                for part in (out_part, in_part)
                for h in range(2)
            ],
            axis=0,
        )
        back_ref[i * out_rows : (i + 1) * out_rows] = mm(t, stack).astype(BF)


def final_kernel(
    quarter, k, gb, home_ref, bias_ref, tok_ref, grad_ref, disp_ref, comb_ref, keys_ref, sel_ref, out_ref,
):
    slots = keys_ref.shape[0]
    step = gb * k
    blocks = slots // step
    per_block = home_ref.shape[0] // blocks
    sel = sel_ref[...]
    sums = [mm(sel, home_ref[i * per_block : (i + 1) * per_block]) for i in range(blocks)]

    def assemble(kind, m):
        halves = []
        for h in range(2):
            start = ((m * 2 + kind) * 2 + h) * step
            halves.append(jnp.concatenate([s[start : start + step] for s in sums], axis=0))
        return jnp.concatenate(halves, axis=1)

    keys = keys_ref[...]
    for m in range(quarter):
        slot_out = (assemble(0, m) + bias_ref[...]).astype(BF)
        slot_in_grad = assemble(1, m).astype(BF)
        comb_grad = mm(slot_out, grad_ref[m], NT)
        disp_grad = mm(slot_in_grad, tok_ref[m], NT)
        disp = disp_ref[m]
        comb = comb_ref[m].astype(F32)
        wide = disp.astype(F32)
        logit_grad = comb * (comb_grad - jnp.sum(comb * comb_grad, axis=0, keepdims=True))
        logit_grad = logit_grad + wide * (
            disp_grad - jnp.sum(wide * disp_grad, axis=1, keepdims=True)
        )
        logit_grad = logit_grad.astype(BF).astype(F32)
        left = jnp.concatenate([wide, logit_grad], axis=0).T.astype(BF)
        right = jnp.concatenate([slot_in_grad, keys], axis=0)
        out_ref[m] = mm(left, right).astype(BF)


def local(n_expert, n_hidden, tokens, slot_keys, w_in, b_in, w_out, b_out, out_grad):
    n_all = n_expert * n_hidden
    images, positions, width = tokens.shape
    quarter = images // n_hidden
    slots = slot_keys.shape[1]
    k, _, units = w_in.shape
    gb = block_of(n_expert)
    half = width // 2
    vmem = pl.BlockSpec(memory_space=pltpu.VMEM)
    keys = slot_keys.T

    order = np.arange(2 * images * gb * k).reshape(2, images, gb, k).transpose(2, 0, 3, 1)
    perm = one_hot_rows(order, order.size)
    send_rows = 2 * k * images
    keys, perm, *across = load(
        keys, jnp.asarray(perm), *(x.transpose(1, 0, 2) for x in (tokens, out_grad))
    )
    tokens, out_grad = (x.transpose(1, 0, 2) for x in across)
    outer, inner = levels(n_expert)
    disp, comb, my_tok, my_grad, *leave = pl.pallas_call(
        functools.partial(dispatch_kernel, images, quarter, k, gb, n_expert),
        out_shape=(
            jax.ShapeDtypeStruct((quarter, slots, positions), BF),
            jax.ShapeDtypeStruct((quarter, slots, positions), BF),
            jax.ShapeDtypeStruct((quarter, positions, width), BF),
            jax.ShapeDtypeStruct((quarter, positions, width), BF),
        )
        + (jax.ShapeDtypeStruct((outer * send_rows, width), BF),) * inner,
        in_specs=[vmem] * 4,
        out_specs=(vmem,) * (4 + inner),
        scratch_shapes=[pltpu.VMEM((n_expert * send_rows, width), BF)]
        + [pltpu.VMEM((images, slots, positions), BF)] * 2,
        compiler_params=pltpu.CompilerParams(vmem_limit_bytes=12 << 20),
        cost_estimate=pl.CostEstimate(flops=8000000000, bytes_accessed=0, transcendentals=0),
        name="dispatch",
    )(tokens, out_grad, keys, perm)

    everyone = [(c, l) for c in range(outer) for l in range(inner)]
    held = leave[:1]
    if inner == 2:
        pairs = [(c * inner + l, c * inner + 1 - l) for c, l in everyone]
        held.append(lax.ppermute(leave[1], "expert", pairs))
    come = []
    for j in range(outer):
        both = jnp.concatenate([r[j * send_rows : (j + 1) * send_rows] for r in held])
        pairs = [(c * inner + l, partner(c, j, outer) * inner + l) for c, l in everyone]
        come.append(lax.ppermute(both, "expert", pairs) if j else both)

    order = np.arange(2 * k * 2 * gb * images).reshape(2, 2, gb, k, n_hidden, quarter)
    order = order.transpose(2, 4, 0, 3, 5, 1)
    spread = one_hot_rows(order, order.size)
    back_rows = 2 * k * quarter * 2
    back = pl.pallas_call(
        functools.partial(expert_kernel, images, n_expert, k, gb),
        out_shape=jax.ShapeDtypeStruct((n_all * back_rows, half), BF),
        in_specs=[vmem] * (4 + outer),
        out_specs=vmem,
        scratch_shapes=[pltpu.VMEM((n_expert, send_rows, width), BF)],
        compiler_params=pltpu.CompilerParams(vmem_limit_bytes=20 << 20),
        name="experts",
    )(w_in, b_in, w_out, spread, *come)

    home = lax.all_to_all(
        back.reshape(n_all, back_rows, half),
        ("expert", "hidden"),
        split_axis=0,
        concat_axis=0,
        tiled=True,
    )

    label = np.arange(quarter * 2 * 2 * gb * k).reshape(quarter, 2, 2, gb, k).transpose(3, 1, 4, 0, 2)
    label = np.broadcast_to(label[:, None], (gb, n_hidden) + label.shape[1:])
    select = np.ascontiguousarray(one_hot_rows(label, quarter * 4 * gb * k).T)
    return pl.pallas_call(
        functools.partial(final_kernel, quarter, k, gb),
        out_shape=jax.ShapeDtypeStruct((quarter, positions, width), BF),
        in_specs=[vmem] * 8,
        out_specs=vmem,
        compiler_params=pltpu.CompilerParams(vmem_limit_bytes=8 << 20),
        name="tokens_back",
    )(home.reshape(n_all * back_rows, half), b_out, my_tok, my_grad, disp, comb, keys, select)


def solution(mesh):
    return jax.shard_map(
        functools.partial(local, mesh.shape["expert"], mesh.shape["hidden"]),
        mesh=mesh,
        in_specs=(
            P("expert", None, None),
            P(),
            P("expert", None, "hidden"),
            P("expert", "hidden"),
            P("expert", "hidden", None),
            P(),
            P("expert", None, None),
        ),
        out_specs=P(("expert", "hidden"), None, None),
        check_vma=False,
    )
```

```python
import functools

import jax
import jax.numpy as jnp
import numpy as np
from jax import lax
from jax.experimental import pallas as pl
from jax.experimental.pallas import tpu as pltpu
from jax.sharding import PartitionSpec as P

BF = jnp.bfloat16
F32 = jnp.float32
NN = (((1,), (0,)), ((), ()))
NT = (((1,), (1,)), ((), ()))


def mm(a, b, dims=NN):
    return lax.dot_general(a, b, dims, preferred_element_type=F32)


def block_of(n_expert):
    return 8 if n_expert % 8 == 0 else n_expert


def one_hot_rows(source, count):
    return np.asarray(np.asarray(source).reshape(-1)[:, None] == np.arange(count)[None], BF)


def partner(me, j, n, back=False):
    if n & (n - 1) == 0:
        return me ^ j
    shifted = me + (n - j if back else j)
    return shifted % n if isinstance(me, int) else lax.rem(shifted, n)


def levels(n_expert):
    inner = 2 if n_expert % 2 == 0 else 1
    return n_expert // inner, inner


def position(inner):
    me = lax.axis_index("expert")
    return lax.div(me, inner), lax.rem(me, inner)


def load_kernel(count, *refs):
    sources, targets, sems = refs[:count], refs[count:-1], refs[-1]
    copies = [
        pltpu.make_async_copy(source, target, sems.at[i])
        for i, (source, target) in enumerate(zip(sources, targets))
    ]
    for copy in copies:
        copy.start()
    for copy in copies:
        copy.wait()


def load(*arrays):
    hbm = pl.BlockSpec(memory_space=pltpu.HBM)
    return pl.pallas_call(
        functools.partial(load_kernel, len(arrays)),
        out_shape=[jax.ShapeDtypeStruct(x.shape, x.dtype) for x in arrays],
        in_specs=[hbm] * len(arrays),
        out_specs=[pl.BlockSpec(memory_space=pltpu.VMEM)] * len(arrays),
        scratch_shapes=[pltpu.SemaphoreType.DMA((len(arrays),))],
        compiler_params=pltpu.CompilerParams(vmem_limit_bytes=8 << 20),
        cost_estimate=pl.CostEstimate(
            flops=0, bytes_accessed=4 * sum(x.size for x in arrays), transcendentals=0
        ),
        name="load",
    )(*(pltpu.with_memory_space_constraint(x, pltpu.HBM) for x in arrays))


def slots_in_kernel(
    images, quarter, tok_ref, keys_ref, sums_ref, all_ref, disp_ref, comb_ref, my_tok_ref, disp_all
):
    slots = keys_ref.shape[0]
    keys = keys_ref[...]
    for b in range(images):
        tok = tok_ref[b]
        logits = mm(keys, tok, NT)
        e = jnp.exp(logits - jnp.max(logits, axis=1, keepdims=True))
        disp = (e / jnp.sum(e, axis=1, keepdims=True)).astype(BF)
        e = jnp.exp(logits - jnp.max(logits, axis=0, keepdims=True))
        comb = (e / jnp.sum(e, axis=0, keepdims=True)).astype(BF)
        disp_all[b] = disp
        all_ref[b] = comb
        sums_ref[b * slots : (b + 1) * slots] = mm(disp, tok).astype(BF)
    first = lax.axis_index("hidden") * quarter
    for m in range(quarter):
        disp_ref[m] = disp_all[first + m]
        comb_ref[m] = all_ref[first + m]
        my_tok_ref[m] = tok_ref[first + m]


def slots_grad_kernel(
    images, quarter, k, gb, n_expert, grad_ref, comb_ref, sums_ref, perm_ref, my_grad_ref, *rest
):
    outer, inner = levels(n_expert)
    leave_refs = rest[:inner]
    send_ref = rest[inner]
    slots = comb_ref.shape[1]
    sums = sums_ref[...]
    slot_rows = [sums[b * slots : (b + 1) * slots] for b in range(images)]
    slot_rows += [mm(comb_ref[b], grad_ref[b]).astype(BF) for b in range(images)]
    perm = perm_ref[...]
    step = gb * k
    rows = perm.shape[0]
    for i in range(slots // step):
        block = jnp.concatenate([r[i * step : (i + 1) * step] for r in slot_rows], axis=0)
        send_ref[i * rows : (i + 1) * rows] = mm(perm, block).astype(BF)
    block = send_ref.shape[0] // n_expert
    c, l = position(inner)
    for i in range(inner):
        for j in range(outer):
            to = partner(c, j, outer) * inner + lax.rem(l + i, inner)
            leave_refs[i][j * block : (j + 1) * block] = send_ref[
                pl.ds(pl.multiple_of(to * block, block), block)
            ]
    first = lax.axis_index("hidden") * quarter
    for m in range(quarter):
        my_grad_ref[m] = grad_ref[first + m]


def expert_kernel(images, n_expert, k, gb, win_ref, bin_ref, wout_ref, t_ref, *rest):
    outer, inner = levels(n_expert)
    come_refs = rest[:outer]
    back_ref, got_ref = rest[outer:]
    rows = k * images
    c, l = position(inner)
    block = got_ref.shape[1]
    for j in range(outer):
        source = partner(c, j, outer, True) * inner
        for i in range(inner):
            got_ref[source + lax.rem(l + i, inner)] = come_refs[j][i * block : (i + 1) * block]
    width = got_ref.shape[2]
    total = n_expert * rows
    got = got_ref[...]
    rows_in = got[:, :rows].reshape(total, width)
    rows_grad = got[:, rows:].reshape(total, width)
    half = width // 2
    expert = lax.rem(lax.div(lax.broadcasted_iota(jnp.int32, (total, 1), 0), images), k)

    def own(parts):
        out = parts[0]
        for e in range(1, k):
            out = jnp.where(expert == e, parts[e], out)
        return out

    pre = own([mm(rows_in, win_ref[e]) + bin_ref[e : e + 1] for e in range(k)])
    cdf = 0.5 * (1.0 + lax.erf(pre * 0.7071067811865476))
    hidden = (pre * cdf).astype(BF)
    slope = cdf + pre * jnp.exp(-0.5 * pre * pre) * 0.3989422804014327
    out_part = own([mm(hidden, wout_ref[e]) for e in range(k)]).astype(BF)
    act_grad = own([mm(rows_grad, wout_ref[e], NT) for e in range(k)])
    pre_grad = (act_grad * slope).astype(BF)
    in_part = own([mm(pre_grad, win_ref[e], NT) for e in range(k)]).astype(BF)
    rows = gb * k * images
    t = t_ref[...]
    out_rows = t.shape[0]
    for i in range(n_expert // gb):
        stack = jnp.concatenate(
            [
                part[i * rows : (i + 1) * rows, h * half : (h + 1) * half]
                for part in (out_part, in_part)
                for h in range(2)
            ],
            axis=0,
        )
        back_ref[i * out_rows : (i + 1) * out_rows] = mm(t, stack).astype(BF)


def final_kernel(
    quarter, k, gb, home_ref, bias_ref, tok_ref, grad_ref, disp_ref, comb_ref, keys_ref, sel_ref, out_ref,
):
    slots = keys_ref.shape[0]
    step = gb * k
    blocks = slots // step
    per_block = home_ref.shape[0] // blocks
    sel = sel_ref[...]
    sums = [mm(sel, home_ref[i * per_block : (i + 1) * per_block]) for i in range(blocks)]

    def assemble(kind, m):
        halves = []
        for h in range(2):
            start = ((m * 2 + kind) * 2 + h) * step
            halves.append(jnp.concatenate([s[start : start + step] for s in sums], axis=0))
        return jnp.concatenate(halves, axis=1)

    keys = keys_ref[...]
    for m in range(quarter):
        slot_out = (assemble(0, m) + bias_ref[...]).astype(BF)
        slot_in_grad = assemble(1, m).astype(BF)
        comb_grad = mm(slot_out, grad_ref[m], NT)
        disp_grad = mm(slot_in_grad, tok_ref[m], NT)
        disp = disp_ref[m]
        comb = comb_ref[m].astype(F32)
        wide = disp.astype(F32)
        logit_grad = comb * (comb_grad - jnp.sum(comb * comb_grad, axis=0, keepdims=True))
        logit_grad = logit_grad + wide * (
            disp_grad - jnp.sum(wide * disp_grad, axis=1, keepdims=True)
        )
        logit_grad = logit_grad.astype(BF).astype(F32)
        left = jnp.concatenate([wide, logit_grad], axis=0).T.astype(BF)
        right = jnp.concatenate([slot_in_grad, keys], axis=0)
        out_ref[m] = mm(left, right).astype(BF)


def local(n_expert, n_hidden, tokens, slot_keys, w_in, b_in, w_out, b_out, out_grad):
    n_all = n_expert * n_hidden
    images, positions, width = tokens.shape
    quarter = images // n_hidden
    slots = slot_keys.shape[1]
    k, _, units = w_in.shape
    gb = block_of(n_expert)
    half = width // 2
    vmem = pl.BlockSpec(memory_space=pltpu.VMEM)
    keys = slot_keys.T

    order = np.arange(2 * images * gb * k).reshape(2, images, gb, k).transpose(2, 0, 3, 1)
    perm = one_hot_rows(order, order.size)
    send_rows = 2 * k * images
    keys, perm, across = load(keys, jnp.asarray(perm), tokens.transpose(1, 0, 2))
    outer, inner = levels(n_expert)
    shape = jax.ShapeDtypeStruct
    sums, comb_all, disp, comb, my_tok = pl.pallas_call(
        functools.partial(slots_in_kernel, images, quarter),
        out_shape=(
            shape((images * slots, width), BF),
            shape((images, slots, positions), BF),
            shape((quarter, slots, positions), BF),
            shape((quarter, slots, positions), BF),
            shape((quarter, positions, width), BF),
        ),
        in_specs=[vmem] * 2,
        out_specs=(vmem,) * 5,
        scratch_shapes=[pltpu.VMEM((images, slots, positions), BF)],
        compiler_params=pltpu.CompilerParams(vmem_limit_bytes=10 << 20),
        name="slots_in",
    )(across.transpose(1, 0, 2), keys)
    out_grad, comb_all = lax.optimization_barrier((out_grad, comb_all))
    my_grad, *leave = pl.pallas_call(
        functools.partial(slots_grad_kernel, images, quarter, k, gb, n_expert),
        out_shape=(shape((quarter, positions, width), BF),)
        + (shape((outer * send_rows, width), BF),) * inner,
        in_specs=[vmem] * 4,
        out_specs=(vmem,) * (1 + inner),
        scratch_shapes=[pltpu.VMEM((n_expert * send_rows, width), BF)],
        compiler_params=pltpu.CompilerParams(vmem_limit_bytes=10 << 20),
        cost_estimate=pl.CostEstimate(flops=8000000000, bytes_accessed=0, transcendentals=0),
        name="slots_grad",
    )(out_grad, comb_all, sums, perm)

    everyone = [(c, l) for c in range(outer) for l in range(inner)]
    held = leave[:1]
    if inner == 2:
        pairs = [(c * inner + l, c * inner + 1 - l) for c, l in everyone]
        held.append(lax.ppermute(leave[1], "expert", pairs))
    come = []
    for j in range(outer):
        both = jnp.concatenate([r[j * send_rows : (j + 1) * send_rows] for r in held])
        pairs = [(c * inner + l, partner(c, j, outer) * inner + l) for c, l in everyone]
        come.append(lax.ppermute(both, "expert", pairs) if j else both)

    order = np.arange(2 * k * 2 * gb * images).reshape(2, 2, gb, k, n_hidden, quarter)
    order = order.transpose(2, 4, 0, 3, 5, 1)
    spread = one_hot_rows(order, order.size)
    back_rows = 2 * k * quarter * 2
    back = pl.pallas_call(
        functools.partial(expert_kernel, images, n_expert, k, gb),
        out_shape=jax.ShapeDtypeStruct((n_all * back_rows, half), BF),
        in_specs=[vmem] * (4 + outer),
        out_specs=vmem,
        scratch_shapes=[pltpu.VMEM((n_expert, send_rows, width), BF)],
        compiler_params=pltpu.CompilerParams(vmem_limit_bytes=20 << 20),
        name="experts",
    )(w_in, b_in, w_out, spread, *come)

    home = lax.all_to_all(
        back.reshape(n_all, back_rows, half),
        ("expert", "hidden"),
        split_axis=0,
        concat_axis=0,
        tiled=True,
    )

    label = np.arange(quarter * 2 * 2 * gb * k).reshape(quarter, 2, 2, gb, k).transpose(3, 1, 4, 0, 2)
    label = np.broadcast_to(label[:, None], (gb, n_hidden) + label.shape[1:])
    select = np.ascontiguousarray(one_hot_rows(label, quarter * 4 * gb * k).T)
    return pl.pallas_call(
        functools.partial(final_kernel, quarter, k, gb),
        out_shape=jax.ShapeDtypeStruct((quarter, positions, width), BF),
        in_specs=[vmem] * 8,
        out_specs=vmem,
        compiler_params=pltpu.CompilerParams(vmem_limit_bytes=8 << 20),
        name="tokens_back",
    )(home.reshape(n_all * back_rows, half), b_out, my_tok, my_grad, disp, comb, keys, select)


def solution(mesh):
    return jax.shard_map(
        functools.partial(local, mesh.shape["expert"], mesh.shape["hidden"]),
        mesh=mesh,
        in_specs=(
            P("expert", None, None),
            P(),
            P("expert", None, "hidden"),
            P("expert", "hidden"),
            P("expert", "hidden", None),
            P(),
            P("expert", None, None),
        ),
        out_specs=P(("expert", "hidden"), None, None),
        check_vma=False,
    )
```

```python
import functools

import jax
import jax.numpy as jnp
import numpy as np
from jax import lax
from jax.experimental import pallas as pl
from jax.experimental.pallas import tpu as pltpu
from jax.sharding import PartitionSpec as P

BF = jnp.bfloat16
F32 = jnp.float32
NN = (((1,), (0,)), ((), ()))
NT = (((1,), (1,)), ((), ()))


def mm(a, b, dims=NN):
    return lax.dot_general(a, b, dims, preferred_element_type=F32)


def block_of(n_expert):
    return 8 if n_expert % 8 == 0 else n_expert


def one_hot_rows(source, count):
    return np.asarray(np.asarray(source).reshape(-1)[:, None] == np.arange(count)[None], BF)


def partner(me, j, n, back=False):
    if n & (n - 1) == 0:
        return me ^ j
    shifted = me + (n - j if back else j)
    return shifted % n if isinstance(me, int) else lax.rem(shifted, n)


def levels(n_expert):
    inner = 2 if n_expert % 2 == 0 else 1
    return n_expert // inner, inner


def turn(l, j, outer):
    if j == 0:
        return 0
    steps = [outer - 1, *range(1, outer - 1)]
    mine, other = steps[j - 1], steps[j - 2]
    if isinstance(l, int):
        return other if l else mine
    return jnp.where(l == 1, other, mine)


def position(inner):
    me = lax.axis_index("expert")
    return lax.div(me, inner), lax.rem(me, inner)


def dispatch_kernel(
    images, quarter, k, gb, n_expert, tok_ref, grad_ref, keys_ref, perm_ref,
    disp_ref, comb_ref, my_tok_ref, my_grad_ref, *rest,
):
    outer, inner = levels(n_expert)
    leave_refs = rest[:inner]
    send_ref, disp_all, comb_all = rest[inner:]
    slots = keys_ref.shape[0]
    keys = keys_ref[...]
    slot_rows = [[], []]
    for b in range(images):
        tok = tok_ref[b]
        logits = mm(keys, tok, NT)
        e = jnp.exp(logits - jnp.max(logits, axis=1, keepdims=True))
        disp = (e / jnp.sum(e, axis=1, keepdims=True)).astype(BF)
        e = jnp.exp(logits - jnp.max(logits, axis=0, keepdims=True))
        comb = (e / jnp.sum(e, axis=0, keepdims=True)).astype(BF)
        disp_all[b] = disp
        comb_all[b] = comb
        slot_rows[0].append(mm(disp, tok).astype(BF))
        slot_rows[1].append(mm(comb, grad_ref[b]).astype(BF))
    perm = perm_ref[...]
    step = gb * k
    rows = perm.shape[0]
    for i in range(slots // step):
        block = jnp.concatenate(
            [r[i * step : (i + 1) * step] for kind in slot_rows for r in kind], axis=0
        )
        send_ref[i * rows : (i + 1) * rows] = mm(perm, block).astype(BF)
    block = send_ref.shape[0] // n_expert
    c, l = position(inner)
    for i in range(inner):
        for j in range(outer):
            core = lax.rem(l + i, inner)
            to = partner(c, turn(core, j, outer), outer) * inner + core
            leave_refs[i][j * block : (j + 1) * block] = send_ref[
                pl.ds(pl.multiple_of(to * block, block), block)
            ]
    first = lax.axis_index("hidden") * quarter
    for m in range(quarter):
        disp_ref[m] = disp_all[first + m]
        comb_ref[m] = comb_all[first + m]
        my_tok_ref[m] = tok_ref[first + m]
        my_grad_ref[m] = grad_ref[first + m]


def expert_kernel(images, n_expert, k, gb, win_ref, bin_ref, wout_ref, t_ref, *rest):
    outer, inner = levels(n_expert)
    come_refs = rest[:outer]
    back_ref, got_ref = rest[outer:]
    rows = k * images
    c, l = position(inner)
    block = got_ref.shape[1]
    for j in range(outer):
        source = partner(c, turn(l, j, outer), outer, True) * inner
        for i in range(inner):
            got_ref[source + lax.rem(l + i, inner)] = come_refs[j][i * block : (i + 1) * block]
    width = got_ref.shape[2]
    total = n_expert * rows
    got = got_ref[...]
    rows_in = got[:, :rows].reshape(total, width)
    rows_grad = got[:, rows:].reshape(total, width)
    half = width // 2
    expert = lax.rem(lax.div(lax.broadcasted_iota(jnp.int32, (total, 1), 0), images), k)

    def own(parts):
        out = parts[0]
        for e in range(1, k):
            out = jnp.where(expert == e, parts[e], out)
        return out

    pre = own([mm(rows_in, win_ref[e]) + bin_ref[e : e + 1] for e in range(k)])
    cdf = 0.5 * (1.0 + lax.erf(pre * 0.7071067811865476))
    hidden = (pre * cdf).astype(BF)
    slope = cdf + pre * jnp.exp(-0.5 * pre * pre) * 0.3989422804014327
    out_part = own([mm(hidden, wout_ref[e]) for e in range(k)]).astype(BF)
    act_grad = own([mm(rows_grad, wout_ref[e], NT) for e in range(k)])
    pre_grad = (act_grad * slope).astype(BF)
    in_part = own([mm(pre_grad, win_ref[e], NT) for e in range(k)]).astype(BF)
    rows = gb * k * images
    t = t_ref[...]
    out_rows = t.shape[0]
    for i in range(n_expert // gb):
        stack = jnp.concatenate(
            [
                part[i * rows : (i + 1) * rows, h * half : (h + 1) * half]
                for part in (out_part, in_part)
                for h in range(2)
            ],
            axis=0,
        )
        back_ref[i * out_rows : (i + 1) * out_rows] = mm(t, stack).astype(BF)


def final_kernel(
    quarter, k, gb, home_ref, bias_ref, tok_ref, grad_ref, disp_ref, comb_ref, keys_ref, sel_ref, out_ref,
):
    slots = keys_ref.shape[0]
    step = gb * k
    blocks = slots // step
    per_block = home_ref.shape[0] // blocks
    sel = sel_ref[...]
    sums = [mm(sel, home_ref[i * per_block : (i + 1) * per_block]) for i in range(blocks)]

    def assemble(kind, m):
        halves = []
        for h in range(2):
            start = ((m * 2 + kind) * 2 + h) * step
            halves.append(jnp.concatenate([s[start : start + step] for s in sums], axis=0))
        return jnp.concatenate(halves, axis=1)

    keys = keys_ref[...]
    for m in range(quarter):
        slot_out = (assemble(0, m) + bias_ref[...]).astype(BF)
        slot_in_grad = assemble(1, m).astype(BF)
        comb_grad = mm(slot_out, grad_ref[m], NT)
        disp_grad = mm(slot_in_grad, tok_ref[m], NT)
        disp = disp_ref[m]
        comb = comb_ref[m].astype(F32)
        wide = disp.astype(F32)
        logit_grad = comb * (comb_grad - jnp.sum(comb * comb_grad, axis=0, keepdims=True))
        logit_grad = logit_grad + wide * (
            disp_grad - jnp.sum(wide * disp_grad, axis=1, keepdims=True)
        )
        logit_grad = logit_grad.astype(BF).astype(F32)
        left = jnp.concatenate([wide, logit_grad], axis=0).T.astype(BF)
        right = jnp.concatenate([slot_in_grad, keys], axis=0)
        out_ref[m] = mm(left, right).astype(BF)


def local(n_expert, n_hidden, tokens, slot_keys, w_in, b_in, w_out, b_out, out_grad):
    n_all = n_expert * n_hidden
    images, positions, width = tokens.shape
    quarter = images // n_hidden
    slots = slot_keys.shape[1]
    k, _, units = w_in.shape
    gb = block_of(n_expert)
    half = width // 2
    vmem = pl.BlockSpec(memory_space=pltpu.VMEM)
    keys = slot_keys.T

    order = np.arange(2 * images * gb * k).reshape(2, images, gb, k).transpose(2, 0, 3, 1)
    perm = one_hot_rows(order, order.size)
    send_rows = 2 * k * images
    outer, inner = levels(n_expert)
    disp, comb, my_tok, my_grad, *leave = pl.pallas_call(
        functools.partial(dispatch_kernel, images, quarter, k, gb, n_expert),
        out_shape=(
            jax.ShapeDtypeStruct((quarter, slots, positions), BF),
            jax.ShapeDtypeStruct((quarter, slots, positions), BF),
            jax.ShapeDtypeStruct((quarter, positions, width), BF),
            jax.ShapeDtypeStruct((quarter, positions, width), BF),
        )
        + (jax.ShapeDtypeStruct((outer * send_rows, width), BF),) * inner,
        in_specs=[vmem] * 4,
        out_specs=(vmem,) * (4 + inner),
        scratch_shapes=[pltpu.VMEM((n_expert * send_rows, width), BF)]
        + [pltpu.VMEM((images, slots, positions), BF)] * 2,
        compiler_params=pltpu.CompilerParams(vmem_limit_bytes=12 << 20),
        cost_estimate=pl.CostEstimate(flops=8000000000, bytes_accessed=0, transcendentals=0),
        name="dispatch",
    )(tokens, out_grad, keys, perm)

    everyone = [(c, l) for c in range(outer) for l in range(inner)]
    held = leave[:1]
    if inner == 2:
        pairs = [(c * inner + l, c * inner + 1 - l) for c, l in everyone]
        held.append(lax.ppermute(leave[1], "expert", pairs))
    come = []
    for j in range(outer):
        both = jnp.concatenate([r[j * send_rows : (j + 1) * send_rows] for r in held])
        pairs = [
            (c * inner + l, partner(c, turn(l, j, outer), outer) * inner + l) for c, l in everyone
        ]
        come.append(lax.ppermute(both, "expert", pairs) if j else both)

    order = np.arange(2 * k * 2 * gb * images).reshape(2, 2, gb, k, n_hidden, quarter)
    order = order.transpose(2, 4, 0, 3, 5, 1)
    spread = one_hot_rows(order, order.size)
    back_rows = 2 * k * quarter * 2
    back = pl.pallas_call(
        functools.partial(expert_kernel, images, n_expert, k, gb),
        out_shape=jax.ShapeDtypeStruct((n_all * back_rows, half), BF),
        in_specs=[vmem] * (4 + outer),
        out_specs=vmem,
        scratch_shapes=[pltpu.VMEM((n_expert, send_rows, width), BF)],
        compiler_params=pltpu.CompilerParams(vmem_limit_bytes=20 << 20),
        name="experts",
    )(w_in, b_in, w_out, spread, *come)

    home = lax.all_to_all(
        back.reshape(n_all, back_rows, half),
        ("expert", "hidden"),
        split_axis=0,
        concat_axis=0,
        tiled=True,
    )

    label = np.arange(quarter * 2 * 2 * gb * k).reshape(quarter, 2, 2, gb, k).transpose(3, 1, 4, 0, 2)
    label = np.broadcast_to(label[:, None], (gb, n_hidden) + label.shape[1:])
    select = np.ascontiguousarray(one_hot_rows(label, quarter * 4 * gb * k).T)
    return pl.pallas_call(
        functools.partial(final_kernel, quarter, k, gb),
        out_shape=jax.ShapeDtypeStruct((quarter, positions, width), BF),
        in_specs=[vmem] * 8,
        out_specs=vmem,
        compiler_params=pltpu.CompilerParams(vmem_limit_bytes=8 << 20),
        name="tokens_back",
    )(home.reshape(n_all * back_rows, half), b_out, my_tok, my_grad, disp, comb, keys, select)


def solution(mesh):
    return jax.shard_map(
        functools.partial(local, mesh.shape["expert"], mesh.shape["hidden"]),
        mesh=mesh,
        in_specs=(
            P("expert", None, None),
            P(),
            P("expert", None, "hidden"),
            P("expert", "hidden"),
            P("expert", "hidden", None),
            P(),
            P("expert", None, None),
        ),
        out_specs=P(("expert", "hidden"), None, None),
        check_vma=False,
    )
```

```python
import functools

import jax
import jax.numpy as jnp
import numpy as np
from jax import lax
from jax.experimental import pallas as pl
from jax.experimental.pallas import tpu as pltpu
from jax.sharding import PartitionSpec as P

BF = jnp.bfloat16
F32 = jnp.float32
NN = (((1,), (0,)), ((), ()))
NT = (((1,), (1,)), ((), ()))


def mm(a, b, dims=NN):
    return lax.dot_general(a, b, dims, preferred_element_type=F32)


def block_of(n_expert):
    return 8 if n_expert % 8 == 0 else n_expert


def one_hot_rows(source, count):
    return np.asarray(np.asarray(source).reshape(-1)[:, None] == np.arange(count)[None], BF)


def partner(me, j, n, back=False):
    if n & (n - 1) == 0:
        return me ^ j
    shifted = me + (n - j if back else j)
    return shifted % n if isinstance(me, int) else lax.rem(shifted, n)


def levels(n_expert):
    inner = 2 if n_expert % 2 == 0 else 1
    return n_expert // inner, inner


def position(inner):
    me = lax.axis_index("expert")
    return lax.div(me, inner), lax.rem(me, inner)


def dispatch_kernel(
    images, quarter, k, gb, n_expert, tok_ref, grad_ref, keys_ref, perm_ref,
    disp_ref, comb_ref, my_tok_ref, my_grad_ref, *rest,
):
    outer, inner = levels(n_expert)
    keep_ref, *give_refs = rest[: 2 * inner - 1]
    send_ref, disp_all, comb_all = rest[2 * inner - 1 :]
    slots = keys_ref.shape[0]
    keys = keys_ref[...]
    slot_rows = [[], []]
    for b in range(images):
        tok = tok_ref[b]
        logits = mm(keys, tok, NT)
        e = jnp.exp(logits - jnp.max(logits, axis=1, keepdims=True))
        disp = (e / jnp.sum(e, axis=1, keepdims=True)).astype(BF)
        e = jnp.exp(logits - jnp.max(logits, axis=0, keepdims=True))
        comb = (e / jnp.sum(e, axis=0, keepdims=True)).astype(BF)
        disp_all[b] = disp
        comb_all[b] = comb
        slot_rows[0].append(mm(disp, tok).astype(BF))
        slot_rows[1].append(mm(comb, grad_ref[b]).astype(BF))
    perm = perm_ref[...]
    step = gb * k
    rows = perm.shape[0]
    for i in range(slots // step):
        block = jnp.concatenate(
            [r[i * step : (i + 1) * step] for kind in slot_rows for r in kind], axis=0
        )
        send_ref[i * rows : (i + 1) * rows] = mm(perm, block).astype(BF)
    block = send_ref.shape[0] // n_expert
    c, l = position(inner)
    for i in range(inner):
        for j in range(outer):
            to = partner(c, j, outer) * inner + lax.rem(l + i, inner)
            rows = send_ref[pl.ds(pl.multiple_of(to * block, block), block)]
            if i == 0:
                keep_ref[j * block : (j + 1) * block] = rows
            elif j == 0:
                give_refs[1][...] = rows
            else:
                give_refs[0][(j - 1) * block : j * block] = rows
    first = lax.axis_index("hidden") * quarter
    for m in range(quarter):
        disp_ref[m] = disp_all[first + m]
        comb_ref[m] = comb_all[first + m]
        my_tok_ref[m] = tok_ref[first + m]
        my_grad_ref[m] = grad_ref[first + m]


def expert_kernel(images, n_expert, k, gb, win_ref, bin_ref, wout_ref, t_ref, *rest):
    outer, inner = levels(n_expert)
    come_refs = rest[: outer + inner - 1]
    back_ref, got_ref = rest[outer + inner - 1 :]
    rows = k * images
    c, l = position(inner)
    block = got_ref.shape[1]
    for j in range(outer):
        source = partner(c, j, outer, True) * inner
        for i in range(inner):
            if j == 0:
                rows_here = come_refs[i * outer][:block]
            else:
                rows_here = come_refs[j][i * block : (i + 1) * block]
            got_ref[source + lax.rem(l + i, inner)] = rows_here
    width = got_ref.shape[2]
    total = n_expert * rows
    got = got_ref[...]
    rows_in = got[:, :rows].reshape(total, width)
    rows_grad = got[:, rows:].reshape(total, width)
    half = width // 2
    expert = lax.rem(lax.div(lax.broadcasted_iota(jnp.int32, (total, 1), 0), images), k)

    def own(parts):
        out = parts[0]
        for e in range(1, k):
            out = jnp.where(expert == e, parts[e], out)
        return out

    pre = own([mm(rows_in, win_ref[e]) + bin_ref[e : e + 1] for e in range(k)])
    cdf = 0.5 * (1.0 + lax.erf(pre * 0.7071067811865476))
    hidden = (pre * cdf).astype(BF)
    slope = cdf + pre * jnp.exp(-0.5 * pre * pre) * 0.3989422804014327
    out_part = own([mm(hidden, wout_ref[e]) for e in range(k)]).astype(BF)
    act_grad = own([mm(rows_grad, wout_ref[e], NT) for e in range(k)])
    pre_grad = (act_grad * slope).astype(BF)
    in_part = own([mm(pre_grad, win_ref[e], NT) for e in range(k)]).astype(BF)
    rows = gb * k * images
    t = t_ref[...]
    out_rows = t.shape[0]
    for i in range(n_expert // gb):
        stack = jnp.concatenate(
            [
                part[i * rows : (i + 1) * rows, h * half : (h + 1) * half]
                for part in (out_part, in_part)
                for h in range(2)
            ],
            axis=0,
        )
        back_ref[i * out_rows : (i + 1) * out_rows] = mm(t, stack).astype(BF)


def final_kernel(
    quarter, k, gb, home_ref, bias_ref, tok_ref, grad_ref, disp_ref, comb_ref, keys_ref, sel_ref, out_ref,
):
    slots = keys_ref.shape[0]
    step = gb * k
    blocks = slots // step
    per_block = home_ref.shape[0] // blocks
    sel = sel_ref[...]
    sums = [mm(sel, home_ref[i * per_block : (i + 1) * per_block]) for i in range(blocks)]

    def assemble(kind, m):
        halves = []
        for h in range(2):
            start = ((m * 2 + kind) * 2 + h) * step
            halves.append(jnp.concatenate([s[start : start + step] for s in sums], axis=0))
        return jnp.concatenate(halves, axis=1)

    keys = keys_ref[...]
    for m in range(quarter):
        slot_out = (assemble(0, m) + bias_ref[...]).astype(BF)
        slot_in_grad = assemble(1, m).astype(BF)
        comb_grad = mm(slot_out, grad_ref[m], NT)
        disp_grad = mm(slot_in_grad, tok_ref[m], NT)
        disp = disp_ref[m]
        comb = comb_ref[m].astype(F32)
        wide = disp.astype(F32)
        logit_grad = comb * (comb_grad - jnp.sum(comb * comb_grad, axis=0, keepdims=True))
        logit_grad = logit_grad + wide * (
            disp_grad - jnp.sum(wide * disp_grad, axis=1, keepdims=True)
        )
        logit_grad = logit_grad.astype(BF).astype(F32)
        left = jnp.concatenate([wide, logit_grad], axis=0).T.astype(BF)
        right = jnp.concatenate([slot_in_grad, keys], axis=0)
        out_ref[m] = mm(left, right).astype(BF)


def local(n_expert, n_hidden, tokens, slot_keys, w_in, b_in, w_out, b_out, out_grad):
    n_all = n_expert * n_hidden
    images, positions, width = tokens.shape
    quarter = images // n_hidden
    slots = slot_keys.shape[1]
    k, _, units = w_in.shape
    gb = block_of(n_expert)
    half = width // 2
    vmem = pl.BlockSpec(memory_space=pltpu.VMEM)
    keys = slot_keys.T

    order = np.arange(2 * images * gb * k).reshape(2, images, gb, k).transpose(2, 0, 3, 1)
    perm = one_hot_rows(order, order.size)
    send_rows = 2 * k * images
    outer, inner = levels(n_expert)
    counts = [outer] + [outer - 1, 1] * (inner - 1)
    disp, comb, my_tok, my_grad, keep, *give = pl.pallas_call(
        functools.partial(dispatch_kernel, images, quarter, k, gb, n_expert),
        out_shape=(
            jax.ShapeDtypeStruct((quarter, slots, positions), BF),
            jax.ShapeDtypeStruct((quarter, slots, positions), BF),
            jax.ShapeDtypeStruct((quarter, positions, width), BF),
            jax.ShapeDtypeStruct((quarter, positions, width), BF),
        )
        + tuple(jax.ShapeDtypeStruct((n * send_rows, width), BF) for n in counts),
        in_specs=[vmem] * 4,
        out_specs=(vmem,) * (4 + len(counts)),
        scratch_shapes=[pltpu.VMEM((n_expert * send_rows, width), BF)]
        + [pltpu.VMEM((images, slots, positions), BF)] * 2,
        compiler_params=pltpu.CompilerParams(vmem_limit_bytes=12 << 20),
        cost_estimate=pl.CostEstimate(flops=8000000000, bytes_accessed=0, transcendentals=0),
        name="dispatch",
    )(tokens, out_grad, keys, perm)

    everyone = [(c, l) for c in range(outer) for l in range(inner)]
    swap = [(c * inner + l, c * inner + inner - 1 - l) for c, l in everyone]
    block = lambda x, j: x[j * send_rows : (j + 1) * send_rows]
    both = [block(keep, j) for j in range(1, outer)]
    if inner == 2:
        other = lax.ppermute(give[0], "expert", swap)
        both = [jnp.concatenate([x, block(other, j)]) for j, x in enumerate(both)]
        *both, own = lax.optimization_barrier((*both, give[1]))
    come = [keep]
    for j in range(1, outer):
        pairs = [(c * inner + l, partner(c, j, outer) * inner + l) for c, l in everyone]
        come.append(lax.ppermute(both[j - 1], "expert", pairs))
    if inner == 2:
        come.append(lax.ppermute(own, "expert", swap))

    order = np.arange(2 * k * 2 * gb * images).reshape(2, 2, gb, k, n_hidden, quarter)
    order = order.transpose(2, 4, 0, 3, 5, 1)
    spread = one_hot_rows(order, order.size)
    back_rows = 2 * k * quarter * 2
    back = pl.pallas_call(
        functools.partial(expert_kernel, images, n_expert, k, gb),
        out_shape=jax.ShapeDtypeStruct((n_all * back_rows, half), BF),
        in_specs=[vmem] * (4 + len(come)),
        out_specs=vmem,
        scratch_shapes=[pltpu.VMEM((n_expert, send_rows, width), BF)],
        compiler_params=pltpu.CompilerParams(vmem_limit_bytes=20 << 20),
        name="experts",
    )(w_in, b_in, w_out, spread, *come)

    home = lax.all_to_all(
        back.reshape(n_all, back_rows, half),
        ("expert", "hidden"),
        split_axis=0,
        concat_axis=0,
        tiled=True,
    )

    label = np.arange(quarter * 2 * 2 * gb * k).reshape(quarter, 2, 2, gb, k).transpose(3, 1, 4, 0, 2)
    label = np.broadcast_to(label[:, None], (gb, n_hidden) + label.shape[1:])
    select = np.ascontiguousarray(one_hot_rows(label, quarter * 4 * gb * k).T)
    return pl.pallas_call(
        functools.partial(final_kernel, quarter, k, gb),
        out_shape=jax.ShapeDtypeStruct((quarter, positions, width), BF),
        in_specs=[vmem] * 8,
        out_specs=vmem,
        compiler_params=pltpu.CompilerParams(vmem_limit_bytes=8 << 20),
        name="tokens_back",
    )(home.reshape(n_all * back_rows, half), b_out, my_tok, my_grad, disp, comb, keys, select)


def solution(mesh):
    return jax.shard_map(
        functools.partial(local, mesh.shape["expert"], mesh.shape["hidden"]),
        mesh=mesh,
        in_specs=(
            P("expert", None, None),
            P(),
            P("expert", None, "hidden"),
            P("expert", "hidden"),
            P("expert", "hidden", None),
            P(),
            P("expert", None, None),
        ),
        out_specs=P(("expert", "hidden"), None, None),
        check_vma=False,
    )
```

```python
import functools

import jax
import jax.numpy as jnp
import numpy as np
from jax import lax
from jax.experimental import pallas as pl
from jax.experimental.pallas import tpu as pltpu
from jax.sharding import PartitionSpec as P

BF = jnp.bfloat16
F32 = jnp.float32
NN = (((1,), (0,)), ((), ()))
NT = (((1,), (1,)), ((), ()))


def mm(a, b, dims=NN):
    return lax.dot_general(a, b, dims, preferred_element_type=F32)


def block_of(n_expert):
    return 8 if n_expert % 8 == 0 else n_expert


def one_hot_rows(source, count):
    return np.asarray(np.asarray(source).reshape(-1)[:, None] == np.arange(count)[None], BF)


def partner(me, j, n, back=False):
    if n & (n - 1) == 0:
        return me ^ j
    shifted = me + (n - j if back else j)
    return shifted % n if isinstance(me, int) else lax.rem(shifted, n)


def levels(n_expert):
    inner = 2 if n_expert % 2 == 0 else 1
    return n_expert // inner, inner


def position(inner):
    me = lax.axis_index("expert")
    return lax.div(me, inner), lax.rem(me, inner)


def dispatch_kernel(
    images, quarter, k, gb, n_expert, tok_ref, grad_ref, keys_ref, perm_ref,
    disp_ref, comb_ref, my_tok_ref, my_grad_ref, *rest,
):
    outer, inner = levels(n_expert)
    leave_refs = rest[:outer]
    send_ref, disp_all, comb_all = rest[outer:]
    slots = keys_ref.shape[0]
    keys = keys_ref[...]
    slot_rows = [[], []]
    for b in range(images):
        tok = tok_ref[b]
        logits = mm(keys, tok, NT)
        e = jnp.exp(logits - jnp.max(logits, axis=1, keepdims=True))
        disp = (e / jnp.sum(e, axis=1, keepdims=True)).astype(BF)
        e = jnp.exp(logits - jnp.max(logits, axis=0, keepdims=True))
        comb = (e / jnp.sum(e, axis=0, keepdims=True)).astype(BF)
        disp_all[b] = disp
        comb_all[b] = comb
        slot_rows[0].append(mm(disp, tok).astype(BF))
        slot_rows[1].append(mm(comb, grad_ref[b]).astype(BF))
    perm = perm_ref[...]
    step = gb * k
    rows = perm.shape[0]
    for i in range(slots // step):
        block = jnp.concatenate(
            [r[i * step : (i + 1) * step] for kind in slot_rows for r in kind], axis=0
        )
        send_ref[i * rows : (i + 1) * rows] = mm(perm, block).astype(BF)
    block = send_ref.shape[0] // n_expert
    c, l = position(inner)
    for i in range(inner):
        for j in range(outer):
            to = partner(c, j, outer) * inner + lax.rem(l + i, inner)
            leave_refs[j][i * block : (i + 1) * block] = send_ref[
                pl.ds(pl.multiple_of(to * block, block), block)
            ]
    first = lax.axis_index("hidden") * quarter
    for m in range(quarter):
        disp_ref[m] = disp_all[first + m]
        comb_ref[m] = comb_all[first + m]
        my_tok_ref[m] = tok_ref[first + m]
        my_grad_ref[m] = grad_ref[first + m]


def expert_kernel(images, n_expert, k, gb, win_ref, bin_ref, wout_ref, t_ref, *rest):
    outer, inner = levels(n_expert)
    come_refs = rest[: outer * inner]
    back_ref, got_ref = rest[outer * inner :]
    rows = k * images
    c, l = position(inner)
    block = got_ref.shape[1]
    for j in range(outer):
        source = partner(c, j, outer, True) * inner
        for i in range(inner):
            got_ref[source + lax.rem(l + i, inner)] = come_refs[i * outer + j][:block]
    width = got_ref.shape[2]
    total = n_expert * rows
    got = got_ref[...]
    rows_in = got[:, :rows].reshape(total, width)
    rows_grad = got[:, rows:].reshape(total, width)
    half = width // 2
    expert = lax.rem(lax.div(lax.broadcasted_iota(jnp.int32, (total, 1), 0), images), k)

    def own(parts):
        out = parts[0]
        for e in range(1, k):
            out = jnp.where(expert == e, parts[e], out)
        return out

    pre = own([mm(rows_in, win_ref[e]) + bin_ref[e : e + 1] for e in range(k)])
    cdf = 0.5 * (1.0 + lax.erf(pre * 0.7071067811865476))
    hidden = (pre * cdf).astype(BF)
    slope = cdf + pre * jnp.exp(-0.5 * pre * pre) * 0.3989422804014327
    out_part = own([mm(hidden, wout_ref[e]) for e in range(k)]).astype(BF)
    act_grad = own([mm(rows_grad, wout_ref[e], NT) for e in range(k)])
    pre_grad = (act_grad * slope).astype(BF)
    in_part = own([mm(pre_grad, win_ref[e], NT) for e in range(k)]).astype(BF)
    rows = gb * k * images
    t = t_ref[...]
    out_rows = t.shape[0]
    for i in range(n_expert // gb):
        stack = jnp.concatenate(
            [
                part[i * rows : (i + 1) * rows, h * half : (h + 1) * half]
                for part in (out_part, in_part)
                for h in range(2)
            ],
            axis=0,
        )
        back_ref[i * out_rows : (i + 1) * out_rows] = mm(t, stack).astype(BF)


def final_kernel(
    quarter, k, gb, home_ref, bias_ref, tok_ref, grad_ref, disp_ref, comb_ref, keys_ref, sel_ref, out_ref,
):
    slots = keys_ref.shape[0]
    step = gb * k
    blocks = slots // step
    per_block = home_ref.shape[0] // blocks
    sel = sel_ref[...]
    sums = [mm(sel, home_ref[i * per_block : (i + 1) * per_block]) for i in range(blocks)]

    def assemble(kind, m):
        halves = []
        for h in range(2):
            start = ((m * 2 + kind) * 2 + h) * step
            halves.append(jnp.concatenate([s[start : start + step] for s in sums], axis=0))
        return jnp.concatenate(halves, axis=1)

    keys = keys_ref[...]
    for m in range(quarter):
        slot_out = (assemble(0, m) + bias_ref[...]).astype(BF)
        slot_in_grad = assemble(1, m).astype(BF)
        comb_grad = mm(slot_out, grad_ref[m], NT)
        disp_grad = mm(slot_in_grad, tok_ref[m], NT)
        disp = disp_ref[m]
        comb = comb_ref[m].astype(F32)
        wide = disp.astype(F32)
        logit_grad = comb * (comb_grad - jnp.sum(comb * comb_grad, axis=0, keepdims=True))
        logit_grad = logit_grad + wide * (
            disp_grad - jnp.sum(wide * disp_grad, axis=1, keepdims=True)
        )
        logit_grad = logit_grad.astype(BF).astype(F32)
        left = jnp.concatenate([wide, logit_grad], axis=0).T.astype(BF)
        right = jnp.concatenate([slot_in_grad, keys], axis=0)
        out_ref[m] = mm(left, right).astype(BF)


def local(n_expert, n_hidden, tokens, slot_keys, w_in, b_in, w_out, b_out, out_grad):
    n_all = n_expert * n_hidden
    images, positions, width = tokens.shape
    quarter = images // n_hidden
    slots = slot_keys.shape[1]
    k, _, units = w_in.shape
    gb = block_of(n_expert)
    half = width // 2
    vmem = pl.BlockSpec(memory_space=pltpu.VMEM)
    keys = slot_keys.T

    order = np.arange(2 * images * gb * k).reshape(2, images, gb, k).transpose(2, 0, 3, 1)
    perm = one_hot_rows(order, order.size)
    send_rows = 2 * k * images
    outer, inner = levels(n_expert)
    disp, comb, my_tok, my_grad, *leave = pl.pallas_call(
        functools.partial(dispatch_kernel, images, quarter, k, gb, n_expert),
        out_shape=(
            jax.ShapeDtypeStruct((quarter, slots, positions), BF),
            jax.ShapeDtypeStruct((quarter, slots, positions), BF),
            jax.ShapeDtypeStruct((quarter, positions, width), BF),
            jax.ShapeDtypeStruct((quarter, positions, width), BF),
        )
        + (jax.ShapeDtypeStruct((inner * send_rows, width), BF),) * outer,
        in_specs=[vmem] * 4,
        out_specs=(vmem,) * (4 + outer),
        scratch_shapes=[pltpu.VMEM((n_expert * send_rows, width), BF)]
        + [pltpu.VMEM((images, slots, positions), BF)] * 2,
        compiler_params=pltpu.CompilerParams(vmem_limit_bytes=12 << 20),
        cost_estimate=pl.CostEstimate(flops=8000000000, bytes_accessed=0, transcendentals=0),
        name="dispatch",
    )(tokens, out_grad, keys, perm)

    everyone = [(c, l) for c in range(outer) for l in range(inner)]
    come = leave[:1]
    for j in range(1, outer):
        pairs = [(c * inner + l, partner(c, j, outer) * inner + l) for c, l in everyone]
        come.append(lax.ppermute(leave[j], "expert", pairs))
    if inner == 2:
        swap = [(c * inner + l, c * inner + 1 - l) for c, l in everyone]
        come += [lax.ppermute(x[send_rows:], "expert", swap) for x in come]

    order = np.arange(2 * k * 2 * gb * images).reshape(2, 2, gb, k, n_hidden, quarter)
    order = order.transpose(2, 4, 0, 3, 5, 1)
    spread = one_hot_rows(order, order.size)
    back_rows = 2 * k * quarter * 2
    back = pl.pallas_call(
        functools.partial(expert_kernel, images, n_expert, k, gb),
        out_shape=jax.ShapeDtypeStruct((n_all * back_rows, half), BF),
        in_specs=[vmem] * (4 + len(come)),
        out_specs=vmem,
        scratch_shapes=[pltpu.VMEM((n_expert, send_rows, width), BF)],
        compiler_params=pltpu.CompilerParams(vmem_limit_bytes=20 << 20),
        name="experts",
    )(w_in, b_in, w_out, spread, *come)

    home = lax.all_to_all(
        back.reshape(n_all, back_rows, half),
        ("expert", "hidden"),
        split_axis=0,
        concat_axis=0,
        tiled=True,
    )

    label = np.arange(quarter * 2 * 2 * gb * k).reshape(quarter, 2, 2, gb, k).transpose(3, 1, 4, 0, 2)
    label = np.broadcast_to(label[:, None], (gb, n_hidden) + label.shape[1:])
    select = np.ascontiguousarray(one_hot_rows(label, quarter * 4 * gb * k).T)
    return pl.pallas_call(
        functools.partial(final_kernel, quarter, k, gb),
        out_shape=jax.ShapeDtypeStruct((quarter, positions, width), BF),
        in_specs=[vmem] * 8,
        out_specs=vmem,
        compiler_params=pltpu.CompilerParams(vmem_limit_bytes=8 << 20),
        name="tokens_back",
    )(home.reshape(n_all * back_rows, half), b_out, my_tok, my_grad, disp, comb, keys, select)


def solution(mesh):
    return jax.shard_map(
        functools.partial(local, mesh.shape["expert"], mesh.shape["hidden"]),
        mesh=mesh,
        in_specs=(
            P("expert", None, None),
            P(),
            P("expert", None, "hidden"),
            P("expert", "hidden"),
            P("expert", "hidden", None),
            P(),
            P("expert", None, None),
        ),
        out_specs=P(("expert", "hidden"), None, None),
        check_vma=False,
    )
```

```python
import functools

import jax
import jax.numpy as jnp
import numpy as np
from jax import lax
from jax.experimental import pallas as pl
from jax.experimental.pallas import tpu as pltpu
from jax.sharding import PartitionSpec as P

BF = jnp.bfloat16
F32 = jnp.float32
NN = (((1,), (0,)), ((), ()))
NT = (((1,), (1,)), ((), ()))


def mm(a, b, dims=NN):
    return lax.dot_general(a, b, dims, preferred_element_type=F32)


def block_of(n_expert):
    return 8 if n_expert % 8 == 0 else n_expert


def one_hot_rows(source, count):
    return np.asarray(np.asarray(source).reshape(-1)[:, None] == np.arange(count)[None], BF)


def partner(me, j, n, back=False):
    if n & (n - 1) == 0:
        return me ^ j
    shifted = me + (n - j if back else j)
    return shifted % n if isinstance(me, int) else lax.rem(shifted, n)


def levels(n_expert):
    inner = 2 if n_expert % 2 == 0 else 1
    return n_expert // inner, inner


def turn(l, j, outer):
    if j == 0:
        return 0
    steps = [outer - 1, *range(1, outer - 1)]
    mine, other = steps[j - 1], steps[j - 2]
    if isinstance(l, int):
        return other if l else mine
    return jnp.where(l == 1, other, mine)


def position(inner):
    me = lax.axis_index("expert")
    return lax.div(me, inner), lax.rem(me, inner)


def dispatch_kernel(
    images, quarter, k, gb, n_expert, tok_ref, grad_ref, keys_ref, perm_ref,
    disp_ref, comb_ref, my_tok_ref, my_grad_ref, *rest,
):
    outer, inner = levels(n_expert)
    leave_refs = rest[:outer]
    send_ref, disp_all, comb_all = rest[outer:]
    slots = keys_ref.shape[0]
    keys = keys_ref[...]
    slot_rows = [[], []]
    for b in range(images):
        tok = tok_ref[b]
        logits = mm(keys, tok, NT)
        e = jnp.exp(logits - jnp.max(logits, axis=1, keepdims=True))
        disp = (e / jnp.sum(e, axis=1, keepdims=True)).astype(BF)
        e = jnp.exp(logits - jnp.max(logits, axis=0, keepdims=True))
        comb = (e / jnp.sum(e, axis=0, keepdims=True)).astype(BF)
        disp_all[b] = disp
        comb_all[b] = comb
        slot_rows[0].append(mm(disp, tok).astype(BF))
        slot_rows[1].append(mm(comb, grad_ref[b]).astype(BF))
    perm = perm_ref[...]
    step = gb * k
    rows = perm.shape[0]
    for i in range(slots // step):
        block = jnp.concatenate(
            [r[i * step : (i + 1) * step] for kind in slot_rows for r in kind], axis=0
        )
        send_ref[i * rows : (i + 1) * rows] = mm(perm, block).astype(BF)
    block = send_ref.shape[0] // n_expert
    c, l = position(inner)
    for i in range(inner):
        for j in range(outer):
            to = partner(c, turn(l, j, outer), outer) * inner + lax.rem(l + i, inner)
            leave_refs[j][i * block : (i + 1) * block] = send_ref[
                pl.ds(pl.multiple_of(to * block, block), block)
            ]
    first = lax.axis_index("hidden") * quarter
    for m in range(quarter):
        disp_ref[m] = disp_all[first + m]
        comb_ref[m] = comb_all[first + m]
        my_tok_ref[m] = tok_ref[first + m]
        my_grad_ref[m] = grad_ref[first + m]


def expert_kernel(images, n_expert, k, gb, win_ref, bin_ref, wout_ref, t_ref, *rest):
    outer, inner = levels(n_expert)
    come_refs = rest[: outer * inner]
    back_ref, got_ref = rest[outer * inner :]
    rows = k * images
    c, l = position(inner)
    block = got_ref.shape[1]
    for j in range(outer):
        for i in range(inner):
            core = lax.rem(l + i, inner)
            source = partner(c, turn(core, j, outer), outer, True) * inner + core
            got_ref[source] = come_refs[i * outer + j][:block]
    width = got_ref.shape[2]
    total = n_expert * rows
    got = got_ref[...]
    rows_in = got[:, :rows].reshape(total, width)
    rows_grad = got[:, rows:].reshape(total, width)
    half = width // 2
    expert = lax.rem(lax.div(lax.broadcasted_iota(jnp.int32, (total, 1), 0), images), k)

    def own(parts):
        out = parts[0]
        for e in range(1, k):
            out = jnp.where(expert == e, parts[e], out)
        return out

    pre = own([mm(rows_in, win_ref[e]) + bin_ref[e : e + 1] for e in range(k)])
    cdf = 0.5 * (1.0 + lax.erf(pre * 0.7071067811865476))
    hidden = (pre * cdf).astype(BF)
    slope = cdf + pre * jnp.exp(-0.5 * pre * pre) * 0.3989422804014327
    out_part = own([mm(hidden, wout_ref[e]) for e in range(k)]).astype(BF)
    act_grad = own([mm(rows_grad, wout_ref[e], NT) for e in range(k)])
    pre_grad = (act_grad * slope).astype(BF)
    in_part = own([mm(pre_grad, win_ref[e], NT) for e in range(k)]).astype(BF)
    rows = gb * k * images
    t = t_ref[...]
    out_rows = t.shape[0]
    for i in range(n_expert // gb):
        stack = jnp.concatenate(
            [
                part[i * rows : (i + 1) * rows, h * half : (h + 1) * half]
                for part in (out_part, in_part)
                for h in range(2)
            ],
            axis=0,
        )
        back_ref[i * out_rows : (i + 1) * out_rows] = mm(t, stack).astype(BF)


def final_kernel(
    quarter, k, gb, home_ref, bias_ref, tok_ref, grad_ref, disp_ref, comb_ref, keys_ref, sel_ref, out_ref,
):
    slots = keys_ref.shape[0]
    step = gb * k
    blocks = slots // step
    per_block = home_ref.shape[0] // blocks
    sel = sel_ref[...]
    sums = [mm(sel, home_ref[i * per_block : (i + 1) * per_block]) for i in range(blocks)]

    def assemble(kind, m):
        halves = []
        for h in range(2):
            start = ((m * 2 + kind) * 2 + h) * step
            halves.append(jnp.concatenate([s[start : start + step] for s in sums], axis=0))
        return jnp.concatenate(halves, axis=1)

    keys = keys_ref[...]
    for m in range(quarter):
        slot_out = (assemble(0, m) + bias_ref[...]).astype(BF)
        slot_in_grad = assemble(1, m).astype(BF)
        comb_grad = mm(slot_out, grad_ref[m], NT)
        disp_grad = mm(slot_in_grad, tok_ref[m], NT)
        disp = disp_ref[m]
        comb = comb_ref[m].astype(F32)
        wide = disp.astype(F32)
        logit_grad = comb * (comb_grad - jnp.sum(comb * comb_grad, axis=0, keepdims=True))
        logit_grad = logit_grad + wide * (
            disp_grad - jnp.sum(wide * disp_grad, axis=1, keepdims=True)
        )
        logit_grad = logit_grad.astype(BF).astype(F32)
        left = jnp.concatenate([wide, logit_grad], axis=0).T.astype(BF)
        right = jnp.concatenate([slot_in_grad, keys], axis=0)
        out_ref[m] = mm(left, right).astype(BF)


def local(n_expert, n_hidden, tokens, slot_keys, w_in, b_in, w_out, b_out, out_grad):
    n_all = n_expert * n_hidden
    images, positions, width = tokens.shape
    quarter = images // n_hidden
    slots = slot_keys.shape[1]
    k, _, units = w_in.shape
    gb = block_of(n_expert)
    half = width // 2
    vmem = pl.BlockSpec(memory_space=pltpu.VMEM)
    keys = slot_keys.T

    order = np.arange(2 * images * gb * k).reshape(2, images, gb, k).transpose(2, 0, 3, 1)
    perm = one_hot_rows(order, order.size)
    send_rows = 2 * k * images
    outer, inner = levels(n_expert)
    disp, comb, my_tok, my_grad, *leave = pl.pallas_call(
        functools.partial(dispatch_kernel, images, quarter, k, gb, n_expert),
        out_shape=(
            jax.ShapeDtypeStruct((quarter, slots, positions), BF),
            jax.ShapeDtypeStruct((quarter, slots, positions), BF),
            jax.ShapeDtypeStruct((quarter, positions, width), BF),
            jax.ShapeDtypeStruct((quarter, positions, width), BF),
        )
        + (jax.ShapeDtypeStruct((inner * send_rows, width), BF),) * outer,
        in_specs=[vmem] * 4,
        out_specs=(vmem,) * (4 + outer),
        scratch_shapes=[pltpu.VMEM((n_expert * send_rows, width), BF)]
        + [pltpu.VMEM((images, slots, positions), BF)] * 2,
        compiler_params=pltpu.CompilerParams(vmem_limit_bytes=12 << 20),
        name="dispatch",
    )(tokens, out_grad, keys, perm)

    everyone = [(c, l) for c in range(outer) for l in range(inner)]
    come = leave[:1]
    for j in range(1, outer):
        pairs = [
            (c * inner + l, partner(c, turn(l, j, outer), outer) * inner + l) for c, l in everyone
        ]
        come.append(lax.ppermute(leave[j], "expert", pairs))
    if inner == 2:
        swap = [(c * inner + l, c * inner + 1 - l) for c, l in everyone]
        come += [lax.ppermute(x[send_rows:], "expert", swap) for x in come]

    order = np.arange(2 * k * 2 * gb * images).reshape(2, 2, gb, k, n_hidden, quarter)
    order = order.transpose(2, 4, 0, 3, 5, 1)
    spread = one_hot_rows(order, order.size)
    back_rows = 2 * k * quarter * 2
    back = pl.pallas_call(
        functools.partial(expert_kernel, images, n_expert, k, gb),
        out_shape=jax.ShapeDtypeStruct((n_all * back_rows, half), BF),
        in_specs=[vmem] * (4 + len(come)),
        out_specs=vmem,
        scratch_shapes=[pltpu.VMEM((n_expert, send_rows, width), BF)],
        compiler_params=pltpu.CompilerParams(vmem_limit_bytes=20 << 20),
        name="experts",
    )(w_in, b_in, w_out, spread, *come)

    home = lax.all_to_all(
        back.reshape(n_all, back_rows, half),
        ("expert", "hidden"),
        split_axis=0,
        concat_axis=0,
        tiled=True,
    )

    label = np.arange(quarter * 2 * 2 * gb * k).reshape(quarter, 2, 2, gb, k).transpose(3, 1, 4, 0, 2)
    label = np.broadcast_to(label[:, None], (gb, n_hidden) + label.shape[1:])
    select = np.ascontiguousarray(one_hot_rows(label, quarter * 4 * gb * k).T)
    return pl.pallas_call(
        functools.partial(final_kernel, quarter, k, gb),
        out_shape=jax.ShapeDtypeStruct((quarter, positions, width), BF),
        in_specs=[vmem] * 8,
        out_specs=vmem,
        compiler_params=pltpu.CompilerParams(vmem_limit_bytes=8 << 20),
        name="tokens_back",
    )(home.reshape(n_all * back_rows, half), b_out, my_tok, my_grad, disp, comb, keys, select)


def solution(mesh):
    return jax.shard_map(
        functools.partial(local, mesh.shape["expert"], mesh.shape["hidden"]),
        mesh=mesh,
        in_specs=(
            P("expert", None, None),
            P(),
            P("expert", None, "hidden"),
            P("expert", "hidden"),
            P("expert", "hidden", None),
            P(),
            P("expert", None, None),
        ),
        out_specs=P(("expert", "hidden"), None, None),
        check_vma=False,
    )
```

```python
import functools

import jax
import jax.numpy as jnp
import numpy as np
from jax import lax
from jax.experimental import pallas as pl
from jax.experimental.pallas import tpu as pltpu
from jax.sharding import PartitionSpec as P

BF = jnp.bfloat16
F32 = jnp.float32
NN = (((1,), (0,)), ((), ()))
NT = (((1,), (1,)), ((), ()))


def mm(a, b, dims=NN):
    return lax.dot_general(a, b, dims, preferred_element_type=F32)


def block_of(n_expert):
    return 8 if n_expert % 8 == 0 else n_expert


def one_hot_rows(source, count):
    return np.asarray(np.asarray(source).reshape(-1)[:, None] == np.arange(count)[None], BF)


def partner(me, j, n, back=False):
    if n & (n - 1) == 0:
        return me ^ j
    shifted = me + (n - j if back else j)
    return shifted % n if isinstance(me, int) else lax.rem(shifted, n)


def levels(n_expert):
    inner = 2 if n_expert % 2 == 0 else 1
    return n_expert // inner, inner


def position(inner):
    me = lax.axis_index("expert")
    return lax.div(me, inner), lax.rem(me, inner)


def dispatch_kernel(
    images, quarter, k, gb, n_expert, tok_ref, grad_ref, keys_ref, perm_ref,
    disp_ref, comb_ref, my_tok_ref, my_grad_ref, *rest,
):
    outer, inner = levels(n_expert)
    leave_refs = rest[:outer]
    send_ref, disp_all, comb_all = rest[outer:]
    slots = keys_ref.shape[0]
    keys = keys_ref[...]
    slot_rows = [[], []]
    for b in range(images):
        tok = tok_ref[b]
        logits = mm(keys, tok, NT)
        e = jnp.exp(logits - jnp.max(logits, axis=1, keepdims=True))
        disp = (e / jnp.sum(e, axis=1, keepdims=True)).astype(BF)
        e = jnp.exp(logits - jnp.max(logits, axis=0, keepdims=True))
        comb = (e / jnp.sum(e, axis=0, keepdims=True)).astype(BF)
        disp_all[b] = disp
        comb_all[b] = comb
        slot_rows[0].append(mm(disp, tok).astype(BF))
        slot_rows[1].append(mm(comb, grad_ref[b]).astype(BF))
    perm = perm_ref[...]
    step = gb * k
    rows = perm.shape[0]
    for i in range(slots // step):
        block = jnp.concatenate(
            [r[i * step : (i + 1) * step] for kind in slot_rows for r in kind], axis=0
        )
        send_ref[i * rows : (i + 1) * rows] = mm(perm, block).astype(BF)
    block = send_ref.shape[0] // n_expert
    c, l = position(inner)
    for i in range(inner):
        for j in range(outer):
            to = partner(c, j, outer) * inner + lax.rem(l + i, inner)
            leave_refs[j][i * block : (i + 1) * block] = send_ref[
                pl.ds(pl.multiple_of(to * block, block), block)
            ]
    first = lax.axis_index("hidden") * quarter
    for m in range(quarter):
        disp_ref[m] = disp_all[first + m]
        comb_ref[m] = comb_all[first + m]
        my_tok_ref[m] = tok_ref[first + m]
        my_grad_ref[m] = grad_ref[first + m]


def expert_kernel(images, n_expert, k, gb, win_ref, bin_ref, wout_ref, t_ref, *rest):
    outer, inner = levels(n_expert)
    come_refs = rest[: outer * inner]
    back_ref, got_ref = rest[outer * inner :]
    rows = k * images
    c, l = position(inner)
    block = got_ref.shape[1]
    for j in range(outer):
        source = partner(c, j, outer, True) * inner
        for i in range(inner):
            got_ref[source + lax.rem(l + i, inner)] = come_refs[i * outer + j][:block]
    width = got_ref.shape[2]
    total = n_expert * rows
    got = got_ref[...]
    rows_in = got[:, :rows].reshape(total, width)
    rows_grad = got[:, rows:].reshape(total, width)
    half = width // 2
    expert = lax.rem(lax.div(lax.broadcasted_iota(jnp.int32, (total, 1), 0), images), k)

    def own(parts):
        out = parts[0]
        for e in range(1, k):
            out = jnp.where(expert == e, parts[e], out)
        return out

    pre = own([mm(rows_in, win_ref[e]) + bin_ref[e : e + 1] for e in range(k)])
    cdf = 0.5 * (1.0 + lax.erf(pre * 0.7071067811865476))
    hidden = (pre * cdf).astype(BF)
    slope = cdf + pre * jnp.exp(-0.5 * pre * pre) * 0.3989422804014327
    out_part = own([mm(hidden, wout_ref[e]) for e in range(k)]).astype(BF)
    act_grad = own([mm(rows_grad, wout_ref[e], NT) for e in range(k)])
    pre_grad = (act_grad * slope).astype(BF)
    in_part = own([mm(pre_grad, win_ref[e], NT) for e in range(k)]).astype(BF)
    rows = gb * k * images
    t = t_ref[...]
    out_rows = t.shape[0]
    for i in range(n_expert // gb):
        stack = jnp.concatenate(
            [
                part[i * rows : (i + 1) * rows, h * half : (h + 1) * half]
                for part in (out_part, in_part)
                for h in range(2)
            ],
            axis=0,
        )
        back_ref[i * out_rows : (i + 1) * out_rows] = mm(t, stack).astype(BF)


def final_kernel(
    quarter, k, gb, home_ref, bias_ref, tok_ref, grad_ref, disp_ref, comb_ref, keys_ref, sel_ref, out_ref,
):
    slots = keys_ref.shape[0]
    step = gb * k
    blocks = slots // step
    per_block = home_ref.shape[0] // blocks
    sel = sel_ref[...]
    sums = [mm(sel, home_ref[i * per_block : (i + 1) * per_block]) for i in range(blocks)]

    def assemble(kind, m):
        halves = []
        for h in range(2):
            start = ((m * 2 + kind) * 2 + h) * step
            halves.append(jnp.concatenate([s[start : start + step] for s in sums], axis=0))
        return jnp.concatenate(halves, axis=1)

    keys = keys_ref[...]
    for m in range(quarter):
        slot_out = (assemble(0, m) + bias_ref[...]).astype(BF)
        slot_in_grad = assemble(1, m).astype(BF)
        wide = disp_ref[m].astype(F32).T
        comb = comb_ref[m].astype(F32).T
        from_slots = mm(wide.astype(BF), slot_in_grad)
        comb_grad = mm(grad_ref[m], slot_out, NT)
        disp_grad = mm(tok_ref[m], slot_in_grad, NT)
        logit_grad = comb * (comb_grad - jnp.sum(comb * comb_grad, axis=1, keepdims=True))
        logit_grad = logit_grad + wide * (
            disp_grad - jnp.sum(wide * disp_grad, axis=0, keepdims=True)
        )
        out_ref[m] = (from_slots + mm(logit_grad.astype(BF), keys)).astype(BF)


def local(n_expert, n_hidden, tokens, slot_keys, w_in, b_in, w_out, b_out, out_grad):
    n_all = n_expert * n_hidden
    images, positions, width = tokens.shape
    quarter = images // n_hidden
    slots = slot_keys.shape[1]
    k, _, units = w_in.shape
    gb = block_of(n_expert)
    half = width // 2
    vmem = pl.BlockSpec(memory_space=pltpu.VMEM)
    keys = slot_keys.T

    order = np.arange(2 * images * gb * k).reshape(2, images, gb, k).transpose(2, 0, 3, 1)
    perm = one_hot_rows(order, order.size)
    send_rows = 2 * k * images
    outer, inner = levels(n_expert)
    disp, comb, my_tok, my_grad, *leave = pl.pallas_call(
        functools.partial(dispatch_kernel, images, quarter, k, gb, n_expert),
        out_shape=(
            jax.ShapeDtypeStruct((quarter, slots, positions), BF),
            jax.ShapeDtypeStruct((quarter, slots, positions), BF),
            jax.ShapeDtypeStruct((quarter, positions, width), BF),
            jax.ShapeDtypeStruct((quarter, positions, width), BF),
        )
        + (jax.ShapeDtypeStruct((inner * send_rows, width), BF),) * outer,
        in_specs=[vmem] * 4,
        out_specs=(vmem,) * (4 + outer),
        scratch_shapes=[pltpu.VMEM((n_expert * send_rows, width), BF)]
        + [pltpu.VMEM((images, slots, positions), BF)] * 2,
        compiler_params=pltpu.CompilerParams(vmem_limit_bytes=12 << 20),
        cost_estimate=pl.CostEstimate(flops=8000000000, bytes_accessed=0, transcendentals=0),
        name="dispatch",
    )(tokens, out_grad, keys, perm)

    everyone = [(c, l) for c in range(outer) for l in range(inner)]
    come = leave[:1]
    for j in range(1, outer):
        pairs = [(c * inner + l, partner(c, j, outer) * inner + l) for c, l in everyone]
        come.append(lax.ppermute(leave[j], "expert", pairs))
    if inner == 2:
        swap = [(c * inner + l, c * inner + 1 - l) for c, l in everyone]
        come += [lax.ppermute(x[send_rows:], "expert", swap) for x in come]

    order = np.arange(2 * k * 2 * gb * images).reshape(2, 2, gb, k, n_hidden, quarter)
    order = order.transpose(2, 4, 0, 3, 5, 1)
    spread = one_hot_rows(order, order.size)
    back_rows = 2 * k * quarter * 2
    back = pl.pallas_call(
        functools.partial(expert_kernel, images, n_expert, k, gb),
        out_shape=jax.ShapeDtypeStruct((n_all * back_rows, half), BF),
        in_specs=[vmem] * (4 + len(come)),
        out_specs=vmem,
        scratch_shapes=[pltpu.VMEM((n_expert, send_rows, width), BF)],
        compiler_params=pltpu.CompilerParams(vmem_limit_bytes=20 << 20),
        name="experts",
    )(w_in, b_in, w_out, spread, *come)

    home = lax.all_to_all(
        back.reshape(n_all, back_rows, half),
        ("expert", "hidden"),
        split_axis=0,
        concat_axis=0,
        tiled=True,
    )

    label = np.arange(quarter * 2 * 2 * gb * k).reshape(quarter, 2, 2, gb, k).transpose(3, 1, 4, 0, 2)
    label = np.broadcast_to(label[:, None], (gb, n_hidden) + label.shape[1:])
    select = np.ascontiguousarray(one_hot_rows(label, quarter * 4 * gb * k).T)
    return pl.pallas_call(
        functools.partial(final_kernel, quarter, k, gb),
        out_shape=jax.ShapeDtypeStruct((quarter, positions, width), BF),
        in_specs=[vmem] * 8,
        out_specs=vmem,
        compiler_params=pltpu.CompilerParams(vmem_limit_bytes=8 << 20),
        name="tokens_back",
    )(home.reshape(n_all * back_rows, half), b_out, my_tok, my_grad, disp, comb, keys, select)


def solution(mesh):
    return jax.shard_map(
        functools.partial(local, mesh.shape["expert"], mesh.shape["hidden"]),
        mesh=mesh,
        in_specs=(
            P("expert", None, None),
            P(),
            P("expert", None, "hidden"),
            P("expert", "hidden"),
            P("expert", "hidden", None),
            P(),
            P("expert", None, None),
        ),
        out_specs=P(("expert", "hidden"), None, None),
        check_vma=False,
    )
```

```python
import functools

import jax
import jax.numpy as jnp
import numpy as np
from jax import lax
from jax.experimental import pallas as pl
from jax.experimental.pallas import tpu as pltpu
from jax.sharding import PartitionSpec as P

BF = jnp.bfloat16
F32 = jnp.float32
NN = (((1,), (0,)), ((), ()))
NT = (((1,), (1,)), ((), ()))


def mm(a, b, dims=NN):
    return lax.dot_general(a, b, dims, preferred_element_type=F32)


def block_of(n_expert):
    return 8 if n_expert % 8 == 0 else n_expert


def one_hot_rows(source, count):
    return np.asarray(np.asarray(source).reshape(-1)[:, None] == np.arange(count)[None], BF)


def partner(me, j, n, back=False):
    if n & (n - 1) == 0:
        return me ^ j
    shifted = me + (n - j if back else j)
    return shifted % n if isinstance(me, int) else lax.rem(shifted, n)


def levels(n_expert):
    inner = 2 if n_expert % 2 == 0 else 1
    return n_expert // inner, inner


def position(inner):
    me = lax.axis_index("expert")
    return lax.div(me, inner), lax.rem(me, inner)


def dispatch_kernel(
    images, quarter, k, gb, n_expert, tok_ref, grad_ref, keys_ref, perm_ref,
    disp_ref, comb_ref, my_tok_ref, my_grad_ref, *rest,
):
    outer, inner = levels(n_expert)
    leave_ref, send_ref, disp_all, comb_all = rest
    slots = keys_ref.shape[0]
    keys = keys_ref[...]
    slot_rows = [[], []]
    for b in range(images):
        tok = tok_ref[b]
        logits = mm(keys, tok, NT)
        e = jnp.exp(logits - jnp.max(logits, axis=1, keepdims=True))
        disp = (e / jnp.sum(e, axis=1, keepdims=True)).astype(BF)
        e = jnp.exp(logits - jnp.max(logits, axis=0, keepdims=True))
        comb = (e / jnp.sum(e, axis=0, keepdims=True)).astype(BF)
        disp_all[b] = disp
        comb_all[b] = comb
        slot_rows[0].append(mm(disp, tok).astype(BF))
        slot_rows[1].append(mm(comb, grad_ref[b]).astype(BF))
    perm = perm_ref[...]
    step = gb * k
    rows = perm.shape[0]
    for i in range(slots // step):
        block = jnp.concatenate(
            [r[i * step : (i + 1) * step] for kind in slot_rows for r in kind], axis=0
        )
        send_ref[i * rows : (i + 1) * rows] = mm(perm, block).astype(BF)
    block = send_ref.shape[0] // n_expert
    c, l = position(inner)
    for i in range(inner):
        for j in range(outer):
            to = j * inner + lax.rem(l + i, inner)
            leave_ref[j, i * block : (i + 1) * block] = send_ref[
                pl.ds(pl.multiple_of(to * block, block), block)
            ]
    first = lax.axis_index("hidden") * quarter
    for m in range(quarter):
        disp_ref[m] = disp_all[first + m]
        comb_ref[m] = comb_all[first + m]
        my_tok_ref[m] = tok_ref[first + m]
        my_grad_ref[m] = grad_ref[first + m]


def expert_kernel(images, n_expert, k, gb, win_ref, bin_ref, wout_ref, t_ref, *rest):
    outer, inner = levels(n_expert)
    come_refs = rest[:inner]
    back_ref, got_ref = rest[inner:]
    rows = k * images
    c, l = position(inner)
    block = got_ref.shape[1]
    for j in range(outer):
        source = j * inner
        for i in range(inner):
            got_ref[source + lax.rem(l + i, inner)] = come_refs[i][j, :block]
    width = got_ref.shape[2]
    total = n_expert * rows
    got = got_ref[...]
    rows_in = got[:, :rows].reshape(total, width)
    rows_grad = got[:, rows:].reshape(total, width)
    half = width // 2
    expert = lax.rem(lax.div(lax.broadcasted_iota(jnp.int32, (total, 1), 0), images), k)

    def own(parts):
        out = parts[0]
        for e in range(1, k):
            out = jnp.where(expert == e, parts[e], out)
        return out

    pre = own([mm(rows_in, win_ref[e]) + bin_ref[e : e + 1] for e in range(k)])
    cdf = 0.5 * (1.0 + lax.erf(pre * 0.7071067811865476))
    hidden = (pre * cdf).astype(BF)
    slope = cdf + pre * jnp.exp(-0.5 * pre * pre) * 0.3989422804014327
    out_part = own([mm(hidden, wout_ref[e]) for e in range(k)]).astype(BF)
    act_grad = own([mm(rows_grad, wout_ref[e], NT) for e in range(k)])
    pre_grad = (act_grad * slope).astype(BF)
    in_part = own([mm(pre_grad, win_ref[e], NT) for e in range(k)]).astype(BF)
    rows = gb * k * images
    t = t_ref[...]
    out_rows = t.shape[0]
    for i in range(n_expert // gb):
        stack = jnp.concatenate(
            [
                part[i * rows : (i + 1) * rows, h * half : (h + 1) * half]
                for part in (out_part, in_part)
                for h in range(2)
            ],
            axis=0,
        )
        back_ref[i * out_rows : (i + 1) * out_rows] = mm(t, stack).astype(BF)


def final_kernel(
    quarter, k, gb, home_ref, bias_ref, tok_ref, grad_ref, disp_ref, comb_ref, keys_ref, sel_ref, out_ref,
):
    slots = keys_ref.shape[0]
    step = gb * k
    blocks = slots // step
    per_block = home_ref.shape[0] // blocks
    sel = sel_ref[...]
    sums = [mm(sel, home_ref[i * per_block : (i + 1) * per_block]) for i in range(blocks)]

    def assemble(kind, m):
        halves = []
        for h in range(2):
            start = ((m * 2 + kind) * 2 + h) * step
            halves.append(jnp.concatenate([s[start : start + step] for s in sums], axis=0))
        return jnp.concatenate(halves, axis=1)

    keys = keys_ref[...]
    for m in range(quarter):
        slot_out = (assemble(0, m) + bias_ref[...]).astype(BF)
        slot_in_grad = assemble(1, m).astype(BF)
        comb_grad = mm(slot_out, grad_ref[m], NT)
        disp_grad = mm(slot_in_grad, tok_ref[m], NT)
        disp = disp_ref[m]
        comb = comb_ref[m].astype(F32)
        wide = disp.astype(F32)
        logit_grad = comb * (comb_grad - jnp.sum(comb * comb_grad, axis=0, keepdims=True))
        logit_grad = logit_grad + wide * (
            disp_grad - jnp.sum(wide * disp_grad, axis=1, keepdims=True)
        )
        logit_grad = logit_grad.astype(BF).astype(F32)
        left = jnp.concatenate([wide, logit_grad], axis=0).T.astype(BF)
        right = jnp.concatenate([slot_in_grad, keys], axis=0)
        out_ref[m] = mm(left, right).astype(BF)


def local(n_expert, n_hidden, tokens, slot_keys, w_in, b_in, w_out, b_out, out_grad):
    n_all = n_expert * n_hidden
    images, positions, width = tokens.shape
    quarter = images // n_hidden
    slots = slot_keys.shape[1]
    k, _, units = w_in.shape
    gb = block_of(n_expert)
    half = width // 2
    vmem = pl.BlockSpec(memory_space=pltpu.VMEM)
    keys = slot_keys.T

    order = np.arange(2 * images * gb * k).reshape(2, images, gb, k).transpose(2, 0, 3, 1)
    perm = one_hot_rows(order, order.size)
    send_rows = 2 * k * images
    outer, inner = levels(n_expert)
    disp, comb, my_tok, my_grad, leave = pl.pallas_call(
        functools.partial(dispatch_kernel, images, quarter, k, gb, n_expert),
        out_shape=(
            jax.ShapeDtypeStruct((quarter, slots, positions), BF),
            jax.ShapeDtypeStruct((quarter, slots, positions), BF),
            jax.ShapeDtypeStruct((quarter, positions, width), BF),
            jax.ShapeDtypeStruct((quarter, positions, width), BF),
        )
        + (jax.ShapeDtypeStruct((outer, inner * send_rows, width), BF),),
        in_specs=[vmem] * 4,
        out_specs=(vmem,) * 5,
        scratch_shapes=[pltpu.VMEM((n_expert * send_rows, width), BF)]
        + [pltpu.VMEM((images, slots, positions), BF)] * 2,
        compiler_params=pltpu.CompilerParams(vmem_limit_bytes=12 << 20),
        cost_estimate=pl.CostEstimate(flops=8000000000, bytes_accessed=0, transcendentals=0),
        name="dispatch",
    )(tokens, out_grad, keys, perm)

    everyone = [(c, l) for c in range(outer) for l in range(inner)]
    groups = [[c * inner + l for c in range(outer)] for l in range(inner)]
    come = [
        lax.all_to_all(
            leave, "expert", split_axis=0, concat_axis=0, axis_index_groups=groups, tiled=True
        )
    ]
    if inner == 2:
        swap = [(c * inner + l, c * inner + 1 - l) for c, l in everyone]
        come.append(lax.ppermute(come[0][:, send_rows:], "expert", swap))

    order = np.arange(2 * k * 2 * gb * images).reshape(2, 2, gb, k, n_hidden, quarter)
    order = order.transpose(2, 4, 0, 3, 5, 1)
    spread = one_hot_rows(order, order.size)
    back_rows = 2 * k * quarter * 2
    back = pl.pallas_call(
        functools.partial(expert_kernel, images, n_expert, k, gb),
        out_shape=jax.ShapeDtypeStruct((n_all * back_rows, half), BF),
        in_specs=[vmem] * (4 + len(come)),
        out_specs=vmem,
        scratch_shapes=[pltpu.VMEM((n_expert, send_rows, width), BF)],
        compiler_params=pltpu.CompilerParams(vmem_limit_bytes=20 << 20),
        name="experts",
    )(w_in, b_in, w_out, spread, *come)

    home = lax.all_to_all(
        back.reshape(n_all, back_rows, half),
        ("expert", "hidden"),
        split_axis=0,
        concat_axis=0,
        tiled=True,
    )

    label = np.arange(quarter * 2 * 2 * gb * k).reshape(quarter, 2, 2, gb, k).transpose(3, 1, 4, 0, 2)
    label = np.broadcast_to(label[:, None], (gb, n_hidden) + label.shape[1:])
    select = np.ascontiguousarray(one_hot_rows(label, quarter * 4 * gb * k).T)
    return pl.pallas_call(
        functools.partial(final_kernel, quarter, k, gb),
        out_shape=jax.ShapeDtypeStruct((quarter, positions, width), BF),
        in_specs=[vmem] * 8,
        out_specs=vmem,
        compiler_params=pltpu.CompilerParams(vmem_limit_bytes=8 << 20),
        name="tokens_back",
    )(home.reshape(n_all * back_rows, half), b_out, my_tok, my_grad, disp, comb, keys, select)


def solution(mesh):
    return jax.shard_map(
        functools.partial(local, mesh.shape["expert"], mesh.shape["hidden"]),
        mesh=mesh,
        in_specs=(
            P("expert", None, None),
            P(),
            P("expert", None, "hidden"),
            P("expert", "hidden"),
            P("expert", "hidden", None),
            P(),
            P("expert", None, None),
        ),
        out_specs=P(("expert", "hidden"), None, None),
        check_vma=False,
    )
```

```python
import functools

import jax
import jax.numpy as jnp
import numpy as np
from jax import lax
from jax.experimental import pallas as pl
from jax.experimental.pallas import tpu as pltpu
from jax.sharding import PartitionSpec as P

BF = jnp.bfloat16
F32 = jnp.float32
NN = (((1,), (0,)), ((), ()))
NT = (((1,), (1,)), ((), ()))


def mm(a, b, dims=NN):
    return lax.dot_general(a, b, dims, preferred_element_type=F32)


def block_of(n_expert):
    return 8 if n_expert % 8 == 0 else n_expert


def one_hot_rows(source, count):
    return np.asarray(np.asarray(source).reshape(-1)[:, None] == np.arange(count)[None], BF)


def partner(me, j, n, back=False):
    if n & (n - 1) == 0:
        return me ^ j
    shifted = me + (n - j if back else j)
    return shifted % n if isinstance(me, int) else lax.rem(shifted, n)


def levels(n_expert):
    inner = 2 if n_expert % 2 == 0 else 1
    return n_expert // inner, inner


def position(inner):
    me = lax.axis_index("expert")
    return lax.div(me, inner), lax.rem(me, inner)


def dispatch_kernel(
    images, quarter, k, gb, n_expert, tok_ref, grad_ref, keys_ref, perm_ref,
    disp_ref, comb_ref, my_tok_ref, my_grad_ref, *rest,
):
    outer, inner = levels(n_expert)
    leave_refs = rest[:outer]
    send_ref, disp_all, comb_all = rest[outer:]
    slots = keys_ref.shape[0]
    keys = keys_ref[...]
    slot_rows = [[], []]
    for b in range(images):
        tok = tok_ref[b]
        logits = mm(keys, tok, NT)
        e = jnp.exp(logits - jnp.max(logits, axis=1, keepdims=True))
        disp = (e / jnp.sum(e, axis=1, keepdims=True)).astype(BF)
        e = jnp.exp(logits - jnp.max(logits, axis=0, keepdims=True))
        comb = (e / jnp.sum(e, axis=0, keepdims=True)).astype(BF)
        disp_all[b] = disp
        comb_all[b] = comb
        slot_rows[0].append(mm(disp, tok).astype(BF))
        slot_rows[1].append(mm(comb, grad_ref[b]).astype(BF))
    perm = perm_ref[...]
    step = gb * k
    rows = perm.shape[0]
    for i in range(slots // step):
        block = jnp.concatenate(
            [r[i * step : (i + 1) * step] for kind in slot_rows for r in kind], axis=0
        )
        send_ref[i * rows : (i + 1) * rows] = mm(perm, block).astype(BF)
    block = send_ref.shape[0] // n_expert
    c, l = position(inner)
    for i in range(inner):
        for j in range(outer):
            to = partner(c, j, outer) * inner + lax.rem(l + i, inner)
            leave_refs[j][i * block : (i + 1) * block] = send_ref[
                pl.ds(pl.multiple_of(to * block, block), block)
            ]
    first = lax.axis_index("hidden") * quarter
    for m in range(quarter):
        disp_ref[m] = disp_all[first + m]
        comb_ref[m] = comb_all[first + m]
        my_tok_ref[m] = tok_ref[first + m]
        my_grad_ref[m] = grad_ref[first + m]


def expert_kernel(images, n_expert, k, gb, win_ref, bin_ref, wout_ref, t_ref, *rest):
    outer, inner = levels(n_expert)
    come_refs = rest[: outer * inner]
    back_ref, got_ref = rest[outer * inner :]
    rows = k * images
    c, l = position(inner)
    block = got_ref.shape[1]
    for j in range(outer):
        source = partner(c, j, outer, True) * inner
        for i in range(inner):
            got_ref[source + lax.rem(l + i, inner)] = come_refs[i * outer + j][:block]
    width = got_ref.shape[2]
    total = n_expert * rows
    got = got_ref[...]
    rows_in = got[:, :rows].reshape(total, width)
    rows_grad = got[:, rows:].reshape(total, width)
    half = width // 2
    expert = lax.rem(lax.div(lax.broadcasted_iota(jnp.int32, (total, 1), 0), images), k)

    def own(parts):
        out = parts[0]
        for e in range(1, k):
            out = jnp.where(expert == e, parts[e], out)
        return out

    pre = own([mm(rows_in, win_ref[e]) + bin_ref[e : e + 1] for e in range(k)])
    cdf = 0.5 * (1.0 + lax.erf(pre * 0.7071067811865476))
    hidden = (pre * cdf).astype(BF)
    slope = cdf + pre * jnp.exp(-0.5 * pre * pre) * 0.3989422804014327
    out_part = own([mm(hidden, wout_ref[e]) for e in range(k)]).astype(BF)
    act_grad = own([mm(rows_grad, wout_ref[e], NT) for e in range(k)])
    pre_grad = (act_grad * slope).astype(BF)
    in_part = own([mm(pre_grad, win_ref[e], NT) for e in range(k)]).astype(BF)
    rows = gb * k * images
    t = t_ref[...]
    out_rows = t.shape[0]
    for i in range(n_expert // gb):
        stack = jnp.concatenate(
            [
                part[i * rows : (i + 1) * rows, h * half : (h + 1) * half]
                for part in (out_part, in_part)
                for h in range(2)
            ],
            axis=0,
        )
        back_ref[i * out_rows : (i + 1) * out_rows] = mm(t, stack).astype(BF)


def final_kernel(
    quarter, k, gb, home_ref, bias_ref, tok_ref, grad_ref, disp_ref, comb_ref, keys_ref, sel_ref, out_ref,
):
    slots = keys_ref.shape[0]
    step = gb * k
    blocks = slots // step
    per_block = home_ref.shape[0] // blocks
    sel = sel_ref[...]
    sums = [mm(sel, home_ref[i * per_block : (i + 1) * per_block]) for i in range(blocks)]

    def assemble(kind, m):
        halves = []
        for h in range(2):
            start = ((m * 2 + kind) * 2 + h) * step
            halves.append(jnp.concatenate([s[start : start + step] for s in sums], axis=0))
        return jnp.concatenate(halves, axis=1)

    keys = keys_ref[...]
    for m in range(quarter):
        slot_out = (assemble(0, m) + bias_ref[...]).astype(BF)
        slot_in_grad = assemble(1, m).astype(BF)
        comb_grad = mm(slot_out, grad_ref[m], NT)
        disp_grad = mm(slot_in_grad, tok_ref[m], NT)
        disp = disp_ref[m]
        comb = comb_ref[m].astype(F32)
        wide = disp.astype(F32)
        logit_grad = comb * (comb_grad - jnp.sum(comb * comb_grad, axis=0, keepdims=True))
        logit_grad = logit_grad + wide * (
            disp_grad - jnp.sum(wide * disp_grad, axis=1, keepdims=True)
        )
        logit_grad = logit_grad.astype(BF).astype(F32)
        left = jnp.concatenate([wide, logit_grad], axis=0).T.astype(BF)
        right = jnp.concatenate([slot_in_grad, keys], axis=0)
        out_ref[m] = mm(left, right).astype(BF)


def local(n_expert, n_hidden, tokens, slot_keys, w_in, b_in, w_out, b_out, out_grad):
    n_all = n_expert * n_hidden
    images, positions, width = tokens.shape
    quarter = images // n_hidden
    slots = slot_keys.shape[1]
    k, _, units = w_in.shape
    gb = block_of(n_expert)
    half = width // 2
    vmem = pl.BlockSpec(memory_space=pltpu.VMEM)
    keys = slot_keys.T

    order = np.arange(2 * images * gb * k).reshape(2, images, gb, k).transpose(2, 0, 3, 1)
    perm = one_hot_rows(order, order.size)
    send_rows = 2 * k * images
    outer, inner = levels(n_expert)
    disp, comb, my_tok, my_grad, *leave = pl.pallas_call(
        functools.partial(dispatch_kernel, images, quarter, k, gb, n_expert),
        out_shape=(
            jax.ShapeDtypeStruct((quarter, slots, positions), BF),
            jax.ShapeDtypeStruct((quarter, slots, positions), BF),
            jax.ShapeDtypeStruct((quarter, positions, width), BF),
            jax.ShapeDtypeStruct((quarter, positions, width), BF),
        )
        + (jax.ShapeDtypeStruct((inner * send_rows, width), BF),) * outer,
        in_specs=[vmem] * 4,
        out_specs=(vmem,) * (4 + outer),
        scratch_shapes=[pltpu.VMEM((n_expert * send_rows, width), BF)]
        + [pltpu.VMEM((images, slots, positions), BF)] * 2,
        compiler_params=pltpu.CompilerParams(vmem_limit_bytes=12 << 20),
        cost_estimate=pl.CostEstimate(flops=8000000000, bytes_accessed=0, transcendentals=0),
        name="dispatch",
    )(tokens, out_grad, keys, perm)

    everyone = [(c, l) for c in range(outer) for l in range(inner)]
    come = leave[:1] + [None] * (outer - 1)
    for j in range(outer - 1, 0, -1):
        pairs = [(c * inner + l, partner(c, j, outer) * inner + l) for c, l in everyone]
        come[j] = lax.ppermute(leave[j], "expert", pairs)
    if inner == 2:
        swap = [(c * inner + l, c * inner + 1 - l) for c, l in everyone]
        come += [lax.ppermute(x[send_rows:], "expert", swap) for x in come]

    order = np.arange(2 * k * 2 * gb * images).reshape(2, 2, gb, k, n_hidden, quarter)
    order = order.transpose(2, 4, 0, 3, 5, 1)
    spread = one_hot_rows(order, order.size)
    back_rows = 2 * k * quarter * 2
    back = pl.pallas_call(
        functools.partial(expert_kernel, images, n_expert, k, gb),
        out_shape=jax.ShapeDtypeStruct((n_all * back_rows, half), BF),
        in_specs=[vmem] * (4 + len(come)),
        out_specs=vmem,
        scratch_shapes=[pltpu.VMEM((n_expert, send_rows, width), BF)],
        compiler_params=pltpu.CompilerParams(vmem_limit_bytes=20 << 20),
        name="experts",
    )(w_in, b_in, w_out, spread, *come)

    home = lax.all_to_all(
        back.reshape(n_all, back_rows, half),
        ("expert", "hidden"),
        split_axis=0,
        concat_axis=0,
        tiled=True,
    )

    label = np.arange(quarter * 2 * 2 * gb * k).reshape(quarter, 2, 2, gb, k).transpose(3, 1, 4, 0, 2)
    label = np.broadcast_to(label[:, None], (gb, n_hidden) + label.shape[1:])
    select = np.ascontiguousarray(one_hot_rows(label, quarter * 4 * gb * k).T)
    return pl.pallas_call(
        functools.partial(final_kernel, quarter, k, gb),
        out_shape=jax.ShapeDtypeStruct((quarter, positions, width), BF),
        in_specs=[vmem] * 8,
        out_specs=vmem,
        compiler_params=pltpu.CompilerParams(vmem_limit_bytes=8 << 20),
        name="tokens_back",
    )(home.reshape(n_all * back_rows, half), b_out, my_tok, my_grad, disp, comb, keys, select)


def solution(mesh):
    return jax.shard_map(
        functools.partial(local, mesh.shape["expert"], mesh.shape["hidden"]),
        mesh=mesh,
        in_specs=(
            P("expert", None, None),
            P(),
            P("expert", None, "hidden"),
            P("expert", "hidden"),
            P("expert", "hidden", None),
            P(),
            P("expert", None, None),
        ),
        out_specs=P(("expert", "hidden"), None, None),
        check_vma=False,
    )
```
